256 devices in a mesh: dp: 32 (over z, x), seq: 8 (over y, core).
Axes of the slice: x: 4, y: 4, z: 8, core: 2. Of those that a mesh axis runs over, the one named last changes fastest.
Arguments:
- query: bfloat16 [32768, 2048], P(('dp', 'seq')), may hold values from -6 to 6
- key_rows: bfloat16 [32768, 1024], P(('dp', 'seq')), may hold values from -6 to 6
- value_rows: bfloat16 [32768, 1024], P(('dp', 'seq')), may hold values from -6 to 6
- attn_out: bfloat16 [32768, 2048], P(('dp', 'seq')), may hold values from -6 to 6
- out_grad: bfloat16 [32768, 2048], P(('dp', 'seq')), may hold values from -6 to 6
- source_row: int32 [32768], P(('dp', 'seq')), may hold values from 0 to 32767, as said below
- segment_ids: int32 [32768], P('dp'), may hold values from 0 to 7, as said below
Outputs:
- grad_query: bfloat16 [32768, 2048], P(('dp', 'seq'))
- grad_key: bfloat16 [32768, 1024], P(('dp', 'seq'))
- grad_value: bfloat16 [32768, 1024], P(('dp', 'seq'))
The draws below stay inside these ranges and needn't reach their ends.
Inputs may be any that keep to these rules, and one draw needn't show every extreme that they name: source_row is a permutation of all rows; a row keeps its seq index; one rollout device sends at most 8 rows to one owner, and every owner takes exactly 8 rows from some rollout device; within one seq index, how many rows go from one device to another depends only on the difference of their dp indices. `segment_ids`: within each pack of 1024 rows the ids start at 0, never fall and rise by at most 1 from one row to the next; every pack holds exactly 8 pairs.
All inputs are finite; a program needn't handle non-finite values.
Results may differ from the reference program's by a relative error of at most 0.0049.
Values may be sent and summed in bfloat16 or wider, within the bound.
No kernel may reach another device: no remote copies, remote signals or barrier semaphores. Data moves between devices by JAX's collectives and lax.ppermute only.
A program may use at most 64 MiB of HBM per device.

```python
import jax
import jax.numpy as jnp
from jax import lax

HEADS = 16
KV_HEADS = 8
HEAD_DIM = 128
TOK_DEV = 128
GROUP = 1024
TOKENS = 32768
CAP = 8
N_DP = 32
N_SEQ = 8


def rough_entries(key, row_count, head_count):
    noise_key = jax.random.fold_in(key, 1)
    values = 1.5 * jax.random.normal(noise_key, (row_count, head_count, HEAD_DIM), jnp.float32)
    return jnp.clip(values, -6.0, 6.0).reshape(row_count, head_count * HEAD_DIM)


def draw_query(key, part):
    key = jax.random.fold_in(key, 3)
    return rough_entries(key, TOKENS, HEADS).astype(jnp.bfloat16)


def draw_key_rows(key, part):
    key = jax.random.fold_in(key, 4)
    return rough_entries(key, TOKENS, KV_HEADS).astype(jnp.bfloat16)


def shuffled_rows(key_list):

    def one_order(single_key):
        return jax.random.permutation(single_key, TOK_DEV).astype(jnp.int32)
    return jax.vmap(one_order)(key_list)


def column_sources(column_key, column):
    shift_key, count_key, source_key, owner_key = jax.random.split(column_key, 4)
    shifts = jax.random.permutation(shift_key, N_DP).astype(jnp.int32)
    halves = jax.random.randint(count_key, (N_DP // 2,), 0, CAP + 1).astype(jnp.int32)
    halves = halves.at[0].set(CAP)
    counts = jnp.stack([halves, CAP - halves], axis=1).reshape(N_DP)
    bounds = jnp.cumsum(counts)
    slots = jnp.arange(TOK_DEV, dtype=jnp.int32)
    which = jnp.sum((bounds[None, :] <= slots[:, None]).astype(jnp.int32), axis=1)
    owners = jnp.arange(N_DP, dtype=jnp.int32)
    sources = (owners[:, None] - shifts[which][None, :]) % N_DP
    orders = shuffled_rows(jax.random.split(source_key, N_DP))
    local = orders[sources, slots[None, :]]
    global_rows = (sources * N_SEQ + column) * TOK_DEV + local
    owner_orders = shuffled_rows(jax.random.split(owner_key, N_DP))
    return jnp.take_along_axis(global_rows, owner_orders, axis=1)


def draw_source_row(key, part):
    key = jax.random.fold_in(key, 1)
    column_keys = jax.random.split(key, N_SEQ)
    columns = jnp.arange(N_SEQ, dtype=jnp.int32)
    table = jax.vmap(column_sources)(column_keys, columns)
    return jnp.transpose(table, (1, 0, 2)).reshape(TOKENS).astype(jnp.int32)


def pack_marks(pack_key):
    pair_count = max(2, GROUP // 128)
    cuts = jax.random.permutation(pack_key, GROUP - 1)[:pair_count - 1].astype(jnp.int32) + 1
    marks = jnp.zeros((GROUP,), jnp.int32).at[cuts].set(1)
    return marks.at[0].set(1)


def draw_segment_ids(key, part):
    key = jax.random.fold_in(key, 2)
    marks = jax.vmap(pack_marks)(jax.random.split(key, N_DP))
    return (jnp.cumsum(marks, axis=1) - 1).reshape(TOKENS).astype(jnp.int32)


def block_levels(key, shape, pieces, low, high):
    def one(dim, shards_of):
        heights = jax.random.uniform(jax.random.fold_in(jax.random.fold_in(key, 6), dim), (shards_of,), jnp.float32, low / len(pieces), high / len(pieces))
        return jnp.repeat(jnp.exp(heights), shape[dim] // shards_of).reshape((-1,) + (1,) * (len(shape) - dim - 1))

    level = one(*pieces[0])
    for cut in pieces[1:]:
        level = level * one(*cut)
    return level


def centred(own_key, dims, scale, limit, pieces=(), kind=jnp.bfloat16):
    values = jax.random.normal(own_key, dims, jnp.float32) * scale
    if len(pieces) > 0:
        values = block_levels(own_key, dims, pieces, -0.22, 0.18) * values
    return jnp.clip(values, min=-limit, max=limit).astype(kind)


def setup_inputs(seed: int = 0) -> dict:
    keys = jax.random.split(jax.random.key(seed), 8)
    query = draw_query(jax.random.fold_in(keys[7], 71), 0)
    key_rows = draw_key_rows(jax.random.fold_in(keys[7], 71), 0)
    value_rows = centred(keys[2], (TOKENS, KV_HEADS * HEAD_DIM), 1.0, 6.0, ((0, 256),))
    attn_out = centred(keys[3], (TOKENS, HEADS * HEAD_DIM), 1.0, 6.0, ((0, 256),))
    out_grad = centred(keys[4], (TOKENS, HEADS * HEAD_DIM), 1.0, 6.0, ((0, 256),))
    source_row = draw_source_row(jax.random.fold_in(keys[7], 71), 0)
    segment_ids = draw_segment_ids(jax.random.fold_in(keys[7], 71), 0)
    return dict(query=query, key_rows=key_rows, value_rows=value_rows, attn_out=attn_out, out_grad=out_grad, source_row=source_row, segment_ids=segment_ids)


scaling = 1.0 / 12.0
softcap = 50.0


def head_grads(query_head, key_head, value_head, out_head, grad_head, allowed):
    score = jnp.dot(query_head, key_head.T, preferred_element_type=jnp.float32) * scaling
    squashed = jnp.tanh(score / softcap)
    weights = jnp.where(allowed, jnp.exp(softcap * squashed), jnp.float32(0.0))
    probabilities = weights / jnp.sum(weights, axis=1, keepdims=True)
    prob_low = probabilities.astype(jnp.bfloat16)
    value_part = jnp.dot(prob_low.T, grad_head, preferred_element_type=jnp.float32)
    prob_grad = jnp.dot(grad_head, value_head.T, preferred_element_type=jnp.float32)
    row_delta = jnp.sum(grad_head.astype(jnp.float32) * out_head.astype(jnp.float32), axis=1, keepdims=True)
    score_grad = (probabilities * (prob_grad - row_delta) * (1.0 - squashed * squashed)).astype(jnp.bfloat16)
    query_part = jnp.dot(score_grad, key_head, preferred_element_type=jnp.float32) * scaling
    key_part = jnp.dot(score_grad.T, query_head, preferred_element_type=jnp.float32) * scaling
    return query_part, key_part, value_part


def pack_grads(operands):
    pack_query, pack_key, pack_value, pack_out, pack_grad, pack_segment = operands
    position = jnp.arange(GROUP)
    allowed = (pack_segment[:, None] == pack_segment[None, :]) & (position[None, :] <= position[:, None])
    query_parts = []
    key_parts = []
    value_parts = []
    for kv_index in range(KV_HEADS):
        kv_cols = slice(kv_index * HEAD_DIM, (kv_index + 1) * HEAD_DIM)
        key_sum = jnp.zeros((GROUP, HEAD_DIM), jnp.float32)
        value_sum = jnp.zeros((GROUP, HEAD_DIM), jnp.float32)
        for member in range(2):
            head_index = 2 * kv_index + member
            cols = slice(head_index * HEAD_DIM, (head_index + 1) * HEAD_DIM)
            query_part, key_part, value_part = head_grads(pack_query[:, cols], pack_key[:, kv_cols], pack_value[:, kv_cols], pack_out[:, cols], pack_grad[:, cols], allowed)
            query_parts.append(query_part.astype(jnp.bfloat16))
            key_sum = key_sum + key_part
            value_sum = value_sum + value_part
        key_parts.append(key_sum.astype(jnp.bfloat16))
        value_parts.append(value_sum.astype(jnp.bfloat16))
    return jnp.concatenate(query_parts, axis=1), jnp.concatenate(key_parts, axis=1), jnp.concatenate(value_parts, axis=1)


def reference(query, key_rows, value_rows, attn_out, out_grad, source_row, segment_ids):
    def owned(array):
        return array[source_row].reshape(N_DP, GROUP, array.shape[1])

    segments = segment_ids.reshape(N_DP, GROUP)
    grad_q, grad_k, grad_v = lax.map(pack_grads, (owned(query), owned(key_rows), owned(value_rows), owned(attn_out), owned(out_grad), segments))
    return (grad_q.reshape(TOKENS, HEADS * HEAD_DIM), grad_k.reshape(TOKENS, KV_HEADS * HEAD_DIM), grad_v.reshape(TOKENS, KV_HEADS * HEAD_DIM))
```

```python
import functools

import jax
import jax.numpy as jnp
from jax import lax
from jax.experimental import pallas as pl
from jax.experimental.pallas import tpu as pltpu
from jax.sharding import PartitionSpec as P

HEAD_DIM = 128
N_DP = 32
N_SEQ = 8
ROWS = 128
GROUP = N_SEQ * ROWS
WIDTH = 6 * HEAD_DIM
LANES = 128
BLOCK = 256
CAPACITIES = (48, 56, 72)

scaling = 1.0 / 12.0
softcap = 50.0

PARAMS = pltpu.CompilerParams(vmem_limit_bytes=48 * 1024 * 1024)


def iota(shape, dim):
    return lax.broadcasted_iota(jnp.int32, shape, dim)


def nt_dot(left, right):
    return lax.dot_general(left, right, (((1,), (1,)), ((), ())), preferred_element_type=jnp.float32)


def nn_dot(left, right):
    return jnp.dot(left, right, preferred_element_type=jnp.float32)


def pack_kernel(query_ref, key_ref, value_ref, out_ref, grad_ref, packed_ref):
    columns = []
    for head in range(2 * N_SEQ):
        cols = slice(head * HEAD_DIM, (head + 1) * HEAD_DIM)
        product = grad_ref[:, cols].astype(jnp.float32) * out_ref[:, cols].astype(jnp.float32)
        columns.append(jnp.sum(product, axis=1, keepdims=True))
    lane = iota((ROWS, LANES), 1)
    table = jnp.zeros((ROWS, LANES), jnp.float32)
    for head in range(2 * N_SEQ):
        table = jnp.where(lane == head, columns[head], table)
    delta = table.T
    high = delta.astype(jnp.bfloat16).astype(jnp.float32)
    low = delta - high
    pad_rows = jnp.zeros((4, LANES), jnp.float32)
    pad_cols = jnp.zeros((8, WIDTH - LANES), jnp.float32)
    for group in range(N_SEQ):
        two = slice(2 * group * HEAD_DIM, 2 * (group + 1) * HEAD_DIM)
        one = slice(group * HEAD_DIM, (group + 1) * HEAD_DIM)
        pair = slice(2 * group, 2 * group + 2)
        rows = jnp.concatenate(
            [query_ref[:, two], key_ref[:, one], value_ref[:, one], grad_ref[:, two]], axis=1
        )
        extra = jnp.concatenate([high[pair], low[pair], pad_rows], axis=0)
        extra = jnp.concatenate([extra, pad_cols], axis=1)
        packed_ref[group] = jnp.concatenate([rows.astype(jnp.float32), extra], axis=0).astype(
            jnp.bfloat16
        )


def wide(rows):
    return jnp.concatenate([rows[s : s + 1] for s in range(N_SEQ)], axis=1)


def index_kernel(list_ref, segment_ref, rows_ref, cols_ref, request_ref, most_ref):
    listed = list_ref[...]
    source = (listed // GROUP).astype(jnp.float32)
    local_row = (listed % ROWS).astype(jnp.float32)
    segment = segment_ref[...].astype(jnp.float32)
    blank = jnp.zeros((LANES - 8, LANES), jnp.float32)
    source_cols = jnp.concatenate([source, blank], axis=0).T
    before = iota((ROWS, ROWS), 0) < iota((ROWS, ROWS), 1)
    slots = []
    for s in range(N_SEQ):
        mine = source[s : s + 1]
        hits = ((source_cols[:, s : s + 1] == mine) & before).astype(jnp.float32)
        for earlier in range(s):
            hits = hits + (source_cols[:, earlier : earlier + 1] == mine).astype(jnp.float32)
        slots.append(jnp.sum(hits, axis=0, keepdims=True))
    slot = jnp.concatenate(slots, axis=0)
    blank = jnp.zeros((LANES - 24, LANES), jnp.float32)
    turned = jnp.concatenate([source, slot, segment, blank], axis=0).T
    lane = iota((ROWS, LANES), 1)
    picks = []
    for s in range(N_SEQ):
        columns = jnp.where(lane == 0, turned[:, s : s + 1], 0.0)
        columns = jnp.where(lane == 1, turned[:, 8 + s : 9 + s], columns)
        columns = jnp.where(lane == 2, turned[:, 16 + s : 17 + s], columns)
        cols_ref[s * ROWS : (s + 1) * ROWS, :] = columns
        picks.append((lane.astype(jnp.float32) == turned[:, 8 + s : 9 + s] + 1.0).astype(jnp.float32))
    rows_ref[0:8, :] = source
    rows_ref[8:16, :] = slot
    rows_ref[16:24, :] = segment
    pick = jnp.concatenate(picks, axis=0).astype(jnp.bfloat16)
    from_source = iota((N_DP, GROUP), 0).astype(jnp.float32) == wide(source)
    column = (iota((1, GROUP), 1) // ROWS).astype(jnp.float32)
    low = jnp.where(from_source, wide(local_row) + 1.0, 0.0).astype(jnp.bfloat16)
    high = jnp.where(from_source, column, 0.0).astype(jnp.bfloat16)
    table = nn_dot(low, pick) + float(ROWS) * nn_dot(high, pick)
    request_ref[...] = table.astype(jnp.int32)
    most_ref[0, 0] = (jnp.max(slot) + 1.0).astype(jnp.int32)


def send_kernel(capacity, request_ref, rows_ref, sent_ref, pick_ref, ext_ref):
    group_rows = 8 * capacity
    blank = jnp.zeros((LANES - N_DP, LANES), jnp.float32)
    turned = jnp.concatenate([request_ref[...].astype(jnp.float32), blank], axis=0).T
    delta_id = (iota((LANES, LANES), 1) + GROUP).astype(jnp.float32)
    turned = jnp.where(iota((LANES, LANES), 0) == 0, delta_id, turned - 1.0)
    deltas = []
    for s in range(N_SEQ):
        whole = rows_ref[s]
        ext_ref[s * ROWS : (s + 1) * ROWS, :] = whole[:ROWS]
        deltas.append(whole[ROWS:, :LANES].astype(jnp.float32))
    delta = jnp.concatenate(deltas, axis=1)
    places = jnp.zeros((8, GROUP), jnp.float32)
    row_id = iota((group_rows, GROUP + LANES), 1).astype(jnp.float32)
    for group in range(N_DP // 8):
        column = jnp.concatenate(
            [turned[:capacity, d : d + 1] for d in range(8 * group, 8 * group + 8)], axis=0
        )
        pick = (column == row_id).astype(jnp.float32).astype(jnp.bfloat16)
        pick_ref[group * group_rows : (group + 1) * group_rows, :] = pick
        index = iota((8, group_rows), 1)
        owner = index // capacity
        kind = iota((8, group_rows), 0)
        value = jnp.where(kind == 0, owner + 8 * group, index - owner * capacity)
        places = places + nn_dot(value.astype(jnp.float32).astype(jnp.bfloat16), pick[:, :GROUP])
    owner_of = places[0:1]
    slot_cols = []
    for s in range(N_SEQ):
        part = places[:, s * ROWS : (s + 1) * ROWS]
        blank = jnp.zeros((LANES - 8, LANES), jnp.float32)
        slot_cols.append(jnp.concatenate([part, blank], axis=0).T[:, 1:2])
    slot_col = jnp.concatenate(slot_cols, axis=0)
    slot_pick = (slot_col == iota((GROUP, LANES), 1).astype(jnp.float32)).astype(jnp.float32)
    to_owner = iota((N_DP, GROUP), 0).astype(jnp.float32) == owner_of
    spread = jnp.concatenate(
        [jnp.where(to_owner, delta[c : c + 1], 0.0) for c in range(4)], axis=0
    ).astype(jnp.bfloat16)
    packed = nn_dot(spread, slot_pick.astype(jnp.bfloat16))
    tail = jnp.concatenate(
        [packed[c * N_DP : (c + 1) * N_DP] for c in range(4)]
        + [jnp.zeros((N_DP, WIDTH - 4 * LANES), jnp.float32)],
        axis=1,
    )
    tail = jnp.concatenate([tail, jnp.zeros((LANES - N_DP, WIDTH), jnp.float32)], axis=0)
    ext_ref[GROUP:, :] = tail.astype(jnp.bfloat16)
    for group in range(N_DP // 8):
        span = slice(group * group_rows, (group + 1) * group_rows)
        sent_ref[span, :] = nn_dot(pick_ref[span, :], ext_ref[...]).astype(jnp.bfloat16)


def attend_kernel(
    capacity,
    segment_ref,
    arrived_ref,
    rows_ref,
    cols_ref,
    out_ref,
    x_ref,
    kt_ref,
    delta_ref,
    weight_ref,
    squash_ref,
    total_ref,
    gqt_ref,
    gk_ref,
    gv_ref,
):
    slots = N_DP * capacity
    blocks = GROUP // BLOCK
    slot_id = iota((BLOCK, slots), 1).astype(jnp.float32)
    for block in range(blocks):
        rows = slice(block * BLOCK, (block + 1) * BLOCK)
        place = cols_ref[rows, 0:1] * float(capacity) + cols_ref[rows, 1:2] + 1.0
        pick = (place == slot_id).astype(jnp.float32).astype(jnp.bfloat16)
        gathered = nn_dot(pick, arrived_ref[...])
        x_ref[rows, :] = gathered.astype(jnp.bfloat16)
        kt_ref[:, rows] = gathered[:, 2 * HEAD_DIM : 3 * HEAD_DIM].T.astype(jnp.bfloat16)
    first = iota((LANES, slots), 0) * capacity == iota((LANES, slots), 1)
    first = first.astype(jnp.float32).astype(jnp.bfloat16)
    parts = nn_dot(first, arrived_ref[:, : 4 * LANES])
    source = wide(rows_ref[0:8, :])
    slot = wide(rows_ref[8:16, :])
    segment = wide(rows_ref[16:24, :])
    from_source = iota((LANES, GROUP), 0).astype(jnp.float32) == source
    from_source = from_source.astype(jnp.float32).astype(jnp.bfloat16)
    in_slot = iota((LANES, GROUP), 0).astype(jnp.float32) == slot + 1.0
    for head in range(2):
        high = parts[:, head * LANES : (head + 1) * LANES].T.astype(jnp.bfloat16)
        low = parts[:, (2 + head) * LANES : (3 + head) * LANES].T.astype(jnp.bfloat16)
        both = nn_dot(high, from_source) + nn_dot(low, from_source)
        delta = jnp.sum(jnp.where(in_slot, both, 0.0), axis=0, keepdims=True)
        delta_ref[head : head + 1, :] = delta
    gk_ref[...] = jnp.zeros_like(gk_ref)
    gv_ref[...] = jnp.zeros_like(gv_ref)
    causal = iota((BLOCK, BLOCK), 0) <= iota((BLOCK, BLOCK), 1)
    causal = jnp.concatenate([causal.astype(jnp.float32)] * 2, axis=1) > 0.0
    for block in range(blocks):
        rows = slice(block * BLOCK, (block + 1) * BLOCK)
        queries = jnp.concatenate([x_ref[rows, 0:128], x_ref[rows, 128:256]], axis=0)
        grads = jnp.concatenate([x_ref[rows, 512:640], x_ref[rows, 640:768]], axis=0)
        delta = jnp.concatenate([delta_ref[0:1, rows], delta_ref[1:2, rows]], axis=1)
        segment_q = jnp.concatenate([segment[:, rows]] * 2, axis=1)

        def weigh(key_block):
            keys = slice(key_block * BLOCK, (key_block + 1) * BLOCK)
            score = nt_dot(x_ref[keys, 256:384], queries)
            squashed = jnp.tanh(score * (scaling / softcap))
            allowed = cols_ref[keys, 2:3] == segment_q
            if key_block == block:
                allowed = allowed & causal
            weights = jnp.where(allowed, jnp.exp(softcap * squashed), 0.0)
            weight_ref[keys, :] = weights
            squash_ref[keys, :] = squashed
            total = jnp.sum(weights, axis=0, keepdims=True)
            if key_block == block:
                total_ref[0:1, :] = total
            else:
                total_ref[0:1, :] += total

        def back(key_block):
            keys = slice(key_block * BLOCK, (key_block + 1) * BLOCK)
            probabilities = weight_ref[keys, :] * (1.0 / total_ref[0:1, :])
            gv_ref[keys, :] += nn_dot(probabilities.astype(jnp.bfloat16), grads)
            prob_grad = nt_dot(x_ref[keys, 384:512], grads)
            squashed = squash_ref[keys, :]
            score_grad = probabilities * (prob_grad - delta) * (1.0 - squashed * squashed)
            score_grad = score_grad.astype(jnp.bfloat16)
            gk_ref[keys, :] += nn_dot(score_grad, queries)
            part = nn_dot(kt_ref[:, keys], score_grad)
            if key_block == block:
                gqt_ref[...] = part
            else:
                gqt_ref[...] += part

        first_segment = segment_ref[block * BLOCK]
        weigh(block)
        for key_block in range(block):
            meets = segment_ref[(key_block + 1) * BLOCK - 1] == first_segment
            pl.when(meets)(functools.partial(weigh, key_block))
        back(block)
        for key_block in range(block):
            meets = segment_ref[(key_block + 1) * BLOCK - 1] == first_segment
            pl.when(meets)(functools.partial(back, key_block))
        turned = (gqt_ref[...].T * scaling).astype(jnp.bfloat16)
        out_ref[rows, 0:128] = turned[:BLOCK]
        out_ref[rows, 128:256] = turned[BLOCK:]
    out_ref[:, 256:384] = (gk_ref[...] * scaling).astype(jnp.bfloat16)
    out_ref[:, 384:512] = gv_ref[...].astype(jnp.bfloat16)


def unpack_kernel(returned_ref, query_ref, key_ref, value_ref):
    for group in range(N_SEQ):
        two = slice(2 * group * HEAD_DIM, 2 * (group + 1) * HEAD_DIM)
        one = slice(group * HEAD_DIM, (group + 1) * HEAD_DIM)
        query_ref[:, two] = returned_ref[group, :, 0:256]
        key_ref[:, one] = returned_ref[group, :, 256:384]
        value_ref[:, one] = returned_ref[group, :, 384:512]


def shape(dims, dtype=jnp.bfloat16):
    return jax.ShapeDtypeStruct(dims, dtype)


def pack(query, key_rows, value_rows, attn_out, out_grad):
    return pl.pallas_call(
        pack_kernel, out_shape=shape((N_SEQ, ROWS + 8, WIDTH)), compiler_params=PARAMS, name="pack"
    )(query, key_rows, value_rows, attn_out, out_grad)


def index(pack_list, segments):
    vmem = pl.BlockSpec(memory_space=pltpu.VMEM)
    return pl.pallas_call(
        index_kernel,
        out_shape=(
            shape((24, LANES), jnp.float32),
            shape((GROUP, LANES), jnp.float32),
            shape((N_DP, LANES), jnp.int32),
            shape((1, 1), jnp.int32),
        ),
        out_specs=(vmem, vmem, vmem, pl.BlockSpec(memory_space=pltpu.SMEM)),
        compiler_params=PARAMS,
        name="index",
    )(pack_list, segments.reshape(N_SEQ, ROWS))


def send(capacity, request, head_rows):
    return pl.pallas_call(
        functools.partial(send_kernel, capacity),
        out_shape=shape((N_DP * capacity, WIDTH)),
        scratch_shapes=[
            pltpu.VMEM((N_DP * capacity, GROUP + LANES), jnp.bfloat16),
            pltpu.VMEM((GROUP + LANES, WIDTH), jnp.bfloat16),
        ],
        compiler_params=PARAMS,
        name="send",
    )(request, head_rows)


def attend(capacity, segments, arrived, rows, cols):
    vmem = pl.BlockSpec(memory_space=pltpu.VMEM)
    return pl.pallas_call(
        functools.partial(attend_kernel, capacity),
        out_shape=shape((GROUP, 4 * HEAD_DIM)),
        in_specs=[pl.BlockSpec(memory_space=pltpu.SMEM), vmem, vmem, vmem],
        scratch_shapes=[
            pltpu.VMEM((GROUP, WIDTH), jnp.bfloat16),
            pltpu.VMEM((HEAD_DIM, GROUP), jnp.bfloat16),
            pltpu.VMEM((8, GROUP), jnp.float32),
            pltpu.VMEM((GROUP, 2 * BLOCK), jnp.float32),
            pltpu.VMEM((GROUP, 2 * BLOCK), jnp.float32),
            pltpu.VMEM((8, 2 * BLOCK), jnp.float32),
            pltpu.VMEM((HEAD_DIM, 2 * BLOCK), jnp.float32),
            pltpu.VMEM((GROUP, HEAD_DIM), jnp.float32),
            pltpu.VMEM((GROUP, HEAD_DIM), jnp.float32),
        ],
        compiler_params=PARAMS,
        name="attend",
    )(segments, arrived, rows, cols)


def unpack(returned):
    return pl.pallas_call(
        unpack_kernel,
        out_shape=(shape((ROWS, 2048)), shape((ROWS, 1024)), shape((ROWS, 1024))),
        compiler_params=PARAMS,
        name="unpack",
    )(returned)


def local(query, key_rows, value_rows, attn_out, out_grad, source_row, segment_ids):
    packed = pack(query, key_rows, value_rows, attn_out, out_grad)
    head_rows = lax.all_to_all(packed, "seq", split_axis=0, concat_axis=0, tiled=True)
    pack_list = lax.all_gather(source_row, "seq", axis=0)
    rows, cols, request, most = index(pack_list, segment_ids)
    request = lax.all_to_all(request, "dp", split_axis=0, concat_axis=0, tiled=True)

    def relay(capacity, request, head_rows, rows, cols):
        sent = send(capacity, request, head_rows)
        arrived = lax.all_to_all(sent, "dp", split_axis=0, concat_axis=0, tiled=True)
        return attend(capacity, segment_ids, arrived, rows, cols)

    need = most[0, 0] + 1
    level = sum((need > capacity).astype(jnp.int32) for capacity in CAPACITIES[:-1])
    branches = [functools.partial(relay, capacity) for capacity in CAPACITIES]
    grads = lax.switch(level, branches, request, head_rows, rows, cols)
    returned = lax.all_to_all(
        grads.reshape(N_SEQ, ROWS, 4 * HEAD_DIM), "seq", split_axis=0, concat_axis=0, tiled=True
    )
    return unpack(returned)


def solution(mesh):
    in_specs = (
        P(("dp", "seq"), None),
        P(("dp", "seq"), None),
        P(("dp", "seq"), None),
        P(("dp", "seq"), None),
        P(("dp", "seq"), None),
        P(("dp", "seq")),
        P("dp"),
    )
    out_specs = (P(("dp", "seq"), None), P(("dp", "seq"), None), P(("dp", "seq"), None))
    return jax.shard_map(local, mesh=mesh, in_specs=in_specs, out_specs=out_specs, check_vma=False)
```

```python
import functools

import jax
import jax.numpy as jnp
from jax import lax
from jax.experimental import pallas as pl
from jax.experimental.pallas import tpu as pltpu
from jax.sharding import PartitionSpec as P

HEAD_DIM = 128
N_DP = 32
N_SEQ = 8
ROWS = 128
GROUP = N_SEQ * ROWS
WIDTH = 6 * HEAD_DIM
LANES = 128
BLOCK = 256
PAIRS = 10
CAPACITY = 56
EXTRA = 16

scaling = 1.0 / 12.0
softcap = 50.0

PARAMS = pltpu.CompilerParams(vmem_limit_bytes=28 * 1024 * 1024)
FULL = pltpu.CompilerParams(vmem_limit_bytes=60 * 1024 * 1024)


def iota(shape, dim):
    return lax.broadcasted_iota(jnp.int32, shape, dim)


def nt_dot(left, right):
    return lax.dot_general(left, right, (((1,), (1,)), ((), ())), preferred_element_type=jnp.float32)


def nn_dot(left, right):
    return jnp.dot(left, right, preferred_element_type=jnp.float32)


def pack_kernel(
    query_hbm, key_hbm, value_hbm, out_hbm, grad_hbm, packed_ref,
    query_ref, key_ref, value_ref, out_ref, grad_ref, sems,
):
    pairs = (
        (grad_hbm, grad_ref),
        (out_hbm, out_ref),
        (query_hbm, query_ref),
        (key_hbm, key_ref),
        (value_hbm, value_ref),
    )
    copies = [
        pltpu.make_async_copy(source, target, sems.at[i])
        for i, (source, target) in enumerate(pairs)
    ]
    for copy in copies:
        copy.start()
    copies[0].wait()
    copies[1].wait()
    columns = []
    for head in range(2 * N_SEQ):
        cols = slice(head * HEAD_DIM, (head + 1) * HEAD_DIM)
        product = grad_ref[:, cols].astype(jnp.float32) * out_ref[:, cols].astype(jnp.float32)
        columns.append(jnp.sum(product, axis=1, keepdims=True))
    lane = iota((ROWS, LANES), 1)
    table = jnp.zeros((ROWS, LANES), jnp.float32)
    for head in range(2 * N_SEQ):
        table = jnp.where(lane == head, columns[head], table)
    delta = table.T
    high = delta.astype(jnp.bfloat16).astype(jnp.float32)
    low = delta - high
    pad_rows = jnp.zeros((4, LANES), jnp.float32)
    pad_cols = jnp.zeros((8, WIDTH - LANES), jnp.float32)
    for copy in copies[2:]:
        copy.wait()
    for group in range(N_SEQ):
        two = slice(2 * group * HEAD_DIM, 2 * (group + 1) * HEAD_DIM)
        one = slice(group * HEAD_DIM, (group + 1) * HEAD_DIM)
        pair = slice(2 * group, 2 * group + 2)
        rows = jnp.concatenate(
            [query_ref[:, two], key_ref[:, one], value_ref[:, one], grad_ref[:, two]], axis=1
        )
        extra = jnp.concatenate([high[pair], low[pair], pad_rows], axis=0)
        extra = jnp.concatenate([extra, pad_cols], axis=1)
        packed_ref[group] = jnp.concatenate([rows.astype(jnp.float32), extra], axis=0).astype(
            jnp.bfloat16
        )


def wide(rows):
    return jnp.concatenate([rows[s : s + 1] for s in range(N_SEQ)], axis=1)


def index_kernel(list_ref, segment_ref, rows_ref, cols_ref, request_ref, most_ref):
    listed = list_ref[...]
    source = (listed // GROUP).astype(jnp.float32)
    local_row = (listed % ROWS).astype(jnp.float32)
    segment = segment_ref[...].astype(jnp.float32)
    blank = jnp.zeros((LANES - 8, LANES), jnp.float32)
    source_cols = jnp.concatenate([source, blank], axis=0).T
    before = iota((ROWS, ROWS), 0) < iota((ROWS, ROWS), 1)
    slots = []
    for s in range(N_SEQ):
        mine = source[s : s + 1]
        hits = ((source_cols[:, s : s + 1] == mine) & before).astype(jnp.float32)
        for earlier in range(s):
            hits = hits + (source_cols[:, earlier : earlier + 1] == mine).astype(jnp.float32)
        slots.append(jnp.sum(hits, axis=0, keepdims=True))
    slot = jnp.concatenate(slots, axis=0)
    blank = jnp.zeros((LANES - 24, LANES), jnp.float32)
    turned = jnp.concatenate([source, slot, segment, blank], axis=0).T
    lane = iota((ROWS, LANES), 1)
    picks = []
    for s in range(N_SEQ):
        columns = jnp.where(lane == 0, turned[:, s : s + 1], 0.0)
        columns = jnp.where(lane == 1, turned[:, 8 + s : 9 + s], columns)
        columns = jnp.where(lane == 2, turned[:, 16 + s : 17 + s], columns)
        cols_ref[s * ROWS : (s + 1) * ROWS, :] = columns
        picks.append((lane.astype(jnp.float32) == turned[:, 8 + s : 9 + s] + 1.0).astype(jnp.float32))
    rows_ref[0:8, :] = source
    rows_ref[8:16, :] = slot
    rows_ref[16:24, :] = segment
    pick = jnp.concatenate(picks, axis=0).astype(jnp.bfloat16)
    from_source = iota((N_DP, GROUP), 0).astype(jnp.float32) == wide(source)
    column = (iota((1, GROUP), 1) // ROWS).astype(jnp.float32)
    low = jnp.where(from_source, wide(local_row) + 1.0, 0.0).astype(jnp.bfloat16)
    high = jnp.where(from_source, column, 0.0).astype(jnp.bfloat16)
    table = nn_dot(low, pick) + float(ROWS) * nn_dot(high, pick)
    request_ref[...] = table.astype(jnp.int32)
    most_ref[0, 0] = (jnp.max(slot) + 1.0).astype(jnp.int32)


def request_picks(turned, group, first, capacity, width):
    column = jnp.concatenate(
        [turned[first : first + capacity, d : d + 1] for d in range(8 * group, 8 * group + 8)], axis=0
    )
    row_id = iota((8 * capacity, width), 1).astype(jnp.float32)
    return (column == row_id).astype(jnp.float32).astype(jnp.bfloat16)


def turned_requests(request_ref):
    blank = jnp.zeros((LANES - N_DP, LANES), jnp.float32)
    turned = jnp.concatenate([request_ref[...].astype(jnp.float32), blank], axis=0).T
    delta_id = (iota((LANES, LANES), 1) + GROUP).astype(jnp.float32)
    return jnp.where(iota((LANES, LANES), 0) == 0, delta_id, turned - 1.0)


def send_kernel(first, capacity, span, request_ref, rows_ref, sent_ref, ext_ref):
    group_rows = 8 * capacity
    turned = turned_requests(request_ref)
    for s in range(N_SEQ):
        ext_ref[s * ROWS : (s + 1) * ROWS, :] = rows_ref[s, :ROWS, span[0] : span[1]]
    for group in range(N_DP // 8):
        pick = request_picks(turned, group, first, capacity, GROUP)
        rows = slice(group * group_rows, (group + 1) * group_rows)
        sent_ref[rows, :] = nn_dot(pick, ext_ref[...]).astype(jnp.bfloat16)


def send_delta_kernel(span, most_ref, request_ref, rows_ref, sent_ref, pick_ref, ext_ref, place_ref):
    capacity = CAPACITY
    group_rows = 8 * capacity
    width = span[1] - span[0]
    turned = turned_requests(request_ref)
    deltas = []
    for s in range(N_SEQ):
        ext_ref[s * ROWS : (s + 1) * ROWS, :] = rows_ref[s, :ROWS, span[0] : span[1]]
        deltas.append(rows_ref[s, ROWS:, :LANES].astype(jnp.float32))
    delta = jnp.concatenate(deltas, axis=1)

    def places(pick, group, first, count):
        index = iota((8, 8 * count), 1)
        owner = index // count
        value = jnp.where(
            iota((8, 8 * count), 0) == 0, owner + 8 * group, index - owner * count + first
        )
        return nn_dot(value.astype(jnp.float32).astype(jnp.bfloat16), pick[:, :GROUP])

    place = jnp.zeros((8, GROUP), jnp.float32)
    for group in range(N_DP // 8):
        pick = request_picks(turned, group, 0, capacity, GROUP + LANES)
        pick_ref[group * group_rows : (group + 1) * group_rows, :] = pick
        place = place + places(pick, group, 0, capacity)
    place_ref[...] = place

    @pl.when(most_ref[0, 0] >= CAPACITY)
    def _():
        more = jnp.zeros((8, GROUP), jnp.float32)
        for group in range(N_DP // 8):
            pick = request_picks(turned, group, CAPACITY, EXTRA, GROUP)
            more = more + places(pick, group, CAPACITY, EXTRA)
        place_ref[...] += more

    place = place_ref[...]
    owner_of = place[0:1]
    slot_cols = []
    for s in range(N_SEQ):
        part = place[:, s * ROWS : (s + 1) * ROWS]
        blank = jnp.zeros((LANES - 8, LANES), jnp.float32)
        slot_cols.append(jnp.concatenate([part, blank], axis=0).T[:, 1:2])
    slot_col = jnp.concatenate(slot_cols, axis=0)
    lane = iota((GROUP, LANES), 1).astype(jnp.float32)
    to_owner = iota((N_DP, GROUP), 0).astype(jnp.float32) == owner_of
    tail = jnp.zeros((2 * N_DP, LANES), jnp.float32)
    for head in range(2):
        spread = jnp.concatenate(
            [jnp.where(to_owner, delta[c : c + 1], 0.0) for c in (head, 2 + head)], axis=0
        )
        slot_pick = (slot_col + (64.0 * head - 1.0) == lane).astype(jnp.float32)
        tail = tail + nn_dot(spread.astype(jnp.bfloat16), slot_pick.astype(jnp.bfloat16))
    tail = jnp.concatenate(
        [tail[:N_DP], tail[N_DP:], jnp.zeros((N_DP, width - 2 * LANES), jnp.float32)], axis=1
    )
    tail = jnp.concatenate([tail, jnp.zeros((LANES - N_DP, width), jnp.float32)], axis=0)
    ext_ref[GROUP:, :] = tail.astype(jnp.bfloat16)
    for group in range(N_DP // 8):
        rows = slice(group * group_rows, (group + 1) * group_rows)
        sent_ref[rows, :] = nn_dot(pick_ref[rows, :], ext_ref[...]).astype(jnp.bfloat16)


def step_pairs():
    order = []
    for block in range(GROUP // BLOCK):
        for key_block in [block] + list(range(block)):
            order.append((block, key_block))
    return order


def meeting(segment_ref, block, key_block):
    return segment_ref[(key_block + 1) * BLOCK - 1] == segment_ref[block * BLOCK]


def place_extra(most_ref, cols_ref, extra_ref, x_ref, span):
    @pl.when(most_ref[0, 0] >= CAPACITY)
    def _():
        slot_id = iota((BLOCK, N_DP * EXTRA), 1).astype(jnp.float32)
        for block in range(GROUP // BLOCK):
            rows = slice(block * BLOCK, (block + 1) * BLOCK)
            slot = cols_ref[rows, 1:2] - float(CAPACITY - 1)
            place = jnp.where(slot >= 0.0, cols_ref[rows, 0:1] * float(EXTRA) + slot, -1.0)
            pick = (place == slot_id).astype(jnp.float32).astype(jnp.bfloat16)
            x_ref[rows, :] += nn_dot(pick, extra_ref[:, span[0] : span[1]]).astype(jnp.bfloat16)


def weigh_kernel(
    segment_ref, most_ref, arrived_ref, extra_ref, rows_ref, cols_ref,
    x_ref, kt_ref, pick_ref, low_ref, slope_ref, weight_ref, squash_ref, total_ref,
):
    slots = N_DP * CAPACITY
    slot_id = iota((BLOCK, slots), 1).astype(jnp.float32)
    for block in range(GROUP // BLOCK):
        rows = slice(block * BLOCK, (block + 1) * BLOCK)
        slot = cols_ref[rows, 1:2] + 1.0
        place = jnp.where(slot < CAPACITY, cols_ref[rows, 0:1] * float(CAPACITY) + slot, -1.0)
        pick = (place == slot_id).astype(jnp.float32).astype(jnp.bfloat16)
        pick_ref[rows, :] = pick
        x_ref[rows, :] = nn_dot(pick, arrived_ref[...]).astype(jnp.bfloat16)
    place_extra(most_ref, cols_ref, extra_ref, x_ref, (0, 3 * HEAD_DIM))
    for block in range(GROUP // BLOCK):
        rows = slice(block * BLOCK, (block + 1) * BLOCK)
        kt_ref[:, rows] = x_ref[rows, 256:384].astype(jnp.float32).T.astype(jnp.bfloat16)
    segment = wide(rows_ref[16:24, :])
    causal = iota((BLOCK, BLOCK), 0) <= iota((BLOCK, BLOCK), 1)
    causal = jnp.concatenate([causal.astype(jnp.float32)] * 2, axis=1) > 0.0

    def weigh(block, key_block, first):
        rows = slice(block * BLOCK, (block + 1) * BLOCK)
        keys = slice(key_block * BLOCK, (key_block + 1) * BLOCK)
        queries = jnp.concatenate([x_ref[rows, 0:128], x_ref[rows, 128:256]], axis=0)
        segment_q = jnp.concatenate([segment[:, rows]] * 2, axis=1)
        score = nt_dot(x_ref[keys, 256:384], queries)
        squashed = jnp.tanh(score * (scaling / softcap))
        allowed = cols_ref[keys, 2:3] == segment_q
        if key_block == block:
            allowed = allowed & causal
        weights = jnp.where(allowed, jnp.exp(softcap * squashed), 0.0)
        weight_ref[keys, :] = weights
        squash_ref[keys, :] = squashed
        total = jnp.sum(weights, axis=0, keepdims=True)
        if first:
            total_ref[0:1, :] = total
        else:
            total_ref[0:1, :] += total

    def finish(step, key_block):
        keys = slice(key_block * BLOCK, (key_block + 1) * BLOCK)
        out = slice(step * BLOCK, (step + 1) * BLOCK)
        probabilities = weight_ref[keys, :] * (1.0 / total_ref[0:1, :])
        squashed = squash_ref[keys, :]
        low_ref[out, :] = probabilities.astype(jnp.bfloat16)
        slope_ref[out, :] = probabilities * (1.0 - squashed * squashed)

    steps = step_pairs()
    for block in range(GROUP // BLOCK):
        mine = [(step, pair[1]) for step, pair in enumerate(steps) if pair[0] == block]
        for step, key_block in mine:
            if key_block == block:
                weigh(block, key_block, True)
            else:
                pl.when(meeting(segment_ref, block, key_block))(
                    functools.partial(weigh, block, key_block, False)
                )
        for step, key_block in mine:
            if key_block == block:
                finish(step, key_block)
            else:
                pl.when(meeting(segment_ref, block, key_block))(
                    functools.partial(finish, step, key_block)
                )


def back_kernel(
    segment_ref, most_ref, arrived_ref, extra_ref, rows_ref, cols_ref, x_ref, kt_ref, pick_ref,
    low_ref, slope_ref, out_ref, y_ref, delta_ref, gqt_ref, gk_ref, gv_ref,
):
    slots = N_DP * CAPACITY
    for block in range(GROUP // BLOCK):
        rows = slice(block * BLOCK, (block + 1) * BLOCK)
        y_ref[rows, :] = nn_dot(pick_ref[rows, :], arrived_ref[...]).astype(jnp.bfloat16)
    place_extra(most_ref, cols_ref, extra_ref, y_ref, (3 * HEAD_DIM, 6 * HEAD_DIM))
    first = iota((LANES, slots), 0) * CAPACITY == iota((LANES, slots), 1)
    first = first.astype(jnp.float32).astype(jnp.bfloat16)
    parts = nn_dot(first, arrived_ref[:, : 2 * LANES])
    source = wide(rows_ref[0:8, :])
    slot = wide(rows_ref[8:16, :])
    from_source = iota((LANES, GROUP), 0).astype(jnp.float32) == source
    from_source = from_source.astype(jnp.float32).astype(jnp.bfloat16)
    high = parts[:, :LANES].T.astype(jnp.bfloat16)
    low = parts[:, LANES:].T.astype(jnp.bfloat16)
    both = nn_dot(high, from_source) + nn_dot(low, from_source)
    place = iota((LANES, GROUP), 0).astype(jnp.float32)
    for head in range(2):
        delta_ref[head : head + 1, :] = jnp.sum(
            jnp.where(place == slot + 64.0 * head, both, 0.0), axis=0, keepdims=True
        )
    gk_ref[...] = jnp.zeros_like(gk_ref)
    gv_ref[...] = jnp.zeros_like(gv_ref)

    def back(block, key_block, step):
        rows = slice(block * BLOCK, (block + 1) * BLOCK)
        keys = slice(key_block * BLOCK, (key_block + 1) * BLOCK)
        held = slice(step * BLOCK, (step + 1) * BLOCK)
        queries = jnp.concatenate([x_ref[rows, 0:128], x_ref[rows, 128:256]], axis=0)
        grads = jnp.concatenate([y_ref[rows, 128:256], y_ref[rows, 256:384]], axis=0)
        delta = jnp.concatenate([delta_ref[0:1, rows], delta_ref[1:2, rows]], axis=1)
        gv_ref[keys, :] += nn_dot(low_ref[held, :], grads)
        prob_grad = nt_dot(y_ref[keys, 0:128], grads)
        score_grad = (slope_ref[held, :] * (prob_grad - delta)).astype(jnp.bfloat16)
        gk_ref[keys, :] += nn_dot(score_grad, queries)
        part = nn_dot(kt_ref[:, keys], score_grad)
        if key_block == block:
            gqt_ref[...] = part
        else:
            gqt_ref[...] += part

    steps = step_pairs()
    for block in range(GROUP // BLOCK):
        rows = slice(block * BLOCK, (block + 1) * BLOCK)
        for step, pair in enumerate(steps):
            if pair[0] != block:
                continue
            run = functools.partial(back, block, pair[1], step)
            if pair[1] == block:
                run()
            else:
                pl.when(meeting(segment_ref, block, pair[1]))(run)
        turned = (gqt_ref[...].T * scaling).astype(jnp.bfloat16)
        out_ref[rows, 0:128] = turned[:BLOCK]
        out_ref[rows, 128:256] = turned[BLOCK:]
    out_ref[:, 256:384] = (gk_ref[...] * scaling).astype(jnp.bfloat16)
    out_ref[:, 384:512] = gv_ref[...].astype(jnp.bfloat16)


def unpack_kernel(returned_ref, query_ref, key_ref, value_ref):
    for group in range(N_SEQ):
        two = slice(2 * group * HEAD_DIM, 2 * (group + 1) * HEAD_DIM)
        one = slice(group * HEAD_DIM, (group + 1) * HEAD_DIM)
        query_ref[:, two] = returned_ref[group, :, 0:256]
        key_ref[:, one] = returned_ref[group, :, 256:384]
        value_ref[:, one] = returned_ref[group, :, 384:512]


def shape(dims, dtype=jnp.bfloat16):
    return jax.ShapeDtypeStruct(dims, dtype)


VMEM = pl.BlockSpec(memory_space=pltpu.VMEM)
SMEM = pl.BlockSpec(memory_space=pltpu.SMEM)


def cost(flops, moved, transcendentals=0):
    return pl.CostEstimate(flops=flops, bytes_accessed=moved, transcendentals=transcendentals)


def pack(query, key_rows, value_rows, attn_out, out_grad):
    return pl.pallas_call(
        pack_kernel,
        out_shape=shape((N_SEQ, ROWS + 8, WIDTH)),
        in_specs=[pl.BlockSpec(memory_space=pltpu.HBM)] * 5,
        out_specs=VMEM,
        scratch_shapes=[
            pltpu.VMEM((ROWS, 2048), jnp.bfloat16),
            pltpu.VMEM((ROWS, 1024), jnp.bfloat16),
            pltpu.VMEM((ROWS, 1024), jnp.bfloat16),
            pltpu.VMEM((ROWS, 2048), jnp.bfloat16),
            pltpu.VMEM((ROWS, 2048), jnp.bfloat16),
            pltpu.SemaphoreType.DMA((5,)),
        ],
        compiler_params=FULL,
        name="pack",
    )(query, key_rows, value_rows, attn_out, out_grad)


def index(pack_list, segments):
    vmem = pl.BlockSpec(memory_space=pltpu.VMEM)
    return pl.pallas_call(
        index_kernel,
        out_shape=(
            shape((24, LANES), jnp.float32),
            shape((GROUP, LANES), jnp.float32),
            shape((N_DP, LANES), jnp.int32),
            shape((1, 1), jnp.int32),
        ),
        out_specs=(vmem, vmem, vmem, pl.BlockSpec(memory_space=pltpu.SMEM)),
        compiler_params=PARAMS,
        name="index",
    )(pack_list, segments.reshape(N_SEQ, ROWS))


def send(first, capacity, span, request, head_rows):
    width = span[1] - span[0]
    return pl.pallas_call(
        functools.partial(send_kernel, first, capacity, span),
        out_shape=shape((N_DP * capacity, width)),
        scratch_shapes=[pltpu.VMEM((GROUP, width), jnp.bfloat16)],
        compiler_params=PARAMS,
        cost_estimate=cost(2 * N_DP * capacity * GROUP * width, 4_000_000),
        name="send",
    )(request, head_rows)


def send_delta(span, most, request, head_rows):
    width = span[1] - span[0]
    return pl.pallas_call(
        functools.partial(send_delta_kernel, span),
        out_shape=shape((N_DP * CAPACITY, width)),
        in_specs=[SMEM, VMEM, VMEM],
        scratch_shapes=[
            pltpu.VMEM((N_DP * CAPACITY, GROUP + LANES), jnp.bfloat16),
            pltpu.VMEM((GROUP + LANES, width), jnp.bfloat16),
            pltpu.VMEM((8, GROUP), jnp.float32),
        ],
        compiler_params=PARAMS,
        cost_estimate=cost(2 * N_DP * CAPACITY * GROUP * width, 4_000_000),
        name="send_delta",
    )(most, request, head_rows)


def weigh(segments, most, arrived, extra, rows, cols):
    steps = PAIRS * BLOCK
    return pl.pallas_call(
        weigh_kernel,
        out_shape=(
            shape((GROUP, 3 * HEAD_DIM)),
            shape((HEAD_DIM, GROUP)),
            shape((GROUP, N_DP * CAPACITY)),
            shape((steps, 2 * BLOCK)),
            shape((steps, 2 * BLOCK), jnp.float32),
        ),
        in_specs=[SMEM, SMEM, VMEM, VMEM, VMEM, VMEM],
        scratch_shapes=[
            pltpu.VMEM((GROUP, 2 * BLOCK), jnp.float32),
            pltpu.VMEM((GROUP, 2 * BLOCK), jnp.float32),
            pltpu.VMEM((8, 2 * BLOCK), jnp.float32),
        ],
        compiler_params=PARAMS,
        cost_estimate=cost(3_000_000_000, 10_000_000, 3_000_000),
        name="weigh",
    )(segments, most, arrived, extra, rows, cols)


def back(segments, most, arrived, extra, rows, cols, held):
    return pl.pallas_call(
        back_kernel,
        out_shape=shape((GROUP, 4 * HEAD_DIM)),
        in_specs=[SMEM, SMEM] + [VMEM] * 9,
        scratch_shapes=[
            pltpu.VMEM((GROUP, 3 * HEAD_DIM), jnp.bfloat16),
            pltpu.VMEM((8, GROUP), jnp.float32),
            pltpu.VMEM((HEAD_DIM, 2 * BLOCK), jnp.float32),
            pltpu.VMEM((GROUP, HEAD_DIM), jnp.float32),
            pltpu.VMEM((GROUP, HEAD_DIM), jnp.float32),
        ],
        compiler_params=PARAMS,
        name="back",
    )(segments, most, arrived, extra, rows, cols, *held)


def unpack(returned):
    return pl.pallas_call(
        unpack_kernel,
        out_shape=(shape((ROWS, 2048)), shape((ROWS, 1024)), shape((ROWS, 1024))),
        compiler_params=PARAMS,
        name="unpack",
    )(returned)


def relay(array):
    return lax.all_to_all(array, "dp", split_axis=0, concat_axis=0, tiled=True)


def local(query, key_rows, value_rows, attn_out, out_grad, source_row, segment_ids):
    packed = pack(query, key_rows, value_rows, attn_out, out_grad)
    packed, source_row = lax.optimization_barrier((packed, source_row))
    head_rows = lax.all_to_all(packed, "seq", split_axis=0, concat_axis=0, tiled=True)
    pack_list = lax.all_gather(source_row, "seq", axis=0)
    rows, cols, request, most = index(pack_list, segment_ids)
    request = relay(request)
    arrived_near = relay(send(0, CAPACITY, (0, 384), request, head_rows))
    arrived_far = relay(send_delta((384, 768), most, request, head_rows))
    extra = lax.cond(
        most[0, 0] >= CAPACITY,
        lambda request, head_rows: relay(send(CAPACITY, EXTRA, (0, 768), request, head_rows)),
        lambda request, head_rows: jnp.zeros((N_DP * EXTRA, WIDTH), jnp.bfloat16),
        request,
        head_rows,
    )
    held = weigh(segment_ids, most, arrived_near, extra, rows, cols)
    grads = back(segment_ids, most, arrived_far, extra, rows, cols, held)
    returned = lax.all_to_all(
        grads.reshape(N_SEQ, ROWS, 4 * HEAD_DIM), "seq", split_axis=0, concat_axis=0, tiled=True
    )
    return unpack(returned)


def solution(mesh):
    in_specs = (
        P(("dp", "seq"), None),
        P(("dp", "seq"), None),
        P(("dp", "seq"), None),
        P(("dp", "seq"), None),
        P(("dp", "seq"), None),
        P(("dp", "seq")),
        P("dp"),
    )
    out_specs = (P(("dp", "seq"), None), P(("dp", "seq"), None), P(("dp", "seq"), None))
    return jax.shard_map(local, mesh=mesh, in_specs=in_specs, out_specs=out_specs, check_vma=False)
```

```python
import functools

import jax
import jax.numpy as jnp
from jax import lax
from jax.experimental import pallas as pl
from jax.experimental.pallas import tpu as pltpu
from jax.sharding import PartitionSpec as P

HEAD_DIM = 128
N_DP = 32
N_SEQ = 8
ROWS = 128
GROUP = N_SEQ * ROWS
WIDTH = 6 * HEAD_DIM
LANES = 128
BLOCK = 256
CAPACITY = 56
EXTRA = 16

scaling = 1.0 / 12.0
softcap = 50.0

PARAMS = pltpu.CompilerParams(vmem_limit_bytes=28 * 1024 * 1024)
FULL = pltpu.CompilerParams(vmem_limit_bytes=60 * 1024 * 1024)


def iota(shape, dim):
    return lax.broadcasted_iota(jnp.int32, shape, dim)


def nt_dot(left, right):
    return lax.dot_general(left, right, (((1,), (1,)), ((), ())), preferred_element_type=jnp.float32)


def nn_dot(left, right):
    return jnp.dot(left, right, preferred_element_type=jnp.float32)


def pack_kernel(me_ref, query_hbm, key_hbm, value_hbm, out_hbm, grad_hbm, *refs):
    packed_refs = refs[:N_SEQ]
    query_ref, key_ref, value_ref, out_ref, grad_ref, delta_ref, sems = refs[N_SEQ:]
    pairs = (
        (grad_hbm, grad_ref),
        (out_hbm, out_ref),
        (query_hbm, query_ref),
        (key_hbm, key_ref),
        (value_hbm, value_ref),
    )
    copies = [
        pltpu.make_async_copy(source, target, sems.at[i])
        for i, (source, target) in enumerate(pairs)
    ]
    for copy in copies:
        copy.start()
    copies[0].wait()
    copies[1].wait()
    lane = iota((ROWS, LANES), 1)
    table = jnp.zeros((ROWS, LANES), jnp.float32)
    for head in range(2 * N_SEQ):
        cols = slice(head * HEAD_DIM, (head + 1) * HEAD_DIM)
        product = grad_ref[:, cols].astype(jnp.float32) * out_ref[:, cols].astype(jnp.float32)
        table = jnp.where(lane == head, jnp.sum(product, axis=1, keepdims=True), table)
    delta = table.T
    high = delta.astype(jnp.bfloat16).astype(jnp.float32)
    low = delta - high
    for group in range(N_SEQ):
        pair = slice(2 * group, 2 * group + 2)
        delta_ref[group] = jnp.concatenate(
            [high[pair], low[pair], jnp.zeros((4, LANES), jnp.float32)], axis=0
        )
    pad_cols = jnp.zeros((8, WIDTH - LANES), jnp.float32)
    for copy in copies[2:]:
        copy.wait()
    me = me_ref[0]
    for m in range(N_SEQ):
        group = jnp.bitwise_xor(me, m)
        two = pl.ds(pl.multiple_of(group * 256, 256), 256)
        one = pl.ds(pl.multiple_of(group * 128, 128), 128)
        rows = jnp.concatenate(
            [query_ref[:, two], key_ref[:, one], value_ref[:, one], grad_ref[:, two]], axis=1
        )
        extra = jnp.concatenate([delta_ref[group], pad_cols], axis=1)
        packed_refs[m][...] = jnp.concatenate([rows.astype(jnp.float32), extra], axis=0).astype(
            jnp.bfloat16
        )


def wide(rows):
    return jnp.concatenate([rows[s : s + 1] for s in range(N_SEQ)], axis=1)


def index_kernel(list_ref, segment_ref, rows_ref, cols_ref, request_ref, most_ref):
    listed = list_ref[...]
    source = (listed // GROUP).astype(jnp.float32)
    local_row = (listed % ROWS).astype(jnp.float32)
    segment = segment_ref[...].astype(jnp.float32)
    blank = jnp.zeros((LANES - 8, LANES), jnp.float32)
    source_cols = jnp.concatenate([source, blank], axis=0).T
    before = iota((ROWS, ROWS), 0) < iota((ROWS, ROWS), 1)
    slots = []
    for s in range(N_SEQ):
        mine = source[s : s + 1]
        hits = ((source_cols[:, s : s + 1] == mine) & before).astype(jnp.float32)
        for earlier in range(s):
            hits = hits + (source_cols[:, earlier : earlier + 1] == mine).astype(jnp.float32)
        slots.append(jnp.sum(hits, axis=0, keepdims=True))
    slot = jnp.concatenate(slots, axis=0)
    blank = jnp.zeros((LANES - 24, LANES), jnp.float32)
    turned = jnp.concatenate([source, slot, segment, blank], axis=0).T
    lane = iota((ROWS, LANES), 1)
    picks = []
    for s in range(N_SEQ):
        columns = jnp.where(lane == 0, turned[:, s : s + 1], 0.0)
        columns = jnp.where(lane == 1, turned[:, 8 + s : 9 + s], columns)
        columns = jnp.where(lane == 2, turned[:, 16 + s : 17 + s], columns)
        cols_ref[s * ROWS : (s + 1) * ROWS, :] = columns
        picks.append((lane.astype(jnp.float32) == turned[:, 8 + s : 9 + s] + 1.0).astype(jnp.float32))
    rows_ref[0:8, :] = source
    rows_ref[8:16, :] = slot
    rows_ref[16:24, :] = segment
    pick = jnp.concatenate(picks, axis=0).astype(jnp.bfloat16)
    from_source = iota((N_DP, GROUP), 0).astype(jnp.float32) == wide(source)
    column = (iota((1, GROUP), 1) // ROWS).astype(jnp.float32)
    low = jnp.where(from_source, wide(local_row) + 1.0, 0.0).astype(jnp.bfloat16)
    high = jnp.where(from_source, column, 0.0).astype(jnp.bfloat16)
    table = nn_dot(low, pick) + float(ROWS) * nn_dot(high, pick)
    request_ref[...] = table.astype(jnp.int32)
    most_ref[0, 0] = (jnp.max(slot) + 1.0).astype(jnp.int32)


def request_picks(turned, group, first, capacity, width):
    column = jnp.concatenate(
        [turned[first : first + capacity, d : d + 1] for d in range(8 * group, 8 * group + 8)], axis=0
    )
    row_id = iota((8 * capacity, width), 1).astype(jnp.float32)
    return (column == row_id).astype(jnp.float32).astype(jnp.bfloat16)


def turned_requests(request_ref):
    blank = jnp.zeros((LANES - N_DP, LANES), jnp.float32)
    turned = jnp.concatenate([request_ref[...].astype(jnp.float32), blank], axis=0).T
    delta_id = (iota((LANES, LANES), 1) + GROUP).astype(jnp.float32)
    return jnp.where(iota((LANES, LANES), 0) == 0, delta_id, turned - 1.0)


def join_columns(me_ref, parts, ext_ref, delta_ref):
    for m in range(N_SEQ):
        column = jnp.bitwise_xor(me_ref[0], m)
        ext_ref[pl.ds(pl.multiple_of(column * ROWS, ROWS), ROWS), :] = parts[m][:ROWS, :]
        if delta_ref is not None:
            delta_ref[column] = parts[m][ROWS:, :LANES].astype(jnp.float32)


def send_extra_kernel(me_ref, request_ref, *refs):
    parts, (sent_ref, ext_ref) = refs[:N_SEQ], refs[N_SEQ:]
    group_rows = 8 * EXTRA
    turned = turned_requests(request_ref)
    join_columns(me_ref, parts, ext_ref, None)
    for group in range(N_DP // 8):
        pick = request_picks(turned, group, CAPACITY, EXTRA, GROUP)
        rows = slice(group * group_rows, (group + 1) * group_rows)
        sent_ref[rows, :] = nn_dot(pick, ext_ref[...]).astype(jnp.bfloat16)


def send_kernel(me_ref, most_ref, request_ref, *refs):
    parts, (sent_ref, pick_ref, ext_ref, place_ref, delta_ref) = refs[:N_SEQ], refs[N_SEQ:]
    capacity = CAPACITY
    group_rows = 8 * capacity
    turned = turned_requests(request_ref)
    join_columns(me_ref, parts, ext_ref, delta_ref)
    delta = jnp.concatenate([delta_ref[s] for s in range(N_SEQ)], axis=1)

    def places(pick, group, first, count):
        index = iota((8, 8 * count), 1)
        owner = index // count
        value = jnp.where(
            iota((8, 8 * count), 0) == 0, owner + 8 * group, index - owner * count + first
        )
        return nn_dot(value.astype(jnp.float32).astype(jnp.bfloat16), pick[:, :GROUP])

    place = jnp.zeros((8, GROUP), jnp.float32)
    for group in range(N_DP // 8):
        pick = request_picks(turned, group, 0, capacity, GROUP + LANES)
        pick_ref[group * group_rows : (group + 1) * group_rows, :] = pick
        place = place + places(pick, group, 0, capacity)
    place_ref[...] = place

    @pl.when(most_ref[0, 0] >= CAPACITY)
    def _():
        more = jnp.zeros((8, GROUP), jnp.float32)
        for group in range(N_DP // 8):
            pick = request_picks(turned, group, CAPACITY, EXTRA, GROUP)
            more = more + places(pick, group, CAPACITY, EXTRA)
        place_ref[...] += more

    place = place_ref[...]
    owner_of = place[0:1]
    slot_cols = []
    for s in range(N_SEQ):
        part = place[:, s * ROWS : (s + 1) * ROWS]
        blank = jnp.zeros((LANES - 8, LANES), jnp.float32)
        slot_cols.append(jnp.concatenate([part, blank], axis=0).T[:, 1:2])
    slot_col = jnp.concatenate(slot_cols, axis=0)
    lane = iota((GROUP, LANES), 1).astype(jnp.float32)
    to_owner = iota((N_DP, GROUP), 0).astype(jnp.float32) == owner_of
    tail = jnp.zeros((2 * N_DP, LANES), jnp.float32)
    for head in range(2):
        spread = jnp.concatenate(
            [jnp.where(to_owner, delta[c : c + 1], 0.0) for c in (head, 2 + head)], axis=0
        )
        slot_pick = (slot_col + (64.0 * head - 1.0) == lane).astype(jnp.float32)
        tail = tail + nn_dot(spread.astype(jnp.bfloat16), slot_pick.astype(jnp.bfloat16))
    tail = jnp.concatenate(
        [tail[:N_DP], tail[N_DP:], jnp.zeros((N_DP, WIDTH - 2 * LANES), jnp.float32)], axis=1
    )
    tail = jnp.concatenate([tail, jnp.zeros((LANES - N_DP, WIDTH), jnp.float32)], axis=0)
    ext_ref[GROUP:, :] = tail.astype(jnp.bfloat16)
    for group in range(N_DP // 8):
        rows = slice(group * group_rows, (group + 1) * group_rows)
        sent_ref[rows, :] = nn_dot(pick_ref[rows, :], ext_ref[...]).astype(jnp.bfloat16)


def attend_kernel(
    segment_ref, most_ref, arrived_ref, extra_ref, rows_ref, cols_ref, out_ref,
    x_ref, kt_ref, delta_ref, weight_ref, squash_ref, total_ref, gqt_ref, gk_ref, gv_ref,
):
    slots = N_DP * CAPACITY
    blocks = GROUP // BLOCK
    slot_id = iota((BLOCK, slots), 1).astype(jnp.float32)
    for block in range(blocks):
        rows = slice(block * BLOCK, (block + 1) * BLOCK)
        slot = cols_ref[rows, 1:2] + 1.0
        place = jnp.where(slot < CAPACITY, cols_ref[rows, 0:1] * float(CAPACITY) + slot, -1.0)
        pick = (place == slot_id).astype(jnp.float32).astype(jnp.bfloat16)
        x_ref[rows, :] = nn_dot(pick, arrived_ref[...]).astype(jnp.bfloat16)

    @pl.when(most_ref[0, 0] >= CAPACITY)
    def _():
        extra_id = iota((BLOCK, N_DP * EXTRA), 1).astype(jnp.float32)
        for block in range(blocks):
            rows = slice(block * BLOCK, (block + 1) * BLOCK)
            slot = cols_ref[rows, 1:2] - float(CAPACITY - 1)
            place = jnp.where(slot >= 0.0, cols_ref[rows, 0:1] * float(EXTRA) + slot, -1.0)
            pick = (place == extra_id).astype(jnp.float32).astype(jnp.bfloat16)
            x_ref[rows, :] += nn_dot(pick, extra_ref[...]).astype(jnp.bfloat16)

    for block in range(blocks):
        rows = slice(block * BLOCK, (block + 1) * BLOCK)
        kt_ref[:, rows] = x_ref[rows, 256:384].astype(jnp.float32).T.astype(jnp.bfloat16)
    first = iota((LANES, slots), 0) * CAPACITY == iota((LANES, slots), 1)
    first = first.astype(jnp.float32).astype(jnp.bfloat16)
    parts = nn_dot(first, arrived_ref[:, : 2 * LANES])
    source = wide(rows_ref[0:8, :])
    slot = wide(rows_ref[8:16, :])
    segment = wide(rows_ref[16:24, :])
    from_source = iota((LANES, GROUP), 0).astype(jnp.float32) == source
    from_source = from_source.astype(jnp.float32).astype(jnp.bfloat16)
    high = parts[:, :LANES].T.astype(jnp.bfloat16)
    low = parts[:, LANES:].T.astype(jnp.bfloat16)
    both = nn_dot(high, from_source) + nn_dot(low, from_source)
    place = iota((LANES, GROUP), 0).astype(jnp.float32)
    for head in range(2):
        delta_ref[head : head + 1, :] = jnp.sum(
            jnp.where(place == slot + 64.0 * head, both, 0.0), axis=0, keepdims=True
        )
    gk_ref[...] = jnp.zeros_like(gk_ref)
    gv_ref[...] = jnp.zeros_like(gv_ref)
    causal = iota((BLOCK, BLOCK), 0) <= iota((BLOCK, BLOCK), 1)
    causal = jnp.concatenate([causal.astype(jnp.float32)] * 2, axis=1) > 0.0
    for block in range(blocks):
        rows = slice(block * BLOCK, (block + 1) * BLOCK)
        queries = jnp.concatenate([x_ref[rows, 0:128], x_ref[rows, 128:256]], axis=0)
        grads = jnp.concatenate([x_ref[rows, 512:640], x_ref[rows, 640:768]], axis=0)
        delta = jnp.concatenate([delta_ref[0:1, rows], delta_ref[1:2, rows]], axis=1)
        segment_q = jnp.concatenate([segment[:, rows]] * 2, axis=1)

        def weigh(key_block):
            keys = slice(key_block * BLOCK, (key_block + 1) * BLOCK)
            score = nt_dot(x_ref[keys, 256:384], queries)
            squashed = jnp.tanh(score * (scaling / softcap))
            allowed = cols_ref[keys, 2:3] == segment_q
            if key_block == block:
                allowed = allowed & causal
            weights = jnp.where(allowed, jnp.exp(softcap * squashed), 0.0)
            weight_ref[keys, :] = weights
            squash_ref[keys, :] = squashed
            total = jnp.sum(weights, axis=0, keepdims=True)
            if key_block == block:
                total_ref[0:1, :] = total
            else:
                total_ref[0:1, :] += total

        def back(key_block):
            keys = slice(key_block * BLOCK, (key_block + 1) * BLOCK)
            probabilities = weight_ref[keys, :] * (1.0 / total_ref[0:1, :])
            gv_ref[keys, :] += nn_dot(probabilities.astype(jnp.bfloat16), grads)
            prob_grad = nt_dot(x_ref[keys, 384:512], grads)
            squashed = squash_ref[keys, :]
            score_grad = probabilities * (prob_grad - delta) * (1.0 - squashed * squashed)
            score_grad = score_grad.astype(jnp.bfloat16)
            gk_ref[keys, :] += nn_dot(score_grad, queries)
            part = nn_dot(kt_ref[:, keys], score_grad)
            if key_block == block:
                gqt_ref[...] = part
            else:
                gqt_ref[...] += part

        first_segment = segment_ref[block * BLOCK]
        for step in (weigh, back):
            step(block)
            for key_block in range(block):
                meets = segment_ref[(key_block + 1) * BLOCK - 1] == first_segment
                pl.when(meets)(functools.partial(step, key_block))
        turned = (gqt_ref[...].T * scaling).astype(jnp.bfloat16)
        out_ref[rows, 0:128] = turned[:BLOCK]
        out_ref[rows, 128:256] = turned[BLOCK:]
    out_ref[:, 256:384] = (gk_ref[...] * scaling).astype(jnp.bfloat16)
    out_ref[:, 384:512] = gv_ref[...].astype(jnp.bfloat16)


def unpack_kernel(returned_ref, query_ref, key_ref, value_ref):
    for group in range(N_SEQ):
        two = slice(2 * group * HEAD_DIM, 2 * (group + 1) * HEAD_DIM)
        one = slice(group * HEAD_DIM, (group + 1) * HEAD_DIM)
        query_ref[:, two] = returned_ref[group, :, 0:256]
        key_ref[:, one] = returned_ref[group, :, 256:384]
        value_ref[:, one] = returned_ref[group, :, 384:512]


def shape(dims, dtype=jnp.bfloat16):
    return jax.ShapeDtypeStruct(dims, dtype)


VMEM = pl.BlockSpec(memory_space=pltpu.VMEM)
SMEM = pl.BlockSpec(memory_space=pltpu.SMEM)


def cost(flops, moved, transcendentals=0):
    return pl.CostEstimate(flops=flops, bytes_accessed=moved, transcendentals=transcendentals)


def pack(me, query, key_rows, value_rows, attn_out, out_grad):
    return pl.pallas_call(
        pack_kernel,
        out_shape=[shape((ROWS + 8, WIDTH))] * N_SEQ,
        in_specs=[SMEM] + [pl.BlockSpec(memory_space=pltpu.HBM)] * 5,
        out_specs=[VMEM] * N_SEQ,
        scratch_shapes=[
            pltpu.VMEM((ROWS, 2048), jnp.bfloat16),
            pltpu.VMEM((ROWS, 1024), jnp.bfloat16),
            pltpu.VMEM((ROWS, 1024), jnp.bfloat16),
            pltpu.VMEM((ROWS, 2048), jnp.bfloat16),
            pltpu.VMEM((ROWS, 2048), jnp.bfloat16),
            pltpu.VMEM((N_SEQ, 8, LANES), jnp.float32),
            pltpu.SemaphoreType.DMA((5,)),
        ],
        compiler_params=FULL,
        name="pack",
    )(me, query, key_rows, value_rows, attn_out, out_grad)


def index(pack_list, segments):
    vmem = pl.BlockSpec(memory_space=pltpu.VMEM)
    return pl.pallas_call(
        index_kernel,
        out_shape=(
            shape((24, LANES), jnp.float32),
            shape((GROUP, LANES), jnp.float32),
            shape((N_DP, LANES), jnp.int32),
            shape((1, 1), jnp.int32),
        ),
        out_specs=(vmem, vmem, vmem, pl.BlockSpec(memory_space=pltpu.SMEM)),
        compiler_params=PARAMS,
        name="index",
    )(pack_list, segments.reshape(N_SEQ, ROWS))


def send(me, most, request, parts):
    return pl.pallas_call(
        send_kernel,
        out_shape=shape((N_DP * CAPACITY, WIDTH)),
        in_specs=[SMEM, SMEM] + [VMEM] * 9,
        scratch_shapes=[
            pltpu.VMEM((N_DP * CAPACITY, GROUP + LANES), jnp.bfloat16),
            pltpu.VMEM((GROUP + LANES, WIDTH), jnp.bfloat16),
            pltpu.VMEM((8, GROUP), jnp.float32),
            pltpu.VMEM((N_SEQ, 8, LANES), jnp.float32),
        ],
        compiler_params=PARAMS,
        cost_estimate=cost(2 * N_DP * CAPACITY * GROUP * WIDTH, 4_000_000),
        name="send",
    )(me, most, request, *parts)


def send_extra(me, request, parts):
    return pl.pallas_call(
        send_extra_kernel,
        out_shape=shape((N_DP * EXTRA, WIDTH)),
        in_specs=[SMEM] + [VMEM] * 9,
        scratch_shapes=[pltpu.VMEM((GROUP, WIDTH), jnp.bfloat16)],
        compiler_params=PARAMS,
        name="send_extra",
    )(me, request, *parts)


def attend(segments, most, arrived, extra, rows, cols):
    return pl.pallas_call(
        attend_kernel,
        out_shape=shape((GROUP, 4 * HEAD_DIM)),
        in_specs=[SMEM, SMEM, VMEM, VMEM, VMEM, VMEM],
        scratch_shapes=[
            pltpu.VMEM((GROUP, WIDTH), jnp.bfloat16),
            pltpu.VMEM((HEAD_DIM, GROUP), jnp.bfloat16),
            pltpu.VMEM((8, GROUP), jnp.float32),
            pltpu.VMEM((GROUP, 2 * BLOCK), jnp.float32),
            pltpu.VMEM((GROUP, 2 * BLOCK), jnp.float32),
            pltpu.VMEM((8, 2 * BLOCK), jnp.float32),
            pltpu.VMEM((HEAD_DIM, 2 * BLOCK), jnp.float32),
            pltpu.VMEM((GROUP, HEAD_DIM), jnp.float32),
            pltpu.VMEM((GROUP, HEAD_DIM), jnp.float32),
        ],
        compiler_params=PARAMS,
        name="attend",
    )(segments, most, arrived, extra, rows, cols)


def unpack(returned):
    return pl.pallas_call(
        unpack_kernel,
        out_shape=(shape((ROWS, 2048)), shape((ROWS, 1024)), shape((ROWS, 1024))),
        compiler_params=PARAMS,
        name="unpack",
    )(returned)


def relay(array):
    return lax.all_to_all(array, "dp", split_axis=0, concat_axis=0, tiled=True)


def local(query, key_rows, value_rows, attn_out, out_grad, source_row, segment_ids):
    me = lax.axis_index("seq").reshape(1)
    packed = pack(me, query, key_rows, value_rows, attn_out, out_grad)
    packed, source_row = lax.optimization_barrier((packed, source_row))
    parts = [packed[0]]
    for m in range(1, N_SEQ):
        parts.append(lax.ppermute(packed[m], "seq", [(s, s ^ m) for s in range(N_SEQ)]))
    pack_list = lax.all_gather(source_row, "seq", axis=0)
    rows, cols, request, most = index(pack_list, segment_ids)
    request = relay(request)
    arrived = relay(send(me, most, request, parts))
    extra = lax.cond(
        most[0, 0] >= CAPACITY,
        lambda request, *parts: relay(send_extra(me, request, parts)),
        lambda request, *parts: jnp.zeros((N_DP * EXTRA, WIDTH), jnp.bfloat16),
        request,
        *parts,
    )
    grads = attend(segment_ids, most, arrived, extra, rows, cols)
    returned = lax.all_to_all(
        grads.reshape(N_SEQ, ROWS, 4 * HEAD_DIM), "seq", split_axis=0, concat_axis=0, tiled=True
    )
    return unpack(returned)


def solution(mesh):
    in_specs = (
        P(("dp", "seq"), None),
        P(("dp", "seq"), None),
        P(("dp", "seq"), None),
        P(("dp", "seq"), None),
        P(("dp", "seq"), None),
        P(("dp", "seq")),
        P("dp"),
    )
    out_specs = (P(("dp", "seq"), None), P(("dp", "seq"), None), P(("dp", "seq"), None))
    return jax.shard_map(local, mesh=mesh, in_specs=in_specs, out_specs=out_specs, check_vma=False)
```

```python
import functools

import jax
import jax.numpy as jnp
from jax import lax
from jax.experimental import pallas as pl
from jax.experimental.pallas import tpu as pltpu
from jax.sharding import PartitionSpec as P

HEAD_DIM = 128
N_DP = 32
N_SEQ = 8
ROWS = 128
GROUP = N_SEQ * ROWS
WIDTH = 6 * HEAD_DIM
LANES = 128
BLOCK = 256
CAPACITY = 56
EXTRA = 16

scaling = 1.0 / 12.0
softcap = 50.0

PARAMS = pltpu.CompilerParams(vmem_limit_bytes=28 * 1024 * 1024)
FULL = pltpu.CompilerParams(vmem_limit_bytes=60 * 1024 * 1024)


def iota(shape, dim):
    return lax.broadcasted_iota(jnp.int32, shape, dim)


def nt_dot(left, right):
    return lax.dot_general(left, right, (((1,), (1,)), ((), ())), preferred_element_type=jnp.float32)


def nn_dot(left, right):
    return jnp.dot(left, right, preferred_element_type=jnp.float32)


def pack_kernel(me_ref, query_hbm, key_hbm, value_hbm, out_hbm, grad_hbm, *refs):
    packed_refs = refs[:N_SEQ]
    query_ref, key_ref, value_ref, out_ref, grad_ref, delta_ref, sems = refs[N_SEQ:]
    pairs = (
        (grad_hbm, grad_ref),
        (out_hbm, out_ref),
        (query_hbm, query_ref),
        (key_hbm, key_ref),
        (value_hbm, value_ref),
    )
    copies = [
        pltpu.make_async_copy(source, target, sems.at[i])
        for i, (source, target) in enumerate(pairs)
    ]
    for copy in copies:
        copy.start()
    copies[0].wait()
    copies[1].wait()
    lane = iota((ROWS, LANES), 1)
    table = jnp.zeros((ROWS, LANES), jnp.float32)
    for head in range(2 * N_SEQ):
        cols = slice(head * HEAD_DIM, (head + 1) * HEAD_DIM)
        product = grad_ref[:, cols].astype(jnp.float32) * out_ref[:, cols].astype(jnp.float32)
        table = jnp.where(lane == head, jnp.sum(product, axis=1, keepdims=True), table)
    delta = table.T
    high = delta.astype(jnp.bfloat16).astype(jnp.float32)
    low = delta - high
    for group in range(N_SEQ):
        pair = slice(2 * group, 2 * group + 2)
        delta_ref[group] = jnp.concatenate(
            [high[pair], low[pair], jnp.zeros((4, LANES), jnp.float32)], axis=0
        )
    pad_cols = jnp.zeros((8, WIDTH - LANES), jnp.float32)
    for copy in copies[2:]:
        copy.wait()
    me = me_ref[0]
    for m in range(N_SEQ):
        group = jnp.bitwise_xor(me, m)
        two = pl.ds(pl.multiple_of(group * 256, 256), 256)
        one = pl.ds(pl.multiple_of(group * 128, 128), 128)
        rows = jnp.concatenate(
            [query_ref[:, two], key_ref[:, one], value_ref[:, one], grad_ref[:, two]], axis=1
        )
        extra = jnp.concatenate([delta_ref[group], pad_cols], axis=1)
        packed_refs[m][...] = jnp.concatenate([rows.astype(jnp.float32), extra], axis=0).astype(
            jnp.bfloat16
        )


def wide(rows):
    return jnp.concatenate([rows[s : s + 1] for s in range(N_SEQ)], axis=1)


def index_kernel(me_ref, segment_ref, *refs):
    lists, (rows_ref, cols_ref, request_ref, most_ref, list_ref) = refs[:N_SEQ], refs[N_SEQ:]
    for m in range(N_SEQ):
        list_ref[pl.ds(jnp.bitwise_xor(me_ref[0], m), 1), :] = lists[m][...]
    listed = list_ref[...]
    source = (listed // GROUP).astype(jnp.float32)
    local_row = (listed % ROWS).astype(jnp.float32)
    segment = segment_ref[...].astype(jnp.float32)
    blank = jnp.zeros((LANES - 8, LANES), jnp.float32)
    source_cols = jnp.concatenate([source, blank], axis=0).T
    before = iota((ROWS, ROWS), 0) < iota((ROWS, ROWS), 1)
    slots = []
    for s in range(N_SEQ):
        mine = source[s : s + 1]
        hits = ((source_cols[:, s : s + 1] == mine) & before).astype(jnp.float32)
        for earlier in range(s):
            hits = hits + (source_cols[:, earlier : earlier + 1] == mine).astype(jnp.float32)
        slots.append(jnp.sum(hits, axis=0, keepdims=True))
    slot = jnp.concatenate(slots, axis=0)
    blank = jnp.zeros((LANES - 24, LANES), jnp.float32)
    turned = jnp.concatenate([source, slot, segment, blank], axis=0).T
    lane = iota((ROWS, LANES), 1)
    picks = []
    for s in range(N_SEQ):
        columns = jnp.where(lane == 0, turned[:, s : s + 1], 0.0)
        columns = jnp.where(lane == 1, turned[:, 8 + s : 9 + s], columns)
        columns = jnp.where(lane == 2, turned[:, 16 + s : 17 + s], columns)
        cols_ref[s * ROWS : (s + 1) * ROWS, :] = columns
        picks.append((lane.astype(jnp.float32) == turned[:, 8 + s : 9 + s] + 1.0).astype(jnp.float32))
    rows_ref[0:8, :] = source
    rows_ref[8:16, :] = slot
    rows_ref[16:24, :] = segment
    pick = jnp.concatenate(picks, axis=0).astype(jnp.bfloat16)
    from_source = iota((N_DP, GROUP), 0).astype(jnp.float32) == wide(source)
    column = (iota((1, GROUP), 1) // ROWS).astype(jnp.float32)
    low = jnp.where(from_source, wide(local_row) + 1.0, 0.0).astype(jnp.bfloat16)
    high = jnp.where(from_source, column, 0.0).astype(jnp.bfloat16)
    table = nn_dot(low, pick) + float(ROWS) * nn_dot(high, pick)
    request_ref[...] = table.astype(jnp.int32)
    most_ref[0, 0] = (jnp.max(slot) + 1.0).astype(jnp.int32)


def spread_requests(request_ref, first, capacity, column_ref):
    blank = jnp.zeros((LANES - N_DP, LANES), jnp.float32)
    turned = jnp.concatenate([request_ref[...].astype(jnp.float32), blank], axis=0).T - 1.0
    for owner in range(N_DP):
        column_ref[owner * capacity : (owner + 1) * capacity, :] = jnp.broadcast_to(
            turned[first : first + capacity, owner : owner + 1], (capacity, LANES)
        )


def group_picks(column_ref, group, group_rows):
    column = column_ref[pl.ds(pl.multiple_of(group * group_rows, group_rows), group_rows), 0:1]
    row_id = iota((group_rows, GROUP), 1).astype(jnp.float32)
    return (column == row_id).astype(jnp.float32).astype(jnp.bfloat16)


def join_columns(me_ref, parts, ext_ref, delta_ref):
    for m in range(N_SEQ):
        column = jnp.bitwise_xor(me_ref[0], m)
        ext_ref[pl.ds(pl.multiple_of(column * ROWS, ROWS), ROWS), :] = parts[m][:ROWS, :]
        if delta_ref is not None:
            delta_ref[column] = parts[m][ROWS:, :LANES].astype(jnp.float32)


def send_extra_kernel(me_ref, request_ref, *refs):
    parts, (sent_ref, ext_ref, column_ref) = refs[:N_SEQ], refs[N_SEQ:]
    group_rows = 8 * EXTRA
    spread_requests(request_ref, CAPACITY, EXTRA, column_ref)
    join_columns(me_ref, parts, ext_ref, None)

    def fill(group, carry):
        pick = group_picks(column_ref, group, group_rows)
        rows = pl.ds(pl.multiple_of(group * group_rows, group_rows), group_rows)
        sent_ref[rows, :] = nn_dot(pick, ext_ref[...]).astype(jnp.bfloat16)
        return carry

    lax.fori_loop(0, N_DP // 8, fill, 0)


def send_kernel(me_ref, most_ref, request_ref, *refs):
    parts = refs[:N_SEQ]
    sent_ref, pick_ref, ext_ref, column_ref, place_ref, delta_ref, tail_ref, more_ref = refs[N_SEQ:]
    capacity = CAPACITY
    group_rows = 8 * capacity
    spread_requests(request_ref, 0, capacity, column_ref)
    join_columns(me_ref, parts, ext_ref, delta_ref)
    delta = jnp.concatenate([delta_ref[s] for s in range(N_SEQ)], axis=1)
    place_ref[...] = jnp.zeros_like(place_ref)

    def add_places(pick, group, first, count):
        index = iota((8, 8 * count), 1)
        owner = index // count
        value = jnp.where(
            iota((8, 8 * count), 0) == 0, owner + 8 * group, index - owner * count + first
        )
        place_ref[...] += nn_dot(value.astype(jnp.float32).astype(jnp.bfloat16), pick)

    def pick_group(group, carry):
        pick = group_picks(column_ref, group, group_rows)
        pick_ref[pl.ds(pl.multiple_of(group * group_rows, group_rows), group_rows), :] = pick
        add_places(pick, group, 0, capacity)
        return carry

    lax.fori_loop(0, N_DP // 8, pick_group, 0)

    @pl.when(most_ref[0, 0] >= CAPACITY)
    def _():
        spread_requests(request_ref, CAPACITY, EXTRA, more_ref)

        def pick_more(group, carry):
            add_places(group_picks(more_ref, group, 8 * EXTRA), group, CAPACITY, EXTRA)
            return carry

        lax.fori_loop(0, N_DP // 8, pick_more, 0)

    place = place_ref[...]
    owner_of = place[0:1]
    slot_cols = []
    for s in range(N_SEQ):
        part = place[:, s * ROWS : (s + 1) * ROWS]
        blank = jnp.zeros((LANES - 8, LANES), jnp.float32)
        slot_cols.append(jnp.concatenate([part, blank], axis=0).T[:, 1:2])
    slot_col = jnp.concatenate(slot_cols, axis=0)
    lane = iota((GROUP, LANES), 1).astype(jnp.float32)
    to_owner = iota((N_DP, GROUP), 0).astype(jnp.float32) == owner_of
    tail = jnp.zeros((2 * N_DP, LANES), jnp.float32)
    for head in range(2):
        spread = jnp.concatenate(
            [jnp.where(to_owner, delta[c : c + 1], 0.0) for c in (head, 2 + head)], axis=0
        )
        slot_pick = (slot_col + (64.0 * head - 1.0) == lane).astype(jnp.float32)
        tail = tail + nn_dot(spread.astype(jnp.bfloat16), slot_pick.astype(jnp.bfloat16))
    tail_ref[...] = jnp.concatenate([tail[:N_DP], tail[N_DP:]], axis=1)

    def fill(group, carry):
        rows = pl.ds(pl.multiple_of(group * group_rows, group_rows), group_rows)
        sent = nn_dot(pick_ref[rows, :], ext_ref[...])
        tails = tail_ref[pl.ds(pl.multiple_of(8 * group, 8), 8), :]
        tails = jnp.concatenate(
            [jnp.broadcast_to(tails[j : j + 1], (capacity, 2 * LANES)) for j in range(8)], axis=0
        )
        index = iota((group_rows, 2 * LANES), 0)
        left = jnp.where(index % capacity == 0, tails, sent[:, : 2 * LANES])
        sent_ref[rows, : 2 * LANES] = left.astype(jnp.bfloat16)
        sent_ref[rows, 2 * LANES :] = sent[:, 2 * LANES :].astype(jnp.bfloat16)
        return carry

    lax.fori_loop(0, N_DP // 8, fill, 0)


def attend_kernel(
    segment_ref, most_ref, arrived_ref, extra_ref, rows_ref, cols_ref, out_ref,
    x_ref, kt_ref, lanes_ref, query_ref, grad_ref, weight_ref, squash_ref, total_ref, gqt_ref,
    gk_ref, gv_ref,
):
    slots = N_DP * CAPACITY
    blocks = GROUP // BLOCK

    def span(block):
        return pl.ds(pl.multiple_of(block * BLOCK, BLOCK), BLOCK)

    def gather(block, carry):
        rows = span(block)
        slot_id = iota((BLOCK, slots), 1).astype(jnp.float32)
        slot = cols_ref[rows, 1:2] + 1.0
        place = jnp.where(slot < CAPACITY, cols_ref[rows, 0:1] * float(CAPACITY) + slot, -1.0)
        pick = (place == slot_id).astype(jnp.float32).astype(jnp.bfloat16)
        x_ref[rows, :] = nn_dot(pick, arrived_ref[...]).astype(jnp.bfloat16)
        return carry

    def gather_extra(block, carry):
        rows = span(block)
        extra_id = iota((BLOCK, N_DP * EXTRA), 1).astype(jnp.float32)
        slot = cols_ref[rows, 1:2] - float(CAPACITY - 1)
        place = jnp.where(slot >= 0.0, cols_ref[rows, 0:1] * float(EXTRA) + slot, -1.0)
        pick = (place == extra_id).astype(jnp.float32).astype(jnp.bfloat16)
        x_ref[rows, :] += nn_dot(pick, extra_ref[...]).astype(jnp.bfloat16)
        return carry

    def turn_keys(block, carry):
        rows = span(block)
        kt_ref[:, rows] = x_ref[rows, 256:384].astype(jnp.float32).T.astype(jnp.bfloat16)
        return carry

    lax.fori_loop(0, blocks, gather, 0)

    @pl.when(most_ref[0, 0] >= CAPACITY)
    def _():
        lax.fori_loop(0, blocks, gather_extra, 0)

    lax.fori_loop(0, blocks, turn_keys, 0)
    first = iota((LANES, slots), 0) * CAPACITY == iota((LANES, slots), 1)
    first = first.astype(jnp.float32).astype(jnp.bfloat16)
    parts = nn_dot(first, arrived_ref[:, : 2 * LANES])
    source = wide(rows_ref[0:8, :])
    slot = wide(rows_ref[8:16, :])
    from_source = iota((LANES, GROUP), 0).astype(jnp.float32) == source
    from_source = from_source.astype(jnp.float32).astype(jnp.bfloat16)
    high = parts[:, :LANES].T.astype(jnp.bfloat16)
    low = parts[:, LANES:].T.astype(jnp.bfloat16)
    both = nn_dot(high, from_source) + nn_dot(low, from_source)
    place = iota((LANES, GROUP), 0).astype(jnp.float32)
    for head in range(2):
        lanes_ref[head : head + 1, :] = jnp.sum(
            jnp.where(place == slot + 64.0 * head, both, 0.0), axis=0, keepdims=True
        )
    lanes_ref[2:3, :] = wide(rows_ref[16:24, :])
    gk_ref[...] = jnp.zeros_like(gk_ref)
    gv_ref[...] = jnp.zeros_like(gv_ref)

    def attend_block(block, carry):
        rows = span(block)
        query_ref[:BLOCK, :] = x_ref[rows, 0:128]
        query_ref[BLOCK:, :] = x_ref[rows, 128:256]
        grad_ref[:BLOCK, :] = x_ref[rows, 512:640]
        grad_ref[BLOCK:, :] = x_ref[rows, 640:768]
        total_ref[...] = jnp.zeros_like(total_ref)
        gqt_ref[...] = jnp.zeros_like(gqt_ref)
        first_segment = segment_ref[block * BLOCK]
        start = jnp.int32(0)
        for key_block in range(blocks - 1):
            ends = segment_ref[(key_block + 1) * BLOCK - 1] < first_segment
            start = start + jnp.where(ends & (key_block < block), 1, 0)

        def weigh(key_block, carry):
            keys = span(key_block)
            score = nt_dot(x_ref[keys, 256:384], query_ref[...])
            squashed = jnp.tanh(score * (scaling / softcap))
            segment_q = jnp.concatenate([lanes_ref[2:3, rows]] * 2, axis=1)
            ahead = iota((BLOCK, BLOCK), 0) - iota((BLOCK, BLOCK), 1)
            ahead = jnp.concatenate([ahead, ahead], axis=1)
            allowed = (cols_ref[keys, 2:3] == segment_q) & (ahead <= (block - key_block) * BLOCK)
            weights = jnp.where(allowed, jnp.exp(softcap * squashed), 0.0)
            weight_ref[keys, :] = weights
            squash_ref[keys, :] = squashed
            total_ref[0:1, :] += jnp.sum(weights, axis=0, keepdims=True)
            return carry

        def back(key_block, carry):
            keys = span(key_block)
            delta = jnp.concatenate([lanes_ref[0:1, rows], lanes_ref[1:2, rows]], axis=1)
            probabilities = weight_ref[keys, :] * total_ref[0:1, :]
            gv_ref[keys, :] += nn_dot(probabilities.astype(jnp.bfloat16), grad_ref[...])
            prob_grad = nt_dot(x_ref[keys, 384:512], grad_ref[...])
            squashed = squash_ref[keys, :]
            score_grad = probabilities * (prob_grad - delta) * (1.0 - squashed * squashed)
            score_grad = score_grad.astype(jnp.bfloat16)
            gk_ref[keys, :] += nn_dot(score_grad, query_ref[...])
            gqt_ref[...] += nn_dot(kt_ref[:, keys], score_grad)
            return carry

        lax.fori_loop(start, block + 1, weigh, 0)
        total_ref[...] = 1.0 / total_ref[...]
        lax.fori_loop(start, block + 1, back, 0)
        turned = (gqt_ref[...].T * scaling).astype(jnp.bfloat16)
        out_ref[rows, 0:128] = turned[:BLOCK]
        out_ref[rows, 128:256] = turned[BLOCK:]
        return carry

    lax.fori_loop(0, blocks, attend_block, 0)
    out_ref[:, 256:384] = (gk_ref[...] * scaling).astype(jnp.bfloat16)
    out_ref[:, 384:512] = gv_ref[...].astype(jnp.bfloat16)


def unpack_kernel(returned_ref, query_ref, key_ref, value_ref):
    for group in range(N_SEQ):
        two = slice(2 * group * HEAD_DIM, 2 * (group + 1) * HEAD_DIM)
        one = slice(group * HEAD_DIM, (group + 1) * HEAD_DIM)
        query_ref[:, two] = returned_ref[group, :, 0:256]
        key_ref[:, one] = returned_ref[group, :, 256:384]
        value_ref[:, one] = returned_ref[group, :, 384:512]


def shape(dims, dtype=jnp.bfloat16):
    return jax.ShapeDtypeStruct(dims, dtype)


VMEM = pl.BlockSpec(memory_space=pltpu.VMEM)
SMEM = pl.BlockSpec(memory_space=pltpu.SMEM)


def cost(flops, moved, transcendentals=0):
    return pl.CostEstimate(flops=flops, bytes_accessed=moved, transcendentals=transcendentals)


def pack(me, query, key_rows, value_rows, attn_out, out_grad):
    return pl.pallas_call(
        pack_kernel,
        out_shape=[shape((ROWS + 8, WIDTH))] * N_SEQ,
        in_specs=[SMEM] + [pl.BlockSpec(memory_space=pltpu.HBM)] * 5,
        out_specs=[VMEM] * N_SEQ,
        scratch_shapes=[
            pltpu.VMEM((ROWS, 2048), jnp.bfloat16),
            pltpu.VMEM((ROWS, 1024), jnp.bfloat16),
            pltpu.VMEM((ROWS, 1024), jnp.bfloat16),
            pltpu.VMEM((ROWS, 2048), jnp.bfloat16),
            pltpu.VMEM((ROWS, 2048), jnp.bfloat16),
            pltpu.VMEM((N_SEQ, 8, LANES), jnp.float32),
            pltpu.SemaphoreType.DMA((5,)),
        ],
        compiler_params=FULL,
        name="pack",
    )(me, query, key_rows, value_rows, attn_out, out_grad)


def index(me, segments, lists):
    return pl.pallas_call(
        index_kernel,
        out_shape=(
            shape((24, LANES), jnp.float32),
            shape((GROUP, LANES), jnp.float32),
            shape((N_DP, LANES), jnp.int32),
            shape((1, 1), jnp.int32),
        ),
        in_specs=[SMEM] + [VMEM] * 9,
        out_specs=(VMEM, VMEM, VMEM, SMEM),
        scratch_shapes=[pltpu.VMEM((N_SEQ, LANES), jnp.int32)],
        compiler_params=PARAMS,
        name="index",
    )(me, segments.reshape(N_SEQ, ROWS), *lists)


def send(me, most, request, parts):
    return pl.pallas_call(
        send_kernel,
        out_shape=shape((N_DP * CAPACITY, WIDTH)),
        in_specs=[SMEM, SMEM] + [VMEM] * 9,
        scratch_shapes=[
            pltpu.VMEM((N_DP * CAPACITY, GROUP), jnp.bfloat16),
            pltpu.VMEM((GROUP, WIDTH), jnp.bfloat16),
            pltpu.VMEM((N_DP * CAPACITY, LANES), jnp.float32),
            pltpu.VMEM((8, GROUP), jnp.float32),
            pltpu.VMEM((N_SEQ, 8, LANES), jnp.float32),
            pltpu.VMEM((N_DP, 2 * LANES), jnp.float32),
            pltpu.VMEM((N_DP * EXTRA, LANES), jnp.float32),
        ],
        compiler_params=PARAMS,
        cost_estimate=cost(2 * N_DP * CAPACITY * GROUP * WIDTH, 4_000_000),
        name="send",
    )(me, most, request, *parts)


def send_extra(me, request, parts):
    return pl.pallas_call(
        send_extra_kernel,
        out_shape=shape((N_DP * EXTRA, WIDTH)),
        in_specs=[SMEM] + [VMEM] * 9,
        scratch_shapes=[
            pltpu.VMEM((GROUP, WIDTH), jnp.bfloat16),
            pltpu.VMEM((N_DP * EXTRA, LANES), jnp.float32),
        ],
        compiler_params=PARAMS,
        name="send_extra",
    )(me, request, *parts)


def attend(segments, most, arrived, extra, rows, cols):
    return pl.pallas_call(
        attend_kernel,
        out_shape=shape((GROUP, 4 * HEAD_DIM)),
        in_specs=[SMEM, SMEM, VMEM, VMEM, VMEM, VMEM],
        scratch_shapes=[
            pltpu.VMEM((GROUP, WIDTH), jnp.bfloat16),
            pltpu.VMEM((HEAD_DIM, GROUP), jnp.bfloat16),
            pltpu.VMEM((8, GROUP), jnp.float32),
            pltpu.VMEM((2 * BLOCK, HEAD_DIM), jnp.bfloat16),
            pltpu.VMEM((2 * BLOCK, HEAD_DIM), jnp.bfloat16),
            pltpu.VMEM((GROUP, 2 * BLOCK), jnp.float32),
            pltpu.VMEM((GROUP, 2 * BLOCK), jnp.float32),
            pltpu.VMEM((8, 2 * BLOCK), jnp.float32),
            pltpu.VMEM((HEAD_DIM, 2 * BLOCK), jnp.float32),
            pltpu.VMEM((GROUP, HEAD_DIM), jnp.float32),
            pltpu.VMEM((GROUP, HEAD_DIM), jnp.float32),
        ],
        compiler_params=PARAMS,
        name="attend",
    )(segments, most, arrived, extra, rows, cols)


def unpack(returned):
    return pl.pallas_call(
        unpack_kernel,
        out_shape=(shape((ROWS, 2048)), shape((ROWS, 1024)), shape((ROWS, 1024))),
        compiler_params=PARAMS,
        name="unpack",
    )(returned)


def relay(array):
    return lax.all_to_all(array, "dp", split_axis=0, concat_axis=0, tiled=True)


def local(query, key_rows, value_rows, attn_out, out_grad, source_row, segment_ids):
    me = lax.axis_index("seq").reshape(1)

    def swap(array, m):
        return lax.ppermute(array, "seq", [(s, s ^ m) for s in range(N_SEQ)]) if m else array

    lists = [swap(source_row.reshape(1, ROWS), m) for m in range(N_SEQ)]
    packed = pack(me, query, key_rows, value_rows, attn_out, out_grad)
    packed, lists = lax.optimization_barrier((packed, lists))
    parts = [swap(packed[m], m) for m in range(N_SEQ)]
    rows, cols, request, most = index(me, segment_ids, lists)
    request = relay(request)
    arrived = relay(send(me, most, request, parts))
    extra = lax.cond(
        most[0, 0] >= CAPACITY,
        lambda request, *parts: relay(send_extra(me, request, parts)),
        lambda request, *parts: jnp.zeros((N_DP * EXTRA, WIDTH), jnp.bfloat16),
        request,
        *parts,
    )
    grads = attend(segment_ids, most, arrived, extra, rows, cols)
    returned = lax.all_to_all(
        grads.reshape(N_SEQ, ROWS, 4 * HEAD_DIM), "seq", split_axis=0, concat_axis=0, tiled=True
    )
    return unpack(returned)


def solution(mesh):
    in_specs = (
        P(("dp", "seq"), None),
        P(("dp", "seq"), None),
        P(("dp", "seq"), None),
        P(("dp", "seq"), None),
        P(("dp", "seq"), None),
        P(("dp", "seq")),
        P("dp"),
    )
    out_specs = (P(("dp", "seq"), None), P(("dp", "seq"), None), P(("dp", "seq"), None))
    return jax.shard_map(local, mesh=mesh, in_specs=in_specs, out_specs=out_specs, check_vma=False)
```

```python
import functools

import jax
import jax.numpy as jnp
from jax import lax
from jax.experimental import pallas as pl
from jax.experimental.pallas import tpu as pltpu
from jax.sharding import PartitionSpec as P

HEAD_DIM = 128
N_DP = 32
N_Z = 8
N_X = 4
N_SEQ = 8
ROWS = 128
GROUP = N_SEQ * ROWS
WIDTH = 6 * HEAD_DIM
LANES = 128
BLOCK = 256
CAPACITY = 56
EXTRA = 16

scaling = 1.0 / 12.0
softcap = 50.0

PARAMS = pltpu.CompilerParams(vmem_limit_bytes=28 * 1024 * 1024)
FULL = pltpu.CompilerParams(vmem_limit_bytes=60 * 1024 * 1024)


def iota(shape, dim):
    return lax.broadcasted_iota(jnp.int32, shape, dim)


def nt_dot(left, right):
    return lax.dot_general(left, right, (((1,), (1,)), ((), ())), preferred_element_type=jnp.float32)


def nn_dot(left, right):
    return jnp.dot(left, right, preferred_element_type=jnp.float32)


def pack_kernel(me_ref, query_hbm, key_hbm, value_hbm, out_hbm, grad_hbm, *refs):
    packed_refs = refs[:N_SEQ]
    query_ref, key_ref, value_ref, out_ref, grad_ref, delta_ref, sems = refs[N_SEQ:]
    pairs = (
        (grad_hbm, grad_ref),
        (out_hbm, out_ref),
        (query_hbm, query_ref),
        (key_hbm, key_ref),
        (value_hbm, value_ref),
    )
    copies = [
        pltpu.make_async_copy(source, target, sems.at[i])
        for i, (source, target) in enumerate(pairs)
    ]
    for copy in copies:
        copy.start()
    copies[0].wait()
    copies[1].wait()
    lane = iota((ROWS, LANES), 1)
    table = jnp.zeros((ROWS, LANES), jnp.float32)
    for head in range(2 * N_SEQ):
        cols = slice(head * HEAD_DIM, (head + 1) * HEAD_DIM)
        product = grad_ref[:, cols].astype(jnp.float32) * out_ref[:, cols].astype(jnp.float32)
        table = jnp.where(lane == head, jnp.sum(product, axis=1, keepdims=True), table)
    delta = table.T
    high = delta.astype(jnp.bfloat16).astype(jnp.float32)
    low = delta - high
    for group in range(N_SEQ):
        pair = slice(2 * group, 2 * group + 2)
        delta_ref[group] = jnp.concatenate(
            [high[pair], low[pair], jnp.zeros((4, LANES), jnp.float32)], axis=0
        )
    pad_cols = jnp.zeros((8, WIDTH - LANES), jnp.float32)
    for copy in copies[2:]:
        copy.wait()
    me = me_ref[0]
    for m in range(N_SEQ):
        group = jnp.bitwise_xor(me, m)
        two = pl.ds(pl.multiple_of(group * 256, 256), 256)
        one = pl.ds(pl.multiple_of(group * 128, 128), 128)
        rows = jnp.concatenate(
            [query_ref[:, two], key_ref[:, one], value_ref[:, one], grad_ref[:, two]], axis=1
        )
        extra = jnp.concatenate([delta_ref[group], pad_cols], axis=1)
        packed_refs[m][...] = jnp.concatenate([rows.astype(jnp.float32), extra], axis=0).astype(
            jnp.bfloat16
        )


def wide(rows):
    return jnp.concatenate([rows[s : s + 1] for s in range(N_SEQ)], axis=1)


def index_kernel(me_ref, segment_ref, *refs):
    lists, (rows_ref, cols_ref, request_ref, most_ref, list_ref) = refs[:N_SEQ], refs[N_SEQ:]
    for m in range(N_SEQ):
        list_ref[pl.ds(jnp.bitwise_xor(me_ref[0], m), 1), :] = lists[m][...]
    listed = list_ref[...]
    source = (listed // GROUP).astype(jnp.float32)
    local_row = (listed % ROWS).astype(jnp.float32)
    segment = segment_ref[...].astype(jnp.float32)
    blank = jnp.zeros((LANES - 8, LANES), jnp.float32)
    source_cols = jnp.concatenate([source, blank], axis=0).T
    before = iota((ROWS, ROWS), 0) < iota((ROWS, ROWS), 1)
    slots = []
    for s in range(N_SEQ):
        mine = source[s : s + 1]
        hits = ((source_cols[:, s : s + 1] == mine) & before).astype(jnp.float32)
        for earlier in range(s):
            hits = hits + (source_cols[:, earlier : earlier + 1] == mine).astype(jnp.float32)
        slots.append(jnp.sum(hits, axis=0, keepdims=True))
    slot = jnp.concatenate(slots, axis=0)
    blank = jnp.zeros((LANES - 24, LANES), jnp.float32)
    turned = jnp.concatenate([source, slot, segment, blank], axis=0).T
    lane = iota((ROWS, LANES), 1)
    picks = []
    for s in range(N_SEQ):
        columns = jnp.where(lane == 0, turned[:, s : s + 1], 0.0)
        columns = jnp.where(lane == 1, turned[:, 8 + s : 9 + s], columns)
        columns = jnp.where(lane == 2, turned[:, 16 + s : 17 + s], columns)
        cols_ref[s * ROWS : (s + 1) * ROWS, :] = columns
        picks.append((lane.astype(jnp.float32) == turned[:, 8 + s : 9 + s] + 1.0).astype(jnp.float32))
    rows_ref[0:8, :] = source
    rows_ref[8:16, :] = slot
    rows_ref[16:24, :] = segment
    pick = jnp.concatenate(picks, axis=0).astype(jnp.bfloat16)
    from_source = iota((N_DP, GROUP), 0).astype(jnp.float32) == wide(source)
    column = (iota((1, GROUP), 1) // ROWS).astype(jnp.float32)
    low = jnp.where(from_source, wide(local_row) + 1.0, 0.0).astype(jnp.bfloat16)
    high = jnp.where(from_source, column, 0.0).astype(jnp.bfloat16)
    table = nn_dot(low, pick) + float(ROWS) * nn_dot(high, pick)
    request_ref[...] = table.astype(jnp.int32)
    most_ref[0, 0] = (jnp.max(slot) + 1.0).astype(jnp.int32)


def turned_requests(request_ref):
    blank = jnp.zeros((LANES - N_DP, LANES), jnp.float32)
    return jnp.concatenate([request_ref[...].astype(jnp.float32), blank], axis=0).T - 1.0


def group_picks(turned, group, first, capacity):
    column = jnp.concatenate(
        [turned[first : first + capacity, d : d + 1] for d in range(8 * group, 8 * group + 8)], axis=0
    )
    row_id = iota((8 * capacity, GROUP), 1).astype(jnp.float32)
    return (column == row_id).astype(jnp.float32).astype(jnp.bfloat16)


def join_columns(me_ref, parts, ext_ref, delta_ref):
    for m in range(N_SEQ):
        column = jnp.bitwise_xor(me_ref[0], m)
        whole = parts[m][...]
        ext_ref[pl.ds(pl.multiple_of(column * ROWS, ROWS), ROWS), :] = whole[:ROWS]
        if delta_ref is not None:
            delta_ref[column] = whole[ROWS:, :LANES].astype(jnp.float32)


def send_extra_kernel(me_ref, request_ref, *refs):
    parts, (sent_ref, ext_ref) = refs[:N_SEQ], refs[N_SEQ:]
    group_rows = 8 * EXTRA
    turned = turned_requests(request_ref)
    join_columns(me_ref, parts, ext_ref, None)
    for group in range(N_DP // 8):
        pick = group_picks(turned, group, CAPACITY, EXTRA)
        rows = slice(group * group_rows, (group + 1) * group_rows)
        sent_ref[rows, :] = nn_dot(pick, ext_ref[...]).astype(jnp.bfloat16)


def send_kernel(me_ref, most_ref, request_ref, *refs):
    parts, (sent_ref, ext_ref, place_ref, delta_ref) = refs[:N_SEQ], refs[N_SEQ:]
    capacity = CAPACITY
    group_rows = 8 * capacity
    turned = turned_requests(request_ref)
    join_columns(me_ref, parts, ext_ref, delta_ref)
    delta = jnp.concatenate([delta_ref[s] for s in range(N_SEQ)], axis=1)

    def places(pick, group, first, count):
        index = iota((8, 8 * count), 1)
        owner = index // count
        value = jnp.where(
            iota((8, 8 * count), 0) == 0, owner + 8 * group, index - owner * count + first
        )
        return nn_dot(value.astype(jnp.float32).astype(jnp.bfloat16), pick)

    place = jnp.zeros((8, GROUP), jnp.float32)
    for group in range(N_DP // 8):
        pick = group_picks(turned, group, 0, capacity)
        place = place + places(pick, group, 0, capacity)
        rows = slice(group * group_rows, (group + 1) * group_rows)
        sent_ref[rows, :] = nn_dot(pick, ext_ref[...]).astype(jnp.bfloat16)
    place_ref[...] = place

    @pl.when(most_ref[0, 0] >= CAPACITY)
    def _():
        more = jnp.zeros((8, GROUP), jnp.float32)
        for group in range(N_DP // 8):
            more = more + places(group_picks(turned, group, CAPACITY, EXTRA), group, CAPACITY, EXTRA)
        place_ref[...] += more

    place = place_ref[...]
    owner_of = place[0:1]
    slot_cols = []
    for s in range(N_SEQ):
        part = place[:, s * ROWS : (s + 1) * ROWS]
        blank = jnp.zeros((LANES - 8, LANES), jnp.float32)
        slot_cols.append(jnp.concatenate([part, blank], axis=0).T[:, 1:2])
    slot_col = jnp.concatenate(slot_cols, axis=0)
    lane = iota((GROUP, LANES), 1).astype(jnp.float32)
    to_owner = iota((N_DP, GROUP), 0).astype(jnp.float32) == owner_of
    tail = jnp.zeros((2 * N_DP, LANES), jnp.float32)
    for head in range(2):
        spread = jnp.concatenate(
            [jnp.where(to_owner, delta[c : c + 1], 0.0) for c in (head, 2 + head)], axis=0
        )
        slot_pick = (slot_col + (64.0 * head - 1.0) == lane).astype(jnp.float32)
        tail = tail + nn_dot(spread.astype(jnp.bfloat16), slot_pick.astype(jnp.bfloat16))
    tail = jnp.concatenate([tail[:N_DP], tail[N_DP:]], axis=1)
    row = iota((16, 2 * LANES), 0)
    for owner in range(N_DP):
        inside = owner * capacity % 16
        rows = slice(owner * capacity - inside, owner * capacity - inside + 16)
        kept = sent_ref[rows, : 2 * LANES].astype(jnp.float32)
        mine = jnp.broadcast_to(tail[owner : owner + 1], (16, 2 * LANES))
        sent_ref[rows, : 2 * LANES] = jnp.where(row == inside, mine, kept).astype(jnp.bfloat16)


def attend_kernel(
    segment_ref, most_ref, arrived_ref, extra_ref, rows_ref, cols_ref, out_ref,
    x_ref, kt_ref, lanes_ref, weight_ref, squash_ref, total_ref, gqt_ref, gk_ref, gv_ref,
):
    slots = N_DP * CAPACITY
    blocks = GROUP // BLOCK
    slot_id = iota((BLOCK, slots), 1).astype(jnp.float32)
    for block in range(blocks):
        rows = slice(block * BLOCK, (block + 1) * BLOCK)
        slot = cols_ref[rows, 1:2] + 1.0
        place = jnp.where(slot < CAPACITY, cols_ref[rows, 0:1] * float(CAPACITY) + slot, -1.0)
        pick = (place == slot_id).astype(jnp.float32).astype(jnp.bfloat16)
        x_ref[rows, :] = nn_dot(pick, arrived_ref[...]).astype(jnp.bfloat16)

    @pl.when(most_ref[0, 0] >= CAPACITY)
    def _():
        extra_id = iota((BLOCK, N_DP * EXTRA), 1).astype(jnp.float32)
        for block in range(blocks):
            rows = slice(block * BLOCK, (block + 1) * BLOCK)
            slot = cols_ref[rows, 1:2] - float(CAPACITY - 1)
            place = jnp.where(slot >= 0.0, cols_ref[rows, 0:1] * float(EXTRA) + slot, -1.0)
            pick = (place == extra_id).astype(jnp.float32).astype(jnp.bfloat16)
            x_ref[rows, :] += nn_dot(pick, extra_ref[...]).astype(jnp.bfloat16)

    for block in range(blocks):
        rows = slice(block * BLOCK, (block + 1) * BLOCK)
        kt_ref[:, rows] = x_ref[rows, 256:384].astype(jnp.float32).T.astype(jnp.bfloat16)
    first = iota((LANES, slots), 0) * CAPACITY == iota((LANES, slots), 1)
    first = first.astype(jnp.float32).astype(jnp.bfloat16)
    parts = nn_dot(first, arrived_ref[:, : 2 * LANES])
    source = wide(rows_ref[0:8, :])
    slot = wide(rows_ref[8:16, :])
    segment = wide(rows_ref[16:24, :])
    from_source = iota((LANES, GROUP), 0).astype(jnp.float32) == source
    from_source = from_source.astype(jnp.float32).astype(jnp.bfloat16)
    high = parts[:, :LANES].T.astype(jnp.bfloat16)
    low = parts[:, LANES:].T.astype(jnp.bfloat16)
    both = nn_dot(high, from_source) + nn_dot(low, from_source)
    place = iota((LANES, GROUP), 0).astype(jnp.float32)
    for head in range(2):
        lanes_ref[head : head + 1, :] = jnp.sum(
            jnp.where(place == slot + 64.0 * head, both, 0.0), axis=0, keepdims=True
        )
    gk_ref[...] = jnp.zeros_like(gk_ref)
    gv_ref[...] = jnp.zeros_like(gv_ref)

    for block in range(blocks):
        rows = slice(block * BLOCK, (block + 1) * BLOCK)
        near = slice(max(block - 1, 0) * BLOCK, (block + 1) * BLOCK)
        near_count = near.stop - near.start
        queries = jnp.concatenate([x_ref[rows, 0:128], x_ref[rows, 128:256]], axis=0)
        grads = jnp.concatenate([x_ref[rows, 512:640], x_ref[rows, 640:768]], axis=0)
        delta = jnp.concatenate([lanes_ref[0:1, rows], lanes_ref[1:2, rows]], axis=1)
        segment_q = jnp.concatenate([segment[:, rows]] * 2, axis=1)
        far = range(block - 1)

        def weigh(keys, causal):
            score = nt_dot(x_ref[keys, 256:384], queries)
            squashed = jnp.tanh(score * (scaling / softcap))
            allowed = cols_ref[keys, 2:3] == segment_q
            if causal is not None:
                allowed = allowed & causal
            return squashed, jnp.where(allowed, jnp.exp(softcap * squashed), 0.0)

        def back(keys, squashed, weights, inverse):
            probabilities = weights * inverse
            gv_ref[keys, :] += nn_dot(probabilities.astype(jnp.bfloat16), grads)
            prob_grad = nt_dot(x_ref[keys, 384:512], grads)
            score_grad = probabilities * (prob_grad - delta) * (1.0 - squashed * squashed)
            score_grad = score_grad.astype(jnp.bfloat16)
            gk_ref[keys, :] += nn_dot(score_grad, queries)
            return nn_dot(kt_ref[:, keys], score_grad)

        def reaches(key_block):
            return segment_ref[(key_block + 1) * BLOCK - 1] == segment_ref[block * BLOCK]

        if len(far) > 0:
            total_ref[...] = jnp.zeros_like(total_ref)
        for key_block in far:

            @pl.when(reaches(key_block))
            def _(keys=slice(key_block * BLOCK, (key_block + 1) * BLOCK)):
                squashed, weights = weigh(keys, None)
                weight_ref[keys, :] = weights
                squash_ref[keys, :] = squashed
                total_ref[0:1, :] += jnp.sum(weights, axis=0, keepdims=True)

        ahead = iota((near_count, BLOCK), 0) - iota((near_count, BLOCK), 1)
        causal = (ahead <= near_count - BLOCK).astype(jnp.float32)
        causal = jnp.concatenate([causal, causal], axis=1) > 0.0
        squashed, weights = weigh(near, causal)
        total = jnp.sum(weights, axis=0, keepdims=True)
        if len(far) > 0:
            total = total + total_ref[0:1, :]
        inverse = 1.0 / total
        gqt_ref[...] = back(near, squashed, weights, inverse)
        if len(far) > 0:
            total_ref[0:1, :] = inverse
        for key_block in far:

            @pl.when(reaches(key_block))
            def _(keys=slice(key_block * BLOCK, (key_block + 1) * BLOCK)):
                gqt_ref[...] += back(
                    keys, squash_ref[keys, :], weight_ref[keys, :], total_ref[0:1, :]
                )

        turned = (gqt_ref[...].T * scaling).astype(jnp.bfloat16)
        out_ref[rows, 0:128] = turned[:BLOCK]
        out_ref[rows, 128:256] = turned[BLOCK:]
    out_ref[:, 256:384] = (gk_ref[...] * scaling).astype(jnp.bfloat16)
    out_ref[:, 384:512] = gv_ref[...].astype(jnp.bfloat16)


def unpack_kernel(returned_ref, query_ref, key_ref, value_ref):
    for group in range(N_SEQ):
        two = slice(2 * group * HEAD_DIM, 2 * (group + 1) * HEAD_DIM)
        one = slice(group * HEAD_DIM, (group + 1) * HEAD_DIM)
        query_ref[:, two] = returned_ref[group, :, 0:256]
        key_ref[:, one] = returned_ref[group, :, 256:384]
        value_ref[:, one] = returned_ref[group, :, 384:512]


def shape(dims, dtype=jnp.bfloat16):
    return jax.ShapeDtypeStruct(dims, dtype)


VMEM = pl.BlockSpec(memory_space=pltpu.VMEM)
SMEM = pl.BlockSpec(memory_space=pltpu.SMEM)


def cost(flops, moved, transcendentals=0):
    return pl.CostEstimate(flops=flops, bytes_accessed=moved, transcendentals=transcendentals)


def pack(me, query, key_rows, value_rows, attn_out, out_grad):
    return pl.pallas_call(
        pack_kernel,
        out_shape=[shape((ROWS + 8, WIDTH))] * N_SEQ,
        in_specs=[SMEM] + [pl.BlockSpec(memory_space=pltpu.HBM)] * 5,
        out_specs=[VMEM] * N_SEQ,
        scratch_shapes=[
            pltpu.VMEM((ROWS, 2048), jnp.bfloat16),
            pltpu.VMEM((ROWS, 1024), jnp.bfloat16),
            pltpu.VMEM((ROWS, 1024), jnp.bfloat16),
            pltpu.VMEM((ROWS, 2048), jnp.bfloat16),
            pltpu.VMEM((ROWS, 2048), jnp.bfloat16),
            pltpu.VMEM((N_SEQ, 8, LANES), jnp.float32),
            pltpu.SemaphoreType.DMA((5,)),
        ],
        compiler_params=FULL,
        name="pack",
    )(me, query, key_rows, value_rows, attn_out, out_grad)


def index(me, segments, lists):
    return pl.pallas_call(
        index_kernel,
        out_shape=(
            shape((24, LANES), jnp.float32),
            shape((GROUP, LANES), jnp.float32),
            shape((N_DP, LANES), jnp.int32),
            shape((1, 1), jnp.int32),
        ),
        in_specs=[SMEM] + [VMEM] * 9,
        out_specs=(VMEM, VMEM, VMEM, SMEM),
        scratch_shapes=[pltpu.VMEM((N_SEQ, LANES), jnp.int32)],
        compiler_params=PARAMS,
        name="index",
    )(me, segments.reshape(N_SEQ, ROWS), *lists)


def send(me, most, request, parts):
    return pl.pallas_call(
        send_kernel,
        out_shape=shape((N_DP * CAPACITY, WIDTH)),
        in_specs=[SMEM, SMEM] + [VMEM] * 9,
        scratch_shapes=[
            pltpu.VMEM((GROUP, WIDTH), jnp.bfloat16),
            pltpu.VMEM((8, GROUP), jnp.float32),
            pltpu.VMEM((N_SEQ, 8, LANES), jnp.float32),
        ],
        compiler_params=PARAMS,
        cost_estimate=cost(2 * N_DP * CAPACITY * GROUP * WIDTH, 4_000_000),
        name="send",
    )(me, most, request, *parts)


def send_extra(me, request, parts):
    return pl.pallas_call(
        send_extra_kernel,
        out_shape=shape((N_DP * EXTRA, WIDTH)),
        in_specs=[SMEM] + [VMEM] * 9,
        scratch_shapes=[pltpu.VMEM((GROUP, WIDTH), jnp.bfloat16)],
        compiler_params=PARAMS,
        name="send_extra",
    )(me, request, *parts)


def attend(segments, most, arrived, extra, rows, cols):
    return pl.pallas_call(
        attend_kernel,
        out_shape=shape((GROUP, 4 * HEAD_DIM)),
        in_specs=[SMEM, SMEM, VMEM, VMEM, VMEM, VMEM],
        scratch_shapes=[
            pltpu.VMEM((GROUP, WIDTH), jnp.bfloat16),
            pltpu.VMEM((HEAD_DIM, GROUP), jnp.bfloat16),
            pltpu.VMEM((8, GROUP), jnp.float32),
            pltpu.VMEM((GROUP - 2 * BLOCK, 2 * BLOCK), jnp.float32),
            pltpu.VMEM((GROUP - 2 * BLOCK, 2 * BLOCK), jnp.float32),
            pltpu.VMEM((8, 2 * BLOCK), jnp.float32),
            pltpu.VMEM((HEAD_DIM, 2 * BLOCK), jnp.float32),
            pltpu.VMEM((GROUP, HEAD_DIM), jnp.float32),
            pltpu.VMEM((GROUP, HEAD_DIM), jnp.float32),
        ],
        compiler_params=PARAMS,
        name="attend",
    )(segments, most, arrived, extra, rows, cols)


def unpack(returned):
    return pl.pallas_call(
        unpack_kernel,
        out_shape=(shape((ROWS, 2048)), shape((ROWS, 1024)), shape((ROWS, 1024))),
        compiler_params=PARAMS,
        name="unpack",
    )(returned)


def relay(array):
    return lax.all_to_all(array, "dp", split_axis=0, concat_axis=0, tiled=True)


def relay_requests(request):
    along_x = [[z * N_X + x for x in range(N_X)] for z in range(N_Z)]
    along_z = [[z * N_X + x for z in range(N_Z)] for x in range(N_X)]
    request = request.reshape(N_Z, N_X, LANES).transpose(1, 0, 2)
    request = lax.all_to_all(request, "dp", 0, 0, axis_index_groups=along_x, tiled=True)
    request = request.transpose(1, 0, 2)
    request = lax.all_to_all(request, "dp", 0, 0, axis_index_groups=along_z, tiled=True)
    return request.reshape(N_DP, LANES)


def local(query, key_rows, value_rows, attn_out, out_grad, source_row, segment_ids):
    me = lax.axis_index("seq").reshape(1)

    def swap(array, m):
        return lax.ppermute(array, "seq", [(s, s ^ m) for s in range(N_SEQ)]) if m else array

    lists = [swap(source_row.reshape(1, ROWS), m) for m in range(N_SEQ)]
    packed = pack(me, query, key_rows, value_rows, attn_out, out_grad)
    packed, lists = lax.optimization_barrier((packed, lists))
    parts = [swap(packed[m], m) for m in range(N_SEQ)]
    rows, cols, request, most = index(me, segment_ids, lists)
    request = relay_requests(request)
    arrived = relay(send(me, most, request, parts))
    extra = lax.cond(
        most[0, 0] >= CAPACITY,
        lambda request, *parts: relay(send_extra(me, request, parts)),
        lambda request, *parts: jnp.zeros((N_DP * EXTRA, WIDTH), jnp.bfloat16),
        request,
        *parts,
    )
    grads = attend(segment_ids, most, arrived, extra, rows, cols)
    returned = lax.all_to_all(
        grads.reshape(N_SEQ, ROWS, 4 * HEAD_DIM), "seq", split_axis=0, concat_axis=0, tiled=True
    )
    return unpack(returned)


def solution(mesh):
    in_specs = (
        P(("dp", "seq"), None),
        P(("dp", "seq"), None),
        P(("dp", "seq"), None),
        P(("dp", "seq"), None),
        P(("dp", "seq"), None),
        P(("dp", "seq")),
        P("dp"),
    )
    out_specs = (P(("dp", "seq"), None), P(("dp", "seq"), None), P(("dp", "seq"), None))
    return jax.shard_map(local, mesh=mesh, in_specs=in_specs, out_specs=out_specs, check_vma=False)
```

```python
import functools

import jax
import jax.numpy as jnp
from jax import lax
from jax.experimental import pallas as pl
from jax.experimental.pallas import tpu as pltpu
from jax.sharding import PartitionSpec as P

HEAD_DIM = 128
N_DP = 32
N_Z = 8
N_X = 4
N_SEQ = 8
ROWS = 128
GROUP = N_SEQ * ROWS
WIDTH = 6 * HEAD_DIM
LANES = 128
BLOCK = 256
GATHER = 512
SEND = 16
CAPACITY = 56
EXTRA = 16

scaling = 1.0 / 12.0
softcap = 50.0

PARAMS = pltpu.CompilerParams(vmem_limit_bytes=28 * 1024 * 1024)
FULL = pltpu.CompilerParams(vmem_limit_bytes=60 * 1024 * 1024)


def iota(shape, dim):
    return lax.broadcasted_iota(jnp.int32, shape, dim)


def nt_dot(left, right):
    return lax.dot_general(left, right, (((1,), (1,)), ((), ())), preferred_element_type=jnp.float32)


def nn_dot(left, right):
    return jnp.dot(left, right, preferred_element_type=jnp.float32)


def pack_kernel(
    query_hbm, key_hbm, value_hbm, out_hbm, grad_hbm, packed_ref,
    query_ref, key_ref, value_ref, out_ref, grad_ref, sems,
):
    pairs = (
        (grad_hbm, grad_ref),
        (out_hbm, out_ref),
        (query_hbm, query_ref),
        (key_hbm, key_ref),
        (value_hbm, value_ref),
    )
    copies = [
        pltpu.make_async_copy(source, target, sems.at[i])
        for i, (source, target) in enumerate(pairs)
    ]
    for copy in copies:
        copy.start()
    copies[0].wait()
    copies[1].wait()
    columns = []
    for head in range(2 * N_SEQ):
        cols = slice(head * HEAD_DIM, (head + 1) * HEAD_DIM)
        product = grad_ref[:, cols].astype(jnp.float32) * out_ref[:, cols].astype(jnp.float32)
        columns.append(jnp.sum(product, axis=1, keepdims=True))
    lane = iota((ROWS, LANES), 1)
    table = jnp.zeros((ROWS, LANES), jnp.float32)
    for head in range(2 * N_SEQ):
        table = jnp.where(lane == head, columns[head], table)
    delta = table.T
    high = delta.astype(jnp.bfloat16).astype(jnp.float32)
    low = delta - high
    pad_rows = jnp.zeros((4, LANES), jnp.float32)
    pad_cols = jnp.zeros((8, WIDTH - LANES), jnp.float32)
    for copy in copies[2:]:
        copy.wait()
    for group in range(N_SEQ):
        two = slice(2 * group * HEAD_DIM, 2 * (group + 1) * HEAD_DIM)
        one = slice(group * HEAD_DIM, (group + 1) * HEAD_DIM)
        pair = slice(2 * group, 2 * group + 2)
        rows = jnp.concatenate(
            [query_ref[:, two], key_ref[:, one], value_ref[:, one], grad_ref[:, two]], axis=1
        )
        extra = jnp.concatenate([high[pair], low[pair], pad_rows], axis=0)
        extra = jnp.concatenate([extra, pad_cols], axis=1)
        packed_ref[group] = jnp.concatenate([rows.astype(jnp.float32), extra], axis=0).astype(
            jnp.bfloat16
        )


def wide(rows):
    return jnp.concatenate([rows[s : s + 1] for s in range(N_SEQ)], axis=1)


def index_kernel(ids_ref, segment_ref, *refs):
    lists, (rows_ref, cols_ref), refs = refs[:N_SEQ], refs[N_SEQ : N_SEQ + 2], refs[N_SEQ + 2 :]
    tables, (most_ref, list_ref, table_ref) = refs[:N_X], refs[N_X:]
    for m in range(N_SEQ):
        list_ref[pl.ds(jnp.bitwise_xor(ids_ref[0], m), 1), :] = lists[m][...]
    listed = list_ref[...]
    source = (listed // GROUP).astype(jnp.float32)
    local_row = (listed % ROWS).astype(jnp.float32)
    segment = segment_ref[...].astype(jnp.float32)
    blank = jnp.zeros((LANES - 8, LANES), jnp.float32)
    source_cols = jnp.concatenate([source, blank], axis=0).T
    before = iota((ROWS, ROWS), 0) < iota((ROWS, ROWS), 1)
    slots = []
    for s in range(N_SEQ):
        mine = source[s : s + 1]
        hits = ((source_cols[:, s : s + 1] == mine) & before).astype(jnp.float32)
        for earlier in range(s):
            hits = hits + (source_cols[:, earlier : earlier + 1] == mine).astype(jnp.float32)
        slots.append(jnp.sum(hits, axis=0, keepdims=True))
    slot = jnp.concatenate(slots, axis=0)
    blank = jnp.zeros((LANES - 24, LANES), jnp.float32)
    turned = jnp.concatenate([source, slot, segment, blank], axis=0).T
    lane = iota((ROWS, LANES), 1)
    picks = []
    for s in range(N_SEQ):
        columns = jnp.where(lane == 0, turned[:, s : s + 1], 0.0)
        columns = jnp.where(lane == 1, turned[:, 8 + s : 9 + s], columns)
        columns = jnp.where(lane == 2, turned[:, 16 + s : 17 + s], columns)
        cols_ref[s * ROWS : (s + 1) * ROWS, :] = columns
        picks.append((lane.astype(jnp.float32) == turned[:, 8 + s : 9 + s] + 1.0).astype(jnp.float32))
    rows_ref[0:8, :] = source
    rows_ref[8:16, :] = slot
    rows_ref[16:24, :] = segment
    pick = jnp.concatenate(picks, axis=0).astype(jnp.bfloat16)
    place = iota((N_DP, GROUP), 0)
    place = (place % N_Z) * N_X + place // N_Z
    from_source = place.astype(jnp.float32) == wide(source)
    column = (iota((1, GROUP), 1) // ROWS).astype(jnp.float32)
    low = jnp.where(from_source, wide(local_row) + 1.0, 0.0).astype(jnp.bfloat16)
    high = jnp.where(from_source, column, 0.0).astype(jnp.bfloat16)
    table = nn_dot(low, pick) + float(ROWS) * nn_dot(high, pick)
    for x in range(N_X):
        table_ref[x] = table[x * N_Z : (x + 1) * N_Z].astype(jnp.int32)
    for m in range(N_X):
        tables[m][...] = table_ref[jnp.bitwise_xor(ids_ref[1], m)]
    most_ref[0, 0] = (jnp.max(slot) + 1.0).astype(jnp.int32)


def turn_kernel(ids_ref, *refs):
    tables, turned = refs[:N_X], refs[N_X:]
    for m in range(N_X):
        x = jnp.bitwise_xor(ids_ref[1], m)
        for n in range(N_Z):
            z = jnp.bitwise_xor(ids_ref[2], n)
            turned[n][pl.ds(x, 1), :] = tables[m][pl.ds(z, 1), :]


def turned_requests(ids_ref, tables, request_ref):
    for n in range(N_Z):
        request_ref[jnp.bitwise_xor(ids_ref[2], n)] = tables[n][...].astype(jnp.float32)
    blank = jnp.zeros((LANES - N_DP, LANES), jnp.float32)
    return jnp.concatenate([request_ref[z] for z in range(N_Z)] + [blank], axis=0).T - 1.0


def group_picks(turned, group, first, capacity):
    owners = range(SEND * group, SEND * (group + 1))
    column = jnp.concatenate([turned[first : first + capacity, d : d + 1] for d in owners], axis=0)
    row_id = iota((SEND * capacity, GROUP), 1).astype(jnp.float32)
    return (column == row_id).astype(jnp.float32).astype(jnp.bfloat16)


def send_extra_kernel(ids_ref, *refs):
    tables, (rows_ref, sent_ref, ext_ref, request_ref) = refs[:N_Z], refs[N_Z:]
    group_rows = SEND * EXTRA
    turned = turned_requests(ids_ref, tables, request_ref)
    for s in range(N_SEQ):
        whole = rows_ref[s]
        ext_ref[s * ROWS : (s + 1) * ROWS, :] = whole[:ROWS]
    for group in range(N_DP // SEND):
        pick = group_picks(turned, group, CAPACITY, EXTRA)
        rows = slice(group * group_rows, (group + 1) * group_rows)
        sent_ref[rows, :] = nn_dot(pick, ext_ref[...]).astype(jnp.bfloat16)


def send_kernel(ids_ref, most_ref, *refs):
    tables, (rows_ref, sent_ref, ext_ref, place_ref, request_ref) = refs[:N_Z], refs[N_Z:]
    capacity = CAPACITY
    group_rows = SEND * capacity
    turned = turned_requests(ids_ref, tables, request_ref)
    deltas = []
    for s in range(N_SEQ):
        whole = rows_ref[s]
        ext_ref[s * ROWS : (s + 1) * ROWS, :] = whole[:ROWS]
        deltas.append(whole[ROWS:, :LANES].astype(jnp.float32))
    delta = jnp.concatenate(deltas, axis=1)

    def places(pick, group, first, count):
        index = iota((8, SEND * count), 1)
        owner = index // count
        value = jnp.where(
            iota((8, SEND * count), 0) == 0, owner + SEND * group, index - owner * count + first
        )
        return nn_dot(value.astype(jnp.float32).astype(jnp.bfloat16), pick)

    place = jnp.zeros((8, GROUP), jnp.float32)
    for group in range(N_DP // SEND):
        pick = group_picks(turned, group, 0, capacity)
        place = place + places(pick, group, 0, capacity)
        rows = slice(group * group_rows, (group + 1) * group_rows)
        sent_ref[rows, :] = nn_dot(pick, ext_ref[...]).astype(jnp.bfloat16)
    place_ref[...] = place

    @pl.when(most_ref[0, 0] >= CAPACITY)
    def _():
        more = jnp.zeros((8, GROUP), jnp.float32)
        for group in range(N_DP // SEND):
            more = more + places(group_picks(turned, group, CAPACITY, EXTRA), group, CAPACITY, EXTRA)
        place_ref[...] += more

    place = place_ref[...]
    owner_of = place[0:1]
    slot_cols = []
    for s in range(N_SEQ):
        part = place[:, s * ROWS : (s + 1) * ROWS]
        blank = jnp.zeros((LANES - 8, LANES), jnp.float32)
        slot_cols.append(jnp.concatenate([part, blank], axis=0).T[:, 1:2])
    slot_col = jnp.concatenate(slot_cols, axis=0)
    lane = iota((GROUP, LANES), 1).astype(jnp.float32)
    to_owner = iota((N_DP, GROUP), 0).astype(jnp.float32) == owner_of
    tail = jnp.zeros((2 * N_DP, LANES), jnp.float32)
    for head in range(2):
        spread = jnp.concatenate(
            [jnp.where(to_owner, delta[c : c + 1], 0.0) for c in (head, 2 + head)], axis=0
        )
        slot_pick = (slot_col + (64.0 * head - 1.0) == lane).astype(jnp.float32)
        tail = tail + nn_dot(spread.astype(jnp.bfloat16), slot_pick.astype(jnp.bfloat16))
    tail = jnp.concatenate([tail[:N_DP], tail[N_DP:]], axis=1)
    row = iota((16, 2 * LANES), 0)
    for owner in range(N_DP):
        inside = owner * capacity % 16
        rows = slice(owner * capacity - inside, owner * capacity - inside + 16)
        kept = sent_ref[rows, : 2 * LANES].astype(jnp.float32)
        mine = jnp.broadcast_to(tail[owner : owner + 1], (16, 2 * LANES))
        sent_ref[rows, : 2 * LANES] = jnp.where(row == inside, mine, kept).astype(jnp.bfloat16)


def attend_kernel(
    segment_ref, most_ref, arrived_ref, extra_ref, rows_ref, cols_ref, out_ref,
    x_ref, kt_ref, lanes_ref, weight_ref, squash_ref, total_ref, gqt_ref, gk_ref, gv_ref,
):
    slots = N_DP * CAPACITY
    blocks = GROUP // BLOCK
    slot_id = iota((GATHER, slots), 1).astype(jnp.float32)
    for block in range(GROUP // GATHER):
        rows = slice(block * GATHER, (block + 1) * GATHER)
        slot = cols_ref[rows, 1:2] + 1.0
        place = jnp.where(slot < CAPACITY, cols_ref[rows, 0:1] * float(CAPACITY) + slot, -1.0)
        pick = (place == slot_id).astype(jnp.float32).astype(jnp.bfloat16)
        x_ref[rows, :] = nn_dot(pick, arrived_ref[...]).astype(jnp.bfloat16)

    @pl.when(most_ref[0, 0] >= CAPACITY)
    def _():
        extra_id = iota((BLOCK, N_DP * EXTRA), 1).astype(jnp.float32)
        for block in range(blocks):
            rows = slice(block * BLOCK, (block + 1) * BLOCK)
            slot = cols_ref[rows, 1:2] - float(CAPACITY - 1)
            place = jnp.where(slot >= 0.0, cols_ref[rows, 0:1] * float(EXTRA) + slot, -1.0)
            pick = (place == extra_id).astype(jnp.float32).astype(jnp.bfloat16)
            x_ref[rows, :] += nn_dot(pick, extra_ref[...]).astype(jnp.bfloat16)

    for block in range(blocks):
        rows = slice(block * BLOCK, (block + 1) * BLOCK)
        kt_ref[:, rows] = x_ref[rows, 256:384].astype(jnp.float32).T.astype(jnp.bfloat16)
    first = iota((LANES, slots), 0) * CAPACITY == iota((LANES, slots), 1)
    first = first.astype(jnp.float32).astype(jnp.bfloat16)
    parts = nn_dot(first, arrived_ref[:, : 2 * LANES])
    source = wide(rows_ref[0:8, :])
    slot = wide(rows_ref[8:16, :])
    segment = wide(rows_ref[16:24, :])
    from_source = iota((LANES, GROUP), 0).astype(jnp.float32) == source
    from_source = from_source.astype(jnp.float32).astype(jnp.bfloat16)
    high = parts[:, :LANES].T.astype(jnp.bfloat16)
    low = parts[:, LANES:].T.astype(jnp.bfloat16)
    both = nn_dot(high, from_source) + nn_dot(low, from_source)
    place = iota((LANES, GROUP), 0).astype(jnp.float32)
    for head in range(2):
        lanes_ref[head : head + 1, :] = jnp.sum(
            jnp.where(place == slot + 64.0 * head, both, 0.0), axis=0, keepdims=True
        )
    gk_ref[...] = jnp.zeros_like(gk_ref)
    gv_ref[...] = jnp.zeros_like(gv_ref)

    for block in range(blocks):
        rows = slice(block * BLOCK, (block + 1) * BLOCK)
        near = slice(max(block - 1, 0) * BLOCK, (block + 1) * BLOCK)
        near_count = near.stop - near.start
        queries = jnp.concatenate([x_ref[rows, 0:128], x_ref[rows, 128:256]], axis=0)
        grads = jnp.concatenate([x_ref[rows, 512:640], x_ref[rows, 640:768]], axis=0)
        delta = jnp.concatenate([lanes_ref[0:1, rows], lanes_ref[1:2, rows]], axis=1)
        segment_q = jnp.concatenate([segment[:, rows]] * 2, axis=1)
        far = range(block - 1)

        def weigh(keys, causal):
            score = nt_dot(x_ref[keys, 256:384], queries)
            squashed = jnp.tanh(score * (scaling / softcap))
            allowed = cols_ref[keys, 2:3] == segment_q
            if causal is not None:
                allowed = allowed & causal
            return squashed, jnp.where(allowed, jnp.exp(softcap * squashed), 0.0)

        def back(keys, squashed, weights, inverse):
            probabilities = weights * inverse
            gv_ref[keys, :] += nn_dot(probabilities.astype(jnp.bfloat16), grads)
            prob_grad = nt_dot(x_ref[keys, 384:512], grads)
            score_grad = probabilities * (prob_grad - delta) * (1.0 - squashed * squashed)
            score_grad = score_grad.astype(jnp.bfloat16)
            gk_ref[keys, :] += nn_dot(score_grad, queries)
            return nn_dot(kt_ref[:, keys], score_grad)

        def reaches(key_block):
            return segment_ref[(key_block + 1) * BLOCK - 1] == segment_ref[block * BLOCK]

        if len(far) > 0:
            total_ref[...] = jnp.zeros_like(total_ref)
        for key_block in far:

            @pl.when(reaches(key_block))
            def _(keys=slice(key_block * BLOCK, (key_block + 1) * BLOCK)):
                squashed, weights = weigh(keys, None)
                weight_ref[keys, :] = weights
                squash_ref[keys, :] = squashed
                total_ref[0:1, :] += jnp.sum(weights, axis=0, keepdims=True)

        ahead = iota((near_count, BLOCK), 0) - iota((near_count, BLOCK), 1)
        causal = (ahead <= near_count - BLOCK).astype(jnp.float32)
        causal = jnp.concatenate([causal, causal], axis=1) > 0.0
        squashed, weights = weigh(near, causal)
        total = jnp.sum(weights, axis=0, keepdims=True)
        if len(far) > 0:
            total = total + total_ref[0:1, :]
        inverse = 1.0 / total
        gqt_ref[...] = back(near, squashed, weights, inverse)
        if len(far) > 0:
            total_ref[0:1, :] = inverse
        for key_block in far:

            @pl.when(reaches(key_block))
            def _(keys=slice(key_block * BLOCK, (key_block + 1) * BLOCK)):
                gqt_ref[...] += back(
                    keys, squash_ref[keys, :], weight_ref[keys, :], total_ref[0:1, :]
                )

        turned = (gqt_ref[...].T * scaling).astype(jnp.bfloat16)
        out_ref[rows, 0:128] = turned[:BLOCK]
        out_ref[rows, 128:256] = turned[BLOCK:]
    out_ref[:, 256:384] = (gk_ref[...] * scaling).astype(jnp.bfloat16)
    out_ref[:, 384:512] = gv_ref[...].astype(jnp.bfloat16)


def unpack_kernel(returned_ref, query_ref, key_ref, value_ref):
    for group in range(N_SEQ):
        two = slice(2 * group * HEAD_DIM, 2 * (group + 1) * HEAD_DIM)
        one = slice(group * HEAD_DIM, (group + 1) * HEAD_DIM)
        query_ref[:, two] = returned_ref[group, :, 0:256]
        key_ref[:, one] = returned_ref[group, :, 256:384]
        value_ref[:, one] = returned_ref[group, :, 384:512]


def shape(dims, dtype=jnp.bfloat16):
    return jax.ShapeDtypeStruct(dims, dtype)


VMEM = pl.BlockSpec(memory_space=pltpu.VMEM)
SMEM = pl.BlockSpec(memory_space=pltpu.SMEM)


def cost(flops, moved, transcendentals=0):
    return pl.CostEstimate(flops=flops, bytes_accessed=moved, transcendentals=transcendentals)


def pack(query, key_rows, value_rows, attn_out, out_grad):
    return pl.pallas_call(
        pack_kernel,
        out_shape=shape((N_SEQ, ROWS + 8, WIDTH)),
        in_specs=[pl.BlockSpec(memory_space=pltpu.HBM)] * 5,
        out_specs=VMEM,
        scratch_shapes=[
            pltpu.VMEM((ROWS, 2048), jnp.bfloat16),
            pltpu.VMEM((ROWS, 1024), jnp.bfloat16),
            pltpu.VMEM((ROWS, 1024), jnp.bfloat16),
            pltpu.VMEM((ROWS, 2048), jnp.bfloat16),
            pltpu.VMEM((ROWS, 2048), jnp.bfloat16),
            pltpu.SemaphoreType.DMA((5,)),
        ],
        compiler_params=FULL,
        name="pack",
    )(query, key_rows, value_rows, attn_out, out_grad)


def index(ids, segments, lists):
    return pl.pallas_call(
        index_kernel,
        out_shape=[shape((24, LANES), jnp.float32), shape((GROUP, LANES), jnp.float32)]
        + [shape((N_Z, LANES), jnp.int32)] * N_X
        + [shape((1, 1), jnp.int32)],
        in_specs=[SMEM] + [VMEM] * 9,
        out_specs=[VMEM] * (2 + N_X) + [SMEM],
        scratch_shapes=[
            pltpu.VMEM((N_SEQ, LANES), jnp.int32),
            pltpu.VMEM((N_X, N_Z, LANES), jnp.int32),
        ],
        compiler_params=PARAMS,
        name="index",
    )(ids, segments.reshape(N_SEQ, ROWS), *lists)


def turn(ids, tables):
    return pl.pallas_call(
        turn_kernel,
        out_shape=[shape((N_X, LANES), jnp.int32)] * N_Z,
        in_specs=[SMEM] + [VMEM] * N_X,
        out_specs=[VMEM] * N_Z,
        compiler_params=PARAMS,
        name="turn",
    )(ids, *tables)


def send(ids, most, tables, head_rows):
    return pl.pallas_call(
        send_kernel,
        out_shape=shape((N_DP * CAPACITY, WIDTH)),
        in_specs=[SMEM, SMEM] + [VMEM] * 9,
        scratch_shapes=[
            pltpu.VMEM((GROUP, WIDTH), jnp.bfloat16),
            pltpu.VMEM((8, GROUP), jnp.float32),
            pltpu.VMEM((N_Z, N_X, LANES), jnp.float32),
        ],
        compiler_params=PARAMS,
        name="send",
    )(ids, most, *tables, head_rows)


def send_extra(ids, tables, head_rows):
    return pl.pallas_call(
        send_extra_kernel,
        out_shape=shape((N_DP * EXTRA, WIDTH)),
        in_specs=[SMEM] + [VMEM] * 9,
        scratch_shapes=[
            pltpu.VMEM((GROUP, WIDTH), jnp.bfloat16),
            pltpu.VMEM((N_Z, N_X, LANES), jnp.float32),
        ],
        compiler_params=PARAMS,
        name="send_extra",
    )(ids, *tables, head_rows)


def attend(segments, most, arrived, extra, rows, cols):
    return pl.pallas_call(
        attend_kernel,
        out_shape=shape((GROUP, 4 * HEAD_DIM)),
        in_specs=[SMEM, SMEM, VMEM, VMEM, VMEM, VMEM],
        scratch_shapes=[
            pltpu.VMEM((GROUP, WIDTH), jnp.bfloat16),
            pltpu.VMEM((HEAD_DIM, GROUP), jnp.bfloat16),
            pltpu.VMEM((8, GROUP), jnp.float32),
            pltpu.VMEM((GROUP - 2 * BLOCK, 2 * BLOCK), jnp.float32),
            pltpu.VMEM((GROUP - 2 * BLOCK, 2 * BLOCK), jnp.float32),
            pltpu.VMEM((8, 2 * BLOCK), jnp.float32),
            pltpu.VMEM((HEAD_DIM, 2 * BLOCK), jnp.float32),
            pltpu.VMEM((GROUP, HEAD_DIM), jnp.float32),
            pltpu.VMEM((GROUP, HEAD_DIM), jnp.float32),
        ],
        compiler_params=PARAMS,
        name="attend",
    )(segments, most, arrived, extra, rows, cols)


def unpack(returned):
    return pl.pallas_call(
        unpack_kernel,
        out_shape=(shape((ROWS, 2048)), shape((ROWS, 1024)), shape((ROWS, 1024))),
        compiler_params=PARAMS,
        name="unpack",
    )(returned)


def relay(array):
    return lax.all_to_all(array, "dp", split_axis=0, concat_axis=0, tiled=True)


def swap_seq(array, m):
    return lax.ppermute(array, "seq", [(s, s ^ m) for s in range(N_SEQ)]) if m else array


def swap_dp(array, m):
    return lax.ppermute(array, "dp", [(d, d ^ m) for d in range(N_DP)]) if m else array


def local(query, key_rows, value_rows, attn_out, out_grad, source_row, segment_ids):
    my_dp = lax.axis_index("dp")
    ids = jnp.stack([lax.axis_index("seq"), my_dp % N_X, my_dp // N_X])
    lists = [swap_seq(source_row.reshape(1, ROWS), m) for m in range(N_SEQ)]
    packed = pack(query, key_rows, value_rows, attn_out, out_grad)
    packed, lists = lax.optimization_barrier((packed, lists))
    head_rows = lax.all_to_all(packed, "seq", split_axis=0, concat_axis=0, tiled=True)
    rows, cols, *tables, most = index(ids, segment_ids, lists)
    tables = turn(ids, [swap_dp(tables[m], m) for m in range(N_X)])
    tables = [swap_dp(tables[n], n * N_X) for n in range(N_Z)]
    arrived = relay(send(ids, most, tables, head_rows))
    extra = lax.cond(
        most[0, 0] >= CAPACITY,
        lambda tables, head_rows: relay(send_extra(ids, tables, head_rows)),
        lambda tables, head_rows: jnp.zeros((N_DP * EXTRA, WIDTH), jnp.bfloat16),
        tables,
        head_rows,
    )
    grads = attend(segment_ids, most, arrived, extra, rows, cols)
    returned = lax.all_to_all(
        grads.reshape(N_SEQ, ROWS, 4 * HEAD_DIM), "seq", split_axis=0, concat_axis=0, tiled=True
    )
    return unpack(returned)


def solution(mesh):
    in_specs = (
        P(("dp", "seq"), None),
        P(("dp", "seq"), None),
        P(("dp", "seq"), None),
        P(("dp", "seq"), None),
        P(("dp", "seq"), None),
        P(("dp", "seq")),
        P("dp"),
    )
    out_specs = (P(("dp", "seq"), None), P(("dp", "seq"), None), P(("dp", "seq"), None))
    return jax.shard_map(local, mesh=mesh, in_specs=in_specs, out_specs=out_specs, check_vma=False)
```

```python
import functools

import jax
import jax.numpy as jnp
from jax import lax
from jax.experimental import pallas as pl
from jax.experimental.pallas import tpu as pltpu
from jax.sharding import PartitionSpec as P

HEAD_DIM = 128
N_DP = 32
N_SEQ = 8
N_Y = 4
ROWS = 128
GROUP = N_SEQ * ROWS
HALF = 3 * HEAD_DIM
LANES = 128
BLOCK = 256
CAPACITY = 56
EXTRA = 16
STEPS = 10
NEAR = 7

scaling = 1.0 / 12.0
softcap = 50.0

PARAMS = pltpu.CompilerParams(vmem_limit_bytes=28 * 1024 * 1024)
FULL = pltpu.CompilerParams(vmem_limit_bytes=60 * 1024 * 1024)
VMEM = pl.BlockSpec(memory_space=pltpu.VMEM)
SMEM = pl.BlockSpec(memory_space=pltpu.SMEM)
HBM = pl.BlockSpec(memory_space=pltpu.HBM)


def iota(shape, dim):
    return lax.broadcasted_iota(jnp.int32, shape, dim)


def float_iota(shape, dim):
    return iota(shape, dim).astype(jnp.float32)


def one_hot(hits):
    return hits.astype(jnp.float32).astype(jnp.bfloat16)


def nt_dot(left, right):
    return lax.dot_general(left, right, (((1,), (1,)), ((), ())), preferred_element_type=jnp.float32)


def nn_dot(left, right):
    return jnp.dot(left, right, preferred_element_type=jnp.float32)


def turned(rows):
    blank = jnp.zeros((LANES - rows.shape[0], LANES), jnp.float32)
    return jnp.concatenate([rows, blank], axis=0).T


def wide(rows):
    return jnp.concatenate([rows[s : s + 1] for s in range(N_SEQ)], axis=1)


def request_kernel(list_ref, request_ref):
    listed = list_ref[...]
    source = (listed // GROUP).astype(jnp.float32)
    local_row = (listed % ROWS).astype(jnp.float32)
    before = iota((ROWS, ROWS), 0) < iota((ROWS, ROWS), 1)
    hits = ((turned(source)[:, 0:1] == source) & before).astype(jnp.float32)
    rank = jnp.sum(hits, axis=0, keepdims=True)
    pick = one_hot(turned(rank)[:, 0:1] == float_iota((ROWS, LANES), 1))
    from_source = float_iota((N_DP, ROWS), 0) == source
    table = nn_dot(jnp.where(from_source, local_row + 1.0, 0.0).astype(jnp.bfloat16), pick)
    request_ref[...] = table.astype(jnp.int32)


def pack_near_kernel(list_ref, request_ref, query_hbm, key_hbm, packed_ref, query_ref, key_ref, sems):
    copies = [
        pltpu.make_async_copy(query_hbm, query_ref, sems.at[0]),
        pltpu.make_async_copy(key_hbm, key_ref, sems.at[1]),
    ]
    for copy in copies:
        copy.start()
    listed = list_ref[...]
    source = (listed // GROUP).astype(jnp.float32)
    local_row = (listed % ROWS).astype(jnp.float32)
    wanted = request_ref[...].astype(jnp.float32) - 1.0
    row_id = float_iota((N_DP, ROWS), 1)
    owner_id = float_iota((N_DP, ROWS), 0)
    owner = jnp.zeros((1, ROWS), jnp.float32)
    rank = jnp.zeros((1, ROWS), jnp.float32)
    for k in range(8):
        hits = (wanted[:, k : k + 1] == row_id).astype(jnp.float32)
        owner = owner + jnp.sum(hits * owner_id, axis=0, keepdims=True)
        rank = rank + float(k) * jnp.sum(hits, axis=0, keepdims=True)
    tail = jnp.concatenate([owner, rank, source, local_row, jnp.zeros((4, LANES), jnp.float32)], axis=0)
    tail = jnp.concatenate([tail, jnp.zeros((8, HALF - LANES), jnp.float32)], axis=1)
    for copy in copies:
        copy.wait()
    for group in range(N_SEQ):
        two = slice(2 * group * HEAD_DIM, 2 * (group + 1) * HEAD_DIM)
        one = slice(group * HEAD_DIM, (group + 1) * HEAD_DIM)
        rows = jnp.concatenate([query_ref[:, two], key_ref[:, one]], axis=1)
        packed_ref[group] = jnp.concatenate([rows.astype(jnp.float32), tail], axis=0).astype(
            jnp.bfloat16
        )


def pack_far_kernel(ids_ref, value_hbm, out_hbm, grad_hbm, *refs):
    packed_refs, (value_ref, out_ref, grad_ref, delta_ref, sems) = refs[:N_Y], refs[N_Y:]
    copies = [
        pltpu.make_async_copy(grad_hbm, grad_ref, sems.at[0]),
        pltpu.make_async_copy(out_hbm, out_ref, sems.at[1]),
        pltpu.make_async_copy(value_hbm, value_ref, sems.at[2]),
    ]
    for copy in copies:
        copy.start()
    copies[0].wait()
    copies[1].wait()
    lane = iota((ROWS, LANES), 1)
    table = jnp.zeros((ROWS, LANES), jnp.float32)
    for head in range(2 * N_SEQ):
        cols = slice(head * HEAD_DIM, (head + 1) * HEAD_DIM)
        product = grad_ref[:, cols].astype(jnp.float32) * out_ref[:, cols].astype(jnp.float32)
        table = jnp.where(lane == head, jnp.sum(product, axis=1, keepdims=True), table)
    delta = table.T
    high = delta.astype(jnp.bfloat16).astype(jnp.float32)
    low = delta - high
    for group in range(N_SEQ):
        pair = slice(2 * group, 2 * group + 2)
        delta_ref[group] = jnp.concatenate(
            [high[pair], low[pair], jnp.zeros((4, LANES), jnp.float32)], axis=0
        )
    copies[2].wait()
    for m in range(N_SEQ):
        group = jnp.bitwise_xor(ids_ref[0], m)
        two = pl.ds(pl.multiple_of(group * 256, 256), 256)
        one = pl.ds(pl.multiple_of(group * 128, 128), 128)
        rows = jnp.concatenate([value_ref[:, one], grad_ref[:, two]], axis=1)
        tail = jnp.concatenate(
            [delta_ref[group], jnp.zeros((8, HALF - LANES), jnp.float32)], axis=1
        )
        packed_refs[m // 2][m % 2] = jnp.concatenate(
            [rows.astype(jnp.float32), tail], axis=0
        ).astype(jnp.bfloat16)


def place_rows(tails, place_ref):
    counts = jnp.zeros((N_DP, 1), jnp.float32)
    for s in range(N_SEQ):
        owner = tails[s][0:1]
        to_owner = (float_iota((N_DP, ROWS), 0) == owner).astype(jnp.float32)
        base = jnp.sum(to_owner * counts, axis=0, keepdims=True)
        counts = counts + jnp.sum(to_owner, axis=1, keepdims=True)
        slot = tails[s][1:2] + base + 1.0
        place_ref[:, s * ROWS : (s + 1) * ROWS] = jnp.concatenate(
            [owner, slot, jnp.zeros((6, LANES), jnp.float32)], axis=0
        )
    return counts


def group_picks(place_ref, group, first, capacity):
    owner = place_ref[0:1, :]
    slot = place_ref[1:2, :] - float(first)
    place = owner * float(capacity) + slot
    place = jnp.where((slot >= 0.0) & (slot < capacity), place, -1.0)
    place = place - float(8 * capacity * group)
    return one_hot(float_iota((8 * capacity, GROUP), 0) == place)


def send_near_kernel(rows_ref, sent_ref, place_ref, most_ref, ext_ref):
    group_rows = 8 * CAPACITY
    tails = []
    for s in range(N_SEQ):
        whole = rows_ref[s]
        ext_ref[s * ROWS : (s + 1) * ROWS, :] = whole[:ROWS]
        tails.append(whole[ROWS:, :LANES].astype(jnp.float32))
    counts = place_rows(tails, place_ref)
    most_ref[0, 0] = jnp.max(counts).astype(jnp.int32)
    for group in range(N_DP // 8):
        pick = group_picks(place_ref, group, 0, CAPACITY)
        rows = slice(group * group_rows, (group + 1) * group_rows)
        sent_ref[rows, :] = nn_dot(pick, ext_ref[...]).astype(jnp.bfloat16)


def join_far(ids_ref, straight, crossed_ref, ext_ref, delta_ref):
    for m in range(N_SEQ):
        column = jnp.bitwise_xor(ids_ref[0], m)
        whole = crossed_ref[m // 2] if m % 2 else straight[m // 2][0]
        ext_ref[pl.ds(pl.multiple_of(column * ROWS, ROWS), ROWS), :] = whole[:ROWS]
        if delta_ref is not None:
            delta_ref[column] = whole[ROWS:, :LANES].astype(jnp.float32)


def send_far_kernel(ids_ref, place_ref, *refs):
    straight, (crossed_ref, sent_ref, ext_ref, delta_ref) = refs[:N_Y], refs[N_Y:]
    group_rows = 8 * CAPACITY
    join_far(ids_ref, straight, crossed_ref, ext_ref, delta_ref)
    delta = jnp.concatenate([delta_ref[s] for s in range(N_SEQ)], axis=1)
    owner = place_ref[0:1, :]
    slot_cols = [
        turned(place_ref[:, s * ROWS : (s + 1) * ROWS])[:, 1:2] for s in range(N_SEQ)
    ]
    slot_col = jnp.concatenate(slot_cols, axis=0)
    lane = float_iota((GROUP, LANES), 1)
    to_owner = float_iota((N_DP, GROUP), 0) == owner
    tail = jnp.zeros((2 * N_DP, LANES), jnp.float32)
    for head in range(2):
        spread = jnp.concatenate(
            [jnp.where(to_owner, delta[c : c + 1], 0.0) for c in (head, 2 + head)], axis=0
        )
        slot_pick = one_hot(slot_col + (64.0 * head - 1.0) == lane)
        tail = tail + nn_dot(spread.astype(jnp.bfloat16), slot_pick)
    tail = jnp.concatenate([tail[:N_DP], tail[N_DP:]], axis=1)
    for group in range(N_DP // 8):
        pick = group_picks(place_ref, group, 0, CAPACITY)
        rows = slice(group * group_rows, (group + 1) * group_rows)
        sent_ref[rows, :] = nn_dot(pick, ext_ref[...]).astype(jnp.bfloat16)
    row = iota((16, 2 * LANES), 0)
    for dp in range(N_DP):
        inside = dp * CAPACITY % 16
        rows = slice(dp * CAPACITY - inside, dp * CAPACITY - inside + 16)
        kept = sent_ref[rows, : 2 * LANES].astype(jnp.float32)
        mine = jnp.broadcast_to(tail[dp : dp + 1], (16, 2 * LANES))
        sent_ref[rows, : 2 * LANES] = jnp.where(row == inside, mine, kept).astype(jnp.bfloat16)


def send_extra_kernel(ids_ref, place_ref, rows_ref, *refs):
    straight, (crossed_ref, sent_ref, near_ref, far_ref) = refs[:N_Y], refs[N_Y:]
    group_rows = 8 * EXTRA
    for s in range(N_SEQ):
        whole = rows_ref[s]
        near_ref[s * ROWS : (s + 1) * ROWS, :] = whole[:ROWS]
    join_far(ids_ref, straight, crossed_ref, far_ref, None)
    for group in range(N_DP // 8):
        pick = group_picks(place_ref, group, CAPACITY, EXTRA)
        rows = slice(group * group_rows, (group + 1) * group_rows)
        sent_ref[rows, :HALF] = nn_dot(pick, near_ref[...]).astype(jnp.bfloat16)
        sent_ref[rows, HALF:] = nn_dot(pick, far_ref[...]).astype(jnp.bfloat16)


def index_kernel(segment_ref, head_ref, rows_ref, cols_ref):
    sources = []
    for s in range(N_SEQ):
        whole = head_ref[s]
        sources.append(whole[ROWS:, :LANES].astype(jnp.float32)[2:3])
    source = jnp.concatenate(sources, axis=0)
    segment = segment_ref[...].astype(jnp.float32)
    source_cols = turned(source)
    before = iota((ROWS, ROWS), 0) < iota((ROWS, ROWS), 1)
    slots = []
    for s in range(N_SEQ):
        mine = source[s : s + 1]
        hits = ((source_cols[:, s : s + 1] == mine) & before).astype(jnp.float32)
        for earlier in range(s):
            hits = hits + (source_cols[:, earlier : earlier + 1] == mine).astype(jnp.float32)
        slots.append(jnp.sum(hits, axis=0, keepdims=True))
    slot = jnp.concatenate(slots, axis=0)
    columns = turned(jnp.concatenate([source, slot, segment], axis=0))
    lane = iota((ROWS, LANES), 1)
    for s in range(N_SEQ):
        column = jnp.where(lane == 0, columns[:, s : s + 1], 0.0)
        column = jnp.where(lane == 1, columns[:, 8 + s : 9 + s], column)
        column = jnp.where(lane == 2, columns[:, 16 + s : 17 + s], column)
        cols_ref[s * ROWS : (s + 1) * ROWS, :] = column
    rows_ref[0:8, :] = source
    rows_ref[8:16, :] = slot
    rows_ref[16:24, :] = segment


def to_owner_order(cols_ref, arrived_ref, x_ref):
    slots = N_DP * CAPACITY
    slot_id = float_iota((BLOCK, slots), 1)
    for block in range(GROUP // BLOCK):
        rows = slice(block * BLOCK, (block + 1) * BLOCK)
        slot = cols_ref[rows, 1:2] + 1.0
        place = jnp.where(slot < CAPACITY, cols_ref[rows, 0:1] * float(CAPACITY) + slot, -1.0)
        x_ref[rows, :] = nn_dot(one_hot(place == slot_id), arrived_ref[...]).astype(jnp.bfloat16)


def add_extra(most_ref, cols_ref, extra_hbm, extra_ref, sem, x_ref, span):
    @pl.when(most_ref[0, 0] >= CAPACITY)
    def _():
        copy = pltpu.make_async_copy(extra_hbm, extra_ref, sem)
        copy.start()
        copy.wait()
        slot_id = float_iota((BLOCK, N_DP * EXTRA), 1)
        for block in range(GROUP // BLOCK):
            rows = slice(block * BLOCK, (block + 1) * BLOCK)
            slot = cols_ref[rows, 1:2] - float(CAPACITY - 1)
            place = jnp.where(slot >= 0.0, cols_ref[rows, 0:1] * float(EXTRA) + slot, -1.0)
            found = nn_dot(one_hot(place == slot_id), extra_ref[:, span])
            x_ref[rows, :] += found.astype(jnp.bfloat16)


def near_rows(block):
    if block == 0:
        return slice(0, BLOCK)
    return slice((2 * block - 1) * BLOCK, (2 * block + 1) * BLOCK)


def far_rows(block, key_block):
    step = NEAR + (0 if block == 2 else 1 + key_block)
    return slice(step * BLOCK, (step + 1) * BLOCK)


def reaches(segment_ref, block, key_block):
    return segment_ref[(key_block + 1) * BLOCK - 1] == segment_ref[block * BLOCK]


def weigh_kernel(
    segment_ref, most_ref, arrived_ref, extra_hbm, rows_ref, cols_ref,
    x_ref, kt_ref, low_ref, slope_ref, extra_ref, weight_ref, squash_ref, total_ref, sem,
):
    to_owner_order(cols_ref, arrived_ref, x_ref)
    add_extra(most_ref, cols_ref, extra_hbm, extra_ref, sem, x_ref, slice(0, HALF))
    segment = wide(rows_ref[16:24, :])
    for block in range(GROUP // BLOCK):
        rows = slice(block * BLOCK, (block + 1) * BLOCK)
        kt_ref[:, rows] = x_ref[rows, 256:384].astype(jnp.float32).T.astype(jnp.bfloat16)
    for block in range(GROUP // BLOCK):
        rows = slice(block * BLOCK, (block + 1) * BLOCK)
        near = slice(max(block - 1, 0) * BLOCK, (block + 1) * BLOCK)
        near_count = near.stop - near.start
        queries = jnp.concatenate([x_ref[rows, 0:128], x_ref[rows, 128:256]], axis=0)
        segment_q = jnp.concatenate([segment[:, rows]] * 2, axis=1)
        far = range(block - 1)

        def weigh(keys, causal):
            score = nt_dot(x_ref[keys, 256:384], queries)
            squashed = jnp.tanh(score * (scaling / softcap))
            allowed = cols_ref[keys, 2:3] == segment_q
            if causal is not None:
                allowed = allowed & causal
            return squashed, jnp.where(allowed, jnp.exp(softcap * squashed), 0.0)

        def finish(held, squashed, weights, inverse):
            probabilities = weights * inverse
            low_ref[held, :] = probabilities.astype(jnp.bfloat16)
            slope_ref[held, :] = probabilities * (1.0 - squashed * squashed)

        if len(far) > 0:
            total_ref[...] = jnp.zeros_like(total_ref)
        for key_block in far:

            @pl.when(reaches(segment_ref, block, key_block))
            def _(keys=slice(key_block * BLOCK, (key_block + 1) * BLOCK)):
                squashed, weights = weigh(keys, None)
                weight_ref[keys, :] = weights
                squash_ref[keys, :] = squashed
                total_ref[0:1, :] += jnp.sum(weights, axis=0, keepdims=True)

        ahead = iota((near_count, BLOCK), 0) - iota((near_count, BLOCK), 1)
        causal = (ahead <= near_count - BLOCK).astype(jnp.float32)
        causal = jnp.concatenate([causal, causal], axis=1) > 0.0
        squashed, weights = weigh(near, causal)
        total = jnp.sum(weights, axis=0, keepdims=True)
        if len(far) > 0:
            total = total + total_ref[0:1, :]
        inverse = 1.0 / total
        finish(near_rows(block), squashed, weights, inverse)
        if len(far) > 0:
            total_ref[0:1, :] = inverse
        for key_block in far:

            @pl.when(reaches(segment_ref, block, key_block))
            def _(
                keys=slice(key_block * BLOCK, (key_block + 1) * BLOCK),
                held=far_rows(block, key_block),
            ):
                finish(held, squash_ref[keys, :], weight_ref[keys, :], total_ref[0:1, :])


def back_kernel(
    segment_ref, most_ref, arrived_ref, extra_hbm, rows_ref, cols_ref,
    x_hbm, kt_hbm, low_hbm, slope_hbm, out_ref,
    extra_ref, x_ref, kt_ref, low_ref, slope_ref, y_ref, lanes_ref, gqt_ref, gk_ref, gv_ref, sems,
):
    fetched = slice(0, NEAR * BLOCK)
    copies = [
        pltpu.make_async_copy(low_hbm.at[fetched], low_ref.at[fetched], sems.at[0]),
        pltpu.make_async_copy(slope_hbm.at[fetched], slope_ref.at[fetched], sems.at[1]),
        pltpu.make_async_copy(x_hbm, x_ref, sems.at[2]),
        pltpu.make_async_copy(kt_hbm, kt_ref, sems.at[3]),
    ]
    for copy in copies:
        copy.start()
    to_owner_order(cols_ref, arrived_ref, y_ref)
    add_extra(most_ref, cols_ref, extra_hbm, extra_ref, sems.at[4], y_ref, slice(HALF, 2 * HALF))
    slots = N_DP * CAPACITY
    first = one_hot(iota((LANES, slots), 0) * CAPACITY == iota((LANES, slots), 1))
    parts = nn_dot(first, arrived_ref[:, : 2 * LANES])
    from_source = one_hot(float_iota((LANES, GROUP), 0) == wide(rows_ref[0:8, :]))
    slot = wide(rows_ref[8:16, :])
    high = parts[:, :LANES].T.astype(jnp.bfloat16)
    low = parts[:, LANES:].T.astype(jnp.bfloat16)
    both = nn_dot(high, from_source) + nn_dot(low, from_source)
    place = float_iota((LANES, GROUP), 0)
    for head in range(2):
        lanes_ref[head : head + 1, :] = jnp.sum(
            jnp.where(place == slot + 64.0 * head, both, 0.0), axis=0, keepdims=True
        )
    gk_ref[...] = jnp.zeros_like(gk_ref)
    gv_ref[...] = jnp.zeros_like(gv_ref)
    for copy in copies:
        copy.wait()
    for block in range(GROUP // BLOCK):
        rows = slice(block * BLOCK, (block + 1) * BLOCK)
        near = slice(max(block - 1, 0) * BLOCK, (block + 1) * BLOCK)
        queries = jnp.concatenate([x_ref[rows, 0:128], x_ref[rows, 128:256]], axis=0)
        grads = jnp.concatenate([y_ref[rows, 128:256], y_ref[rows, 256:384]], axis=0)
        delta = jnp.concatenate([lanes_ref[0:1, rows], lanes_ref[1:2, rows]], axis=1)

        def back(keys, held):
            gv_ref[keys, :] += nn_dot(low_ref[held, :], grads)
            prob_grad = nt_dot(y_ref[keys, 0:128], grads)
            score_grad = (slope_ref[held, :] * (prob_grad - delta)).astype(jnp.bfloat16)
            gk_ref[keys, :] += nn_dot(score_grad, queries)
            return nn_dot(kt_ref[:, keys], score_grad)

        gqt_ref[...] = back(near, near_rows(block))
        for key_block in range(block - 1):

            @pl.when(reaches(segment_ref, block, key_block))
            def _(
                keys=slice(key_block * BLOCK, (key_block + 1) * BLOCK),
                held=far_rows(block, key_block),
            ):
                late = [
                    pltpu.make_async_copy(low_hbm.at[held], low_ref.at[held], sems.at[0]),
                    pltpu.make_async_copy(slope_hbm.at[held], slope_ref.at[held], sems.at[1]),
                ]
                for copy in late:
                    copy.start()
                for copy in late:
                    copy.wait()
                gqt_ref[...] += back(keys, held)

        turned_back = (gqt_ref[...].T * scaling).astype(jnp.bfloat16)
        out_ref[rows, 0:128] = turned_back[:BLOCK]
        out_ref[rows, 128:256] = turned_back[BLOCK:]
    out_ref[:, 256:384] = (gk_ref[...] * scaling).astype(jnp.bfloat16)
    out_ref[:, 384:512] = gv_ref[...].astype(jnp.bfloat16)


def unpack_kernel(returned_ref, query_ref, key_ref, value_ref):
    for group in range(N_SEQ):
        two = slice(2 * group * HEAD_DIM, 2 * (group + 1) * HEAD_DIM)
        one = slice(group * HEAD_DIM, (group + 1) * HEAD_DIM)
        query_ref[:, two] = returned_ref[group, :, 0:256]
        key_ref[:, one] = returned_ref[group, :, 256:384]
        value_ref[:, one] = returned_ref[group, :, 384:512]


def shape(dims, dtype=jnp.bfloat16):
    return jax.ShapeDtypeStruct(dims, dtype)


def call(kernel, name, out_shape, in_specs, out_specs, scratch=(), params=PARAMS, flops=0):
    estimate = pl.CostEstimate(flops=flops, bytes_accessed=4_000_000, transcendentals=0)
    return pl.pallas_call(
        kernel,
        out_shape=out_shape,
        in_specs=in_specs,
        out_specs=out_specs,
        scratch_shapes=list(scratch),
        compiler_params=params,
        cost_estimate=estimate if flops else None,
        name=name,
    )


def rows_vmem(dims, dtype=jnp.bfloat16):
    return pltpu.VMEM(dims, dtype)


PACKED = (ROWS + 8, HALF)
HELD = (STEPS * BLOCK, 2 * BLOCK)
SLOTS = (N_DP * CAPACITY, HALF)

make_request = call(request_kernel, "request", shape((N_DP, LANES), jnp.int32), [VMEM], VMEM)
pack_near = call(
    pack_near_kernel, "pack_near", shape((N_SEQ,) + PACKED), [VMEM, VMEM, HBM, HBM], VMEM,
    [rows_vmem((ROWS, 2048)), rows_vmem((ROWS, 1024)), pltpu.SemaphoreType.DMA((2,))], FULL,
)
pack_far = call(
    pack_far_kernel, "pack_far", [shape((2,) + PACKED)] * N_Y, [SMEM, HBM, HBM, HBM], [VMEM] * N_Y,
    [
        rows_vmem((ROWS, 1024)), rows_vmem((ROWS, 2048)), rows_vmem((ROWS, 2048)),
        rows_vmem((N_SEQ, 8, LANES), jnp.float32), pltpu.SemaphoreType.DMA((3,)),
    ],
    FULL,
)
send_near = call(
    send_near_kernel, "send_near",
    [shape(SLOTS), shape((8, GROUP), jnp.float32), shape((1, 1), jnp.int32)],
    [VMEM], [VMEM, VMEM, SMEM], [rows_vmem((GROUP, HALF))], flops=1_400_000_000,
)
send_far = call(
    send_far_kernel, "send_far", shape(SLOTS), [SMEM] + [VMEM] * (2 + N_Y), VMEM,
    [rows_vmem((GROUP, HALF)), rows_vmem((N_SEQ, 8, LANES), jnp.float32)], flops=1_400_000_000,
)
send_extra = call(
    send_extra_kernel, "send_extra", shape((N_DP * EXTRA, 2 * HALF)), [SMEM] + [VMEM] * (3 + N_Y), VMEM,
    [rows_vmem((GROUP, HALF)), rows_vmem((GROUP, HALF))],
)
make_index = call(
    index_kernel, "index",
    [shape((24, LANES), jnp.float32), shape((GROUP, LANES), jnp.float32)], [VMEM, VMEM], [VMEM, VMEM],
    flops=200_000_000,
)
weigh = call(
    weigh_kernel, "weigh",
    [shape((GROUP, HALF)), shape((HEAD_DIM, GROUP)), shape(HELD), shape(HELD, jnp.float32)],
    [SMEM, SMEM, VMEM, HBM, VMEM, VMEM], [VMEM] * 4,
    [
        rows_vmem((N_DP * EXTRA, 2 * HALF)),
        rows_vmem((GROUP - 2 * BLOCK, 2 * BLOCK), jnp.float32),
        rows_vmem((GROUP - 2 * BLOCK, 2 * BLOCK), jnp.float32),
        rows_vmem((8, 2 * BLOCK), jnp.float32),
        pltpu.SemaphoreType.DMA,
    ],
    flops=3_000_000_000,
)
back = call(
    back_kernel, "back", shape((GROUP, 4 * HEAD_DIM)),
    [SMEM, SMEM, VMEM, HBM, VMEM, VMEM, HBM, HBM, HBM, HBM], VMEM,
    [
        rows_vmem((N_DP * EXTRA, 2 * HALF)),
        rows_vmem((GROUP, HALF)),
        rows_vmem((HEAD_DIM, GROUP)),
        rows_vmem(HELD),
        rows_vmem(HELD, jnp.float32),
        rows_vmem((GROUP, HALF)),
        rows_vmem((8, GROUP), jnp.float32),
        rows_vmem((HEAD_DIM, 2 * BLOCK), jnp.float32),
        rows_vmem((GROUP, HEAD_DIM), jnp.float32),
        rows_vmem((GROUP, HEAD_DIM), jnp.float32),
        pltpu.SemaphoreType.DMA((5,)),
    ],
    FULL,
)
unpack = call(
    unpack_kernel, "unpack", [shape((ROWS, 2048)), shape((ROWS, 1024)), shape((ROWS, 1024))],
    [VMEM], [VMEM] * 3,
)


def relay(array):
    return lax.all_to_all(array, "dp", split_axis=0, concat_axis=0, tiled=True)


def swap(array, m):
    return lax.ppermute(array, "seq", [(s, s ^ m) for s in range(N_SEQ)]) if m else array


def local(query, key_rows, value_rows, attn_out, out_grad, source_row, segment_ids):
    ids = lax.axis_index("seq").reshape(1)
    listed = source_row.reshape(1, ROWS)
    asked = relay(make_request(listed))
    far = pack_far(ids, value_rows, attn_out, out_grad)
    asked, far = lax.optimization_barrier((asked, far))
    near = pack_near(listed, asked, query, key_rows)
    near = lax.all_to_all(near, "seq", split_axis=0, concat_axis=0, tiled=True)
    sent, place, most = send_near(near)
    sent, far, near = lax.optimization_barrier((sent, far, near))
    arrived_near = relay(sent)
    straight = [swap(far[m], 2 * m) for m in range(N_Y)]
    crossed = swap(jnp.stack([array[1] for array in straight]), 1)
    rows, cols = make_index(segment_ids.reshape(N_SEQ, ROWS), near)
    arrived_far = relay(send_far(ids, place, *straight, crossed))
    extra = lax.cond(
        most[0, 0] >= CAPACITY,
        lambda place, near, straight, crossed: relay(
            send_extra(ids, place, near, *straight, crossed)
        ),
        lambda place, near, straight, crossed: jnp.zeros((N_DP * EXTRA, 2 * HALF), jnp.bfloat16),
        place,
        near,
        straight,
        crossed,
    )
    held = weigh(segment_ids, most, arrived_near, extra, rows, cols)
    grads = back(segment_ids, most, arrived_far, extra, rows, cols, *held)
    returned = lax.all_to_all(
        grads.reshape(N_SEQ, ROWS, 4 * HEAD_DIM), "seq", split_axis=0, concat_axis=0, tiled=True
    )
    return unpack(returned)


def solution(mesh):
    in_specs = (
        P(("dp", "seq"), None),
        P(("dp", "seq"), None),
        P(("dp", "seq"), None),
        P(("dp", "seq"), None),
        P(("dp", "seq"), None),
        P(("dp", "seq")),
        P("dp"),
    )
    out_specs = (P(("dp", "seq"), None), P(("dp", "seq"), None), P(("dp", "seq"), None))
    return jax.shard_map(local, mesh=mesh, in_specs=in_specs, out_specs=out_specs, check_vma=False)
```

```python
import functools

import jax
import jax.numpy as jnp
from jax import lax
from jax.experimental import pallas as pl
from jax.experimental.pallas import tpu as pltpu
from jax.sharding import PartitionSpec as P

HEAD_DIM = 128
N_DP = 32
N_SEQ = 8
ROWS = 128
GROUP = N_SEQ * ROWS
WIDTH = 6 * HEAD_DIM
LANES = 128
BLOCK = 256
CAPACITY = 56
EXTRA = 16

scaling = 1.0 / 12.0
softcap = 50.0

PARAMS = pltpu.CompilerParams(vmem_limit_bytes=28 * 1024 * 1024)
FULL = pltpu.CompilerParams(vmem_limit_bytes=60 * 1024 * 1024)


def iota(shape, dim):
    return lax.broadcasted_iota(jnp.int32, shape, dim)


def nt_dot(left, right):
    return lax.dot_general(left, right, (((1,), (1,)), ((), ())), preferred_element_type=jnp.float32)


def nn_dot(left, right):
    return jnp.dot(left, right, preferred_element_type=jnp.float32)


def pack_kernel(me_ref, query_hbm, key_hbm, value_hbm, out_hbm, grad_hbm, *refs):
    packed_refs = refs[:N_SEQ]
    query_ref, key_ref, value_ref, out_ref, grad_ref, delta_ref, sems = refs[N_SEQ:]
    pairs = (
        (grad_hbm, grad_ref),
        (out_hbm, out_ref),
        (query_hbm, query_ref),
        (key_hbm, key_ref),
        (value_hbm, value_ref),
    )
    copies = [
        pltpu.make_async_copy(source, target, sems.at[i])
        for i, (source, target) in enumerate(pairs)
    ]
    for copy in copies:
        copy.start()
    copies[0].wait()
    copies[1].wait()
    lane = iota((ROWS, LANES), 1)
    table = jnp.zeros((ROWS, LANES), jnp.float32)
    for head in range(2 * N_SEQ):
        cols = slice(head * HEAD_DIM, (head + 1) * HEAD_DIM)
        product = grad_ref[:, cols].astype(jnp.float32) * out_ref[:, cols].astype(jnp.float32)
        table = jnp.where(lane == head, jnp.sum(product, axis=1, keepdims=True), table)
    delta = table.T
    high = delta.astype(jnp.bfloat16).astype(jnp.float32)
    low = delta - high
    for group in range(N_SEQ):
        pair = slice(2 * group, 2 * group + 2)
        delta_ref[group] = jnp.concatenate(
            [high[pair], low[pair], jnp.zeros((4, LANES), jnp.float32)], axis=0
        )
    pad_cols = jnp.zeros((8, WIDTH - LANES), jnp.float32)
    for copy in copies[2:]:
        copy.wait()
    me = me_ref[0]
    for m in range(N_SEQ):
        group = jnp.bitwise_xor(me, m)
        two = pl.ds(pl.multiple_of(group * 256, 256), 256)
        one = pl.ds(pl.multiple_of(group * 128, 128), 128)
        rows = jnp.concatenate(
            [query_ref[:, two], key_ref[:, one], value_ref[:, one], grad_ref[:, two]], axis=1
        )
        extra = jnp.concatenate([delta_ref[group], pad_cols], axis=1)
        packed_refs[m][...] = jnp.concatenate([rows.astype(jnp.float32), extra], axis=0).astype(
            jnp.bfloat16
        )


def wide(rows):
    return jnp.concatenate([rows[s : s + 1] for s in range(N_SEQ)], axis=1)


def index_kernel(me_ref, segment_ref, *refs):
    lists, (rows_ref, cols_ref, request_ref, most_ref, list_ref) = refs[:N_SEQ], refs[N_SEQ:]
    for m in range(N_SEQ):
        list_ref[pl.ds(jnp.bitwise_xor(me_ref[0], m), 1), :] = lists[m][...]
    listed = list_ref[...]
    source = (listed // GROUP).astype(jnp.float32)
    local_row = (listed % ROWS).astype(jnp.float32)
    segment = segment_ref[...].astype(jnp.float32)
    blank = jnp.zeros((LANES - 8, LANES), jnp.float32)
    source_cols = jnp.concatenate([source, blank], axis=0).T
    before = iota((ROWS, ROWS), 0) < iota((ROWS, ROWS), 1)
    slots = []
    for s in range(N_SEQ):
        mine = source[s : s + 1]
        hits = ((source_cols[:, s : s + 1] == mine) & before).astype(jnp.float32)
        for earlier in range(s):
            hits = hits + (source_cols[:, earlier : earlier + 1] == mine).astype(jnp.float32)
        slots.append(jnp.sum(hits, axis=0, keepdims=True))
    slot = jnp.concatenate(slots, axis=0)
    blank = jnp.zeros((LANES - 24, LANES), jnp.float32)
    turned = jnp.concatenate([source, slot, segment, blank], axis=0).T
    lane = iota((ROWS, LANES), 1)
    picks = []
    for s in range(N_SEQ):
        columns = jnp.where(lane == 0, turned[:, s : s + 1], 0.0)
        columns = jnp.where(lane == 1, turned[:, 8 + s : 9 + s], columns)
        columns = jnp.where(lane == 2, turned[:, 16 + s : 17 + s], columns)
        cols_ref[s * ROWS : (s + 1) * ROWS, :] = columns
        picks.append((lane.astype(jnp.float32) == turned[:, 8 + s : 9 + s] + 1.0).astype(jnp.float32))
    rows_ref[0:8, :] = source
    rows_ref[8:16, :] = slot
    rows_ref[16:24, :] = segment
    pick = jnp.concatenate(picks, axis=0).astype(jnp.bfloat16)
    from_source = iota((N_DP, GROUP), 0).astype(jnp.float32) == wide(source)
    column = (iota((1, GROUP), 1) // ROWS).astype(jnp.float32)
    low = jnp.where(from_source, wide(local_row) + 1.0, 0.0).astype(jnp.bfloat16)
    high = jnp.where(from_source, column, 0.0).astype(jnp.bfloat16)
    table = nn_dot(low, pick) + float(ROWS) * nn_dot(high, pick)
    request_ref[...] = table.astype(jnp.int32)
    most_ref[0, 0] = (jnp.max(slot) + 1.0).astype(jnp.int32)


def turned_requests(request_ref):
    blank = jnp.zeros((LANES - N_DP, LANES), jnp.float32)
    return jnp.concatenate([request_ref[...].astype(jnp.float32), blank], axis=0).T - 1.0


def group_picks(turned, group, first, capacity):
    column = jnp.concatenate(
        [turned[first : first + capacity, d : d + 1] for d in range(8 * group, 8 * group + 8)], axis=0
    )
    row_id = iota((8 * capacity, GROUP), 1).astype(jnp.float32)
    return (column == row_id).astype(jnp.float32).astype(jnp.bfloat16)


def join_columns(me_ref, parts, ext_ref, delta_ref):
    for m in range(N_SEQ):
        column = jnp.bitwise_xor(me_ref[0], m)
        whole = parts[m][...]
        ext_ref[pl.ds(pl.multiple_of(column * ROWS, ROWS), ROWS), :] = whole[:ROWS]
        if delta_ref is not None:
            delta_ref[column] = whole[ROWS:, :LANES].astype(jnp.float32)


def send_extra_kernel(me_ref, request_ref, *refs):
    parts, (sent_ref, ext_ref) = refs[:N_SEQ], refs[N_SEQ:]
    group_rows = 8 * EXTRA
    turned = turned_requests(request_ref)
    join_columns(me_ref, parts, ext_ref, None)
    for group in range(N_DP // 8):
        pick = group_picks(turned, group, CAPACITY, EXTRA)
        rows = slice(group * group_rows, (group + 1) * group_rows)
        sent_ref[rows, :] = nn_dot(pick, ext_ref[...]).astype(jnp.bfloat16)


def send_kernel(me_ref, most_ref, request_ref, *refs):
    parts, (sent_ref, ext_ref, place_ref, delta_ref) = refs[:N_SEQ], refs[N_SEQ:]
    capacity = CAPACITY
    group_rows = 8 * capacity
    turned = turned_requests(request_ref)
    join_columns(me_ref, parts, ext_ref, delta_ref)
    delta = jnp.concatenate([delta_ref[s] for s in range(N_SEQ)], axis=1)

    def places(pick, group, first, count):
        index = iota((8, 8 * count), 1)
        owner = index // count
        value = jnp.where(
            iota((8, 8 * count), 0) == 0, owner + 8 * group, index - owner * count + first
        )
        return nn_dot(value.astype(jnp.float32).astype(jnp.bfloat16), pick)

    place = jnp.zeros((8, GROUP), jnp.float32)
    for group in range(N_DP // 8):
        pick = group_picks(turned, group, 0, capacity)
        place = place + places(pick, group, 0, capacity)
        rows = slice(group * group_rows, (group + 1) * group_rows)
        sent_ref[rows, :] = nn_dot(pick, ext_ref[...]).astype(jnp.bfloat16)
    place_ref[...] = place

    @pl.when(most_ref[0, 0] >= CAPACITY)
    def _():
        more = jnp.zeros((8, GROUP), jnp.float32)
        for group in range(N_DP // 8):
            more = more + places(group_picks(turned, group, CAPACITY, EXTRA), group, CAPACITY, EXTRA)
        place_ref[...] += more

    place = place_ref[...]
    owner_of = place[0:1]
    slot_cols = []
    for s in range(N_SEQ):
        part = place[:, s * ROWS : (s + 1) * ROWS]
        blank = jnp.zeros((LANES - 8, LANES), jnp.float32)
        slot_cols.append(jnp.concatenate([part, blank], axis=0).T[:, 1:2])
    slot_col = jnp.concatenate(slot_cols, axis=0)
    lane = iota((GROUP, LANES), 1).astype(jnp.float32)
    to_owner = iota((N_DP, GROUP), 0).astype(jnp.float32) == owner_of
    tail = jnp.zeros((2 * N_DP, LANES), jnp.float32)
    for head in range(2):
        spread = jnp.concatenate(
            [jnp.where(to_owner, delta[c : c + 1], 0.0) for c in (head, 2 + head)], axis=0
        )
        slot_pick = (slot_col + (64.0 * head - 1.0) == lane).astype(jnp.float32)
        tail = tail + nn_dot(spread.astype(jnp.bfloat16), slot_pick.astype(jnp.bfloat16))
    tail = jnp.concatenate([tail[:N_DP], tail[N_DP:]], axis=1)
    row = iota((16, 2 * LANES), 0)
    for owner in range(N_DP):
        inside = owner * capacity % 16
        rows = slice(owner * capacity - inside, owner * capacity - inside + 16)
        kept = sent_ref[rows, : 2 * LANES].astype(jnp.float32)
        mine = jnp.broadcast_to(tail[owner : owner + 1], (16, 2 * LANES))
        sent_ref[rows, : 2 * LANES] = jnp.where(row == inside, mine, kept).astype(jnp.bfloat16)


def attend_kernel(
    segment_ref, most_ref, arrived_ref, extra_ref, rows_ref, cols_ref, out_ref,
    x_ref, kt_ref, lanes_ref, weight_ref, squash_ref, total_ref, gqt_ref, gk_ref, gv_ref,
):
    slots = N_DP * CAPACITY
    blocks = GROUP // BLOCK
    slot_id = iota((BLOCK, slots), 1).astype(jnp.float32)
    for block in range(blocks):
        rows = slice(block * BLOCK, (block + 1) * BLOCK)
        slot = cols_ref[rows, 1:2] + 1.0
        place = jnp.where(slot < CAPACITY, cols_ref[rows, 0:1] * float(CAPACITY) + slot, -1.0)
        pick = (place == slot_id).astype(jnp.float32).astype(jnp.bfloat16)
        x_ref[rows, :] = nn_dot(pick, arrived_ref[...]).astype(jnp.bfloat16)

    @pl.when(most_ref[0, 0] >= CAPACITY)
    def _():
        extra_id = iota((BLOCK, N_DP * EXTRA), 1).astype(jnp.float32)
        for block in range(blocks):
            rows = slice(block * BLOCK, (block + 1) * BLOCK)
            slot = cols_ref[rows, 1:2] - float(CAPACITY - 1)
            place = jnp.where(slot >= 0.0, cols_ref[rows, 0:1] * float(EXTRA) + slot, -1.0)
            pick = (place == extra_id).astype(jnp.float32).astype(jnp.bfloat16)
            x_ref[rows, :] += nn_dot(pick, extra_ref[...]).astype(jnp.bfloat16)

    for block in range(blocks):
        rows = slice(block * BLOCK, (block + 1) * BLOCK)
        kt_ref[:, rows] = x_ref[rows, 256:384].astype(jnp.float32).T.astype(jnp.bfloat16)
    first = iota((LANES, slots), 0) * CAPACITY == iota((LANES, slots), 1)
    first = first.astype(jnp.float32).astype(jnp.bfloat16)
    parts = nn_dot(first, arrived_ref[:, : 2 * LANES])
    source = wide(rows_ref[0:8, :])
    slot = wide(rows_ref[8:16, :])
    segment = wide(rows_ref[16:24, :])
    from_source = iota((LANES, GROUP), 0).astype(jnp.float32) == source
    from_source = from_source.astype(jnp.float32).astype(jnp.bfloat16)
    high = parts[:, :LANES].T.astype(jnp.bfloat16)
    low = parts[:, LANES:].T.astype(jnp.bfloat16)
    both = nn_dot(high, from_source) + nn_dot(low, from_source)
    place = iota((LANES, GROUP), 0).astype(jnp.float32)
    for head in range(2):
        lanes_ref[head : head + 1, :] = jnp.sum(
            jnp.where(place == slot + 64.0 * head, both, 0.0), axis=0, keepdims=True
        )
    gk_ref[...] = jnp.zeros_like(gk_ref)
    gv_ref[...] = jnp.zeros_like(gv_ref)

    for block in range(blocks):
        rows = slice(block * BLOCK, (block + 1) * BLOCK)
        near = slice(max(block - 1, 0) * BLOCK, (block + 1) * BLOCK)
        near_count = near.stop - near.start
        queries = jnp.concatenate([x_ref[rows, 0:128], x_ref[rows, 128:256]], axis=0)
        grads = jnp.concatenate([x_ref[rows, 512:640], x_ref[rows, 640:768]], axis=0)
        delta = jnp.concatenate([lanes_ref[0:1, rows], lanes_ref[1:2, rows]], axis=1)
        segment_q = jnp.concatenate([segment[:, rows]] * 2, axis=1)
        far = range(block - 1)

        def weigh(keys, causal):
            score = nt_dot(x_ref[keys, 256:384], queries)
            squashed = jnp.tanh(score * (scaling / softcap))
            allowed = cols_ref[keys, 2:3] == segment_q
            if causal is not None:
                allowed = allowed & causal
            return squashed, jnp.where(allowed, jnp.exp(softcap * squashed), 0.0)

        def back(keys, squashed, weights, inverse):
            probabilities = weights * inverse
            gv_ref[keys, :] += nn_dot(probabilities.astype(jnp.bfloat16), grads)
            prob_grad = nt_dot(x_ref[keys, 384:512], grads)
            score_grad = probabilities * (prob_grad - delta) * (1.0 - squashed * squashed)
            score_grad = score_grad.astype(jnp.bfloat16)
            gk_ref[keys, :] += nn_dot(score_grad, queries)
            return nn_dot(kt_ref[:, keys], score_grad)

        def reaches(key_block):
            return segment_ref[(key_block + 1) * BLOCK - 1] == segment_ref[block * BLOCK]

        if len(far) > 0:
            total_ref[...] = jnp.zeros_like(total_ref)
        for key_block in far:

            @pl.when(reaches(key_block))
            def _(keys=slice(key_block * BLOCK, (key_block + 1) * BLOCK)):
                squashed, weights = weigh(keys, None)
                weight_ref[keys, :] = weights
                squash_ref[keys, :] = squashed
                total_ref[0:1, :] += jnp.sum(weights, axis=0, keepdims=True)

        ahead = iota((near_count, BLOCK), 0) - iota((near_count, BLOCK), 1)
        causal = (ahead <= near_count - BLOCK).astype(jnp.float32)
        causal = jnp.concatenate([causal, causal], axis=1) > 0.0
        squashed, weights = weigh(near, causal)
        total = jnp.sum(weights, axis=0, keepdims=True)
        if len(far) > 0:
            total = total + total_ref[0:1, :]
        inverse = 1.0 / total
        gqt_ref[...] = back(near, squashed, weights, inverse)
        if len(far) > 0:
            total_ref[0:1, :] = inverse
        for key_block in far:

            @pl.when(reaches(key_block))
            def _(keys=slice(key_block * BLOCK, (key_block + 1) * BLOCK)):
                gqt_ref[...] += back(
                    keys, squash_ref[keys, :], weight_ref[keys, :], total_ref[0:1, :]
                )

        turned = (gqt_ref[...].T * scaling).astype(jnp.bfloat16)
        out_ref[rows, 0:128] = turned[:BLOCK]
        out_ref[rows, 128:256] = turned[BLOCK:]
    out_ref[:, 256:384] = (gk_ref[...] * scaling).astype(jnp.bfloat16)
    out_ref[:, 384:512] = gv_ref[...].astype(jnp.bfloat16)


def unpack_kernel(returned_ref, query_ref, key_ref, value_ref):
    for group in range(N_SEQ):
        two = slice(2 * group * HEAD_DIM, 2 * (group + 1) * HEAD_DIM)
        one = slice(group * HEAD_DIM, (group + 1) * HEAD_DIM)
        query_ref[:, two] = returned_ref[group, :, 0:256]
        key_ref[:, one] = returned_ref[group, :, 256:384]
        value_ref[:, one] = returned_ref[group, :, 384:512]


def shape(dims, dtype=jnp.bfloat16):
    return jax.ShapeDtypeStruct(dims, dtype)


VMEM = pl.BlockSpec(memory_space=pltpu.VMEM)
SMEM = pl.BlockSpec(memory_space=pltpu.SMEM)


def cost(flops, moved, transcendentals=0):
    return pl.CostEstimate(flops=flops, bytes_accessed=moved, transcendentals=transcendentals)


def pack(me, query, key_rows, value_rows, attn_out, out_grad):
    return pl.pallas_call(
        pack_kernel,
        out_shape=[shape((ROWS + 8, WIDTH))] * N_SEQ,
        in_specs=[SMEM] + [pl.BlockSpec(memory_space=pltpu.HBM)] * 5,
        out_specs=[VMEM] * N_SEQ,
        scratch_shapes=[
            pltpu.VMEM((ROWS, 2048), jnp.bfloat16),
            pltpu.VMEM((ROWS, 1024), jnp.bfloat16),
            pltpu.VMEM((ROWS, 1024), jnp.bfloat16),
            pltpu.VMEM((ROWS, 2048), jnp.bfloat16),
            pltpu.VMEM((ROWS, 2048), jnp.bfloat16),
            pltpu.VMEM((N_SEQ, 8, LANES), jnp.float32),
            pltpu.SemaphoreType.DMA((5,)),
        ],
        compiler_params=FULL,
        name="pack",
    )(me, query, key_rows, value_rows, attn_out, out_grad)


def index(me, segments, lists):
    return pl.pallas_call(
        index_kernel,
        out_shape=(
            shape((24, LANES), jnp.float32),
            shape((GROUP, LANES), jnp.float32),
            shape((N_DP, LANES), jnp.int32),
            shape((1, 1), jnp.int32),
        ),
        in_specs=[SMEM] + [VMEM] * 9,
        out_specs=(VMEM, VMEM, VMEM, SMEM),
        scratch_shapes=[pltpu.VMEM((N_SEQ, LANES), jnp.int32)],
        compiler_params=PARAMS,
        name="index",
    )(me, segments.reshape(N_SEQ, ROWS), *lists)


def send(me, most, request, parts):
    return pl.pallas_call(
        send_kernel,
        out_shape=shape((N_DP * CAPACITY, WIDTH)),
        in_specs=[SMEM, SMEM] + [VMEM] * 9,
        scratch_shapes=[
            pltpu.VMEM((GROUP, WIDTH), jnp.bfloat16),
            pltpu.VMEM((8, GROUP), jnp.float32),
            pltpu.VMEM((N_SEQ, 8, LANES), jnp.float32),
        ],
        compiler_params=PARAMS,
        cost_estimate=cost(2 * N_DP * CAPACITY * GROUP * WIDTH, 4_000_000),
        name="send",
    )(me, most, request, *parts)


def send_extra(me, request, parts):
    return pl.pallas_call(
        send_extra_kernel,
        out_shape=shape((N_DP * EXTRA, WIDTH)),
        in_specs=[SMEM] + [VMEM] * 9,
        scratch_shapes=[pltpu.VMEM((GROUP, WIDTH), jnp.bfloat16)],
        compiler_params=PARAMS,
        name="send_extra",
    )(me, request, *parts)


def attend(segments, most, arrived, extra, rows, cols):
    return pl.pallas_call(
        attend_kernel,
        out_shape=shape((GROUP, 4 * HEAD_DIM)),
        in_specs=[SMEM, SMEM, VMEM, VMEM, VMEM, VMEM],
        scratch_shapes=[
            pltpu.VMEM((GROUP, WIDTH), jnp.bfloat16),
            pltpu.VMEM((HEAD_DIM, GROUP), jnp.bfloat16),
            pltpu.VMEM((8, GROUP), jnp.float32),
            pltpu.VMEM((GROUP - 2 * BLOCK, 2 * BLOCK), jnp.float32),
            pltpu.VMEM((GROUP - 2 * BLOCK, 2 * BLOCK), jnp.float32),
            pltpu.VMEM((8, 2 * BLOCK), jnp.float32),
            pltpu.VMEM((HEAD_DIM, 2 * BLOCK), jnp.float32),
            pltpu.VMEM((GROUP, HEAD_DIM), jnp.float32),
            pltpu.VMEM((GROUP, HEAD_DIM), jnp.float32),
        ],
        compiler_params=PARAMS,
        name="attend",
    )(segments, most, arrived, extra, rows, cols)


def unpack(returned):
    return pl.pallas_call(
        unpack_kernel,
        out_shape=(shape((ROWS, 2048)), shape((ROWS, 1024)), shape((ROWS, 1024))),
        compiler_params=PARAMS,
        name="unpack",
    )(returned)


def relay(array):
    return lax.all_to_all(array, "dp", split_axis=0, concat_axis=0, tiled=True)


def local(query, key_rows, value_rows, attn_out, out_grad, source_row, segment_ids):
    me = lax.axis_index("seq").reshape(1)

    def swap(array, m):
        return lax.ppermute(array, "seq", [(s, s ^ m) for s in range(N_SEQ)]) if m else array

    lists = [swap(source_row.reshape(1, ROWS), m) for m in range(N_SEQ)]
    packed = pack(me, query, key_rows, value_rows, attn_out, out_grad)
    packed, lists = lax.optimization_barrier((packed, lists))
    parts = [swap(packed[m], m) for m in range(N_SEQ)]
    rows, cols, request, most = index(me, segment_ids, lists)
    request, rows, cols, most, segment_ids = lax.optimization_barrier(
        (relay(request), rows, cols, most, segment_ids)
    )
    arrived = relay(send(me, most, request, parts))
    extra = lax.cond(
        most[0, 0] >= CAPACITY,
        lambda request, *parts: relay(send_extra(me, request, parts)),
        lambda request, *parts: jnp.zeros((N_DP * EXTRA, WIDTH), jnp.bfloat16),
        request,
        *parts,
    )
    grads = attend(segment_ids, most, arrived, extra, rows, cols)
    returned = lax.all_to_all(
        grads.reshape(N_SEQ, ROWS, 4 * HEAD_DIM), "seq", split_axis=0, concat_axis=0, tiled=True
    )
    return unpack(returned)


def solution(mesh):
    in_specs = (
        P(("dp", "seq"), None),
        P(("dp", "seq"), None),
        P(("dp", "seq"), None),
        P(("dp", "seq"), None),
        P(("dp", "seq"), None),
        P(("dp", "seq")),
        P("dp"),
    )
    out_specs = (P(("dp", "seq"), None), P(("dp", "seq"), None), P(("dp", "seq"), None))
    return jax.shard_map(local, mesh=mesh, in_specs=in_specs, out_specs=out_specs, check_vma=False)
```

```python
import functools

import jax
import jax.numpy as jnp
from jax import lax
from jax.experimental import pallas as pl
from jax.experimental.pallas import tpu as pltpu
from jax.sharding import PartitionSpec as P

HEAD_DIM = 128
N_DP = 32
N_SEQ = 8
ROWS = 128
GROUP = N_SEQ * ROWS
WIDTH = 6 * HEAD_DIM
LANES = 128
BLOCK = 256
SMALL = 48
CAPACITY = 56
EXTRA = 16

scaling = 1.0 / 12.0
softcap = 50.0

PARAMS = pltpu.CompilerParams(vmem_limit_bytes=28 * 1024 * 1024)
FULL = pltpu.CompilerParams(vmem_limit_bytes=60 * 1024 * 1024)


def iota(shape, dim):
    return lax.broadcasted_iota(jnp.int32, shape, dim)


def nt_dot(left, right):
    return lax.dot_general(left, right, (((1,), (1,)), ((), ())), preferred_element_type=jnp.float32)


def nn_dot(left, right):
    return jnp.dot(left, right, preferred_element_type=jnp.float32)


def pack_kernel(me_ref, query_hbm, key_hbm, value_hbm, out_hbm, grad_hbm, *refs):
    packed_refs = refs[:N_SEQ]
    query_ref, key_ref, value_ref, out_ref, grad_ref, delta_ref, sems = refs[N_SEQ:]
    pairs = (
        (grad_hbm, grad_ref),
        (out_hbm, out_ref),
        (query_hbm, query_ref),
        (key_hbm, key_ref),
        (value_hbm, value_ref),
    )
    copies = [
        pltpu.make_async_copy(source, target, sems.at[i])
        for i, (source, target) in enumerate(pairs)
    ]
    for copy in copies:
        copy.start()
    copies[0].wait()
    copies[1].wait()
    lane = iota((ROWS, LANES), 1)
    table = jnp.zeros((ROWS, LANES), jnp.float32)
    for head in range(2 * N_SEQ):
        cols = slice(head * HEAD_DIM, (head + 1) * HEAD_DIM)
        product = grad_ref[:, cols].astype(jnp.float32) * out_ref[:, cols].astype(jnp.float32)
        table = jnp.where(lane == head, jnp.sum(product, axis=1, keepdims=True), table)
    delta = table.T
    high = delta.astype(jnp.bfloat16).astype(jnp.float32)
    low = delta - high
    for group in range(N_SEQ):
        pair = slice(2 * group, 2 * group + 2)
        delta_ref[group] = jnp.concatenate(
            [high[pair], low[pair], jnp.zeros((4, LANES), jnp.float32)], axis=0
        )
    pad_cols = jnp.zeros((8, WIDTH - LANES), jnp.float32)
    for copy in copies[2:]:
        copy.wait()
    me = me_ref[0]
    for m in range(N_SEQ):
        group = jnp.bitwise_xor(me, m)
        two = pl.ds(pl.multiple_of(group * 256, 256), 256)
        one = pl.ds(pl.multiple_of(group * 128, 128), 128)
        rows = jnp.concatenate(
            [query_ref[:, two], key_ref[:, one], value_ref[:, one], grad_ref[:, two]], axis=1
        )
        extra = jnp.concatenate([delta_ref[group], pad_cols], axis=1)
        packed_refs[m][...] = jnp.concatenate([rows.astype(jnp.float32), extra], axis=0).astype(
            jnp.bfloat16
        )


def wide(rows):
    return jnp.concatenate([rows[s : s + 1] for s in range(N_SEQ)], axis=1)


def index_kernel(me_ref, segment_ref, *refs):
    lists, (rows_ref, cols_ref, request_ref, most_ref, list_ref) = refs[:N_SEQ], refs[N_SEQ:]
    for m in range(N_SEQ):
        list_ref[pl.ds(jnp.bitwise_xor(me_ref[0], m), 1), :] = lists[m][...]
    listed = list_ref[...]
    source = (listed // GROUP).astype(jnp.float32)
    local_row = (listed % ROWS).astype(jnp.float32)
    segment = segment_ref[...].astype(jnp.float32)
    blank = jnp.zeros((LANES - 8, LANES), jnp.float32)
    source_cols = jnp.concatenate([source, blank], axis=0).T
    before = iota((ROWS, ROWS), 0) < iota((ROWS, ROWS), 1)
    slots = []
    for s in range(N_SEQ):
        mine = source[s : s + 1]
        hits = ((source_cols[:, s : s + 1] == mine) & before).astype(jnp.float32)
        for earlier in range(s):
            hits = hits + (source_cols[:, earlier : earlier + 1] == mine).astype(jnp.float32)
        slots.append(jnp.sum(hits, axis=0, keepdims=True))
    slot = jnp.concatenate(slots, axis=0)
    blank = jnp.zeros((LANES - 24, LANES), jnp.float32)
    turned = jnp.concatenate([source, slot, segment, blank], axis=0).T
    lane = iota((ROWS, LANES), 1)
    picks = []
    for s in range(N_SEQ):
        columns = jnp.where(lane == 0, turned[:, s : s + 1], 0.0)
        columns = jnp.where(lane == 1, turned[:, 8 + s : 9 + s], columns)
        columns = jnp.where(lane == 2, turned[:, 16 + s : 17 + s], columns)
        cols_ref[s * ROWS : (s + 1) * ROWS, :] = columns
        picks.append((lane.astype(jnp.float32) == turned[:, 8 + s : 9 + s] + 1.0).astype(jnp.float32))
    rows_ref[0:8, :] = source
    rows_ref[8:16, :] = slot
    rows_ref[16:24, :] = segment
    pick = jnp.concatenate(picks, axis=0).astype(jnp.bfloat16)
    from_source = iota((N_DP, GROUP), 0).astype(jnp.float32) == wide(source)
    column = (iota((1, GROUP), 1) // ROWS).astype(jnp.float32)
    low = jnp.where(from_source, wide(local_row) + 1.0, 0.0).astype(jnp.bfloat16)
    high = jnp.where(from_source, column, 0.0).astype(jnp.bfloat16)
    table = nn_dot(low, pick) + float(ROWS) * nn_dot(high, pick)
    request_ref[...] = table.astype(jnp.int32)
    most_ref[0, 0] = (jnp.max(slot) + 1.0).astype(jnp.int32)


def turned_requests(request_ref):
    blank = jnp.zeros((LANES - N_DP, LANES), jnp.float32)
    return jnp.concatenate([request_ref[...].astype(jnp.float32), blank], axis=0).T - 1.0


def group_picks(turned, group, first, capacity):
    column = jnp.concatenate(
        [turned[first : first + capacity, d : d + 1] for d in range(8 * group, 8 * group + 8)], axis=0
    )
    row_id = iota((8 * capacity, GROUP), 1).astype(jnp.float32)
    return (column == row_id).astype(jnp.float32).astype(jnp.bfloat16)


def join_columns(me_ref, parts, ext_ref, delta_ref):
    for m in range(N_SEQ):
        column = jnp.bitwise_xor(me_ref[0], m)
        whole = parts[m][...]
        ext_ref[pl.ds(pl.multiple_of(column * ROWS, ROWS), ROWS), :] = whole[:ROWS]
        if delta_ref is not None:
            delta_ref[column] = whole[ROWS:, :LANES].astype(jnp.float32)


def send_extra_kernel(me_ref, request_ref, *refs):
    parts, (sent_ref, ext_ref) = refs[:N_SEQ], refs[N_SEQ:]
    group_rows = 8 * EXTRA
    turned = turned_requests(request_ref)
    join_columns(me_ref, parts, ext_ref, None)
    for group in range(N_DP // 8):
        pick = group_picks(turned, group, CAPACITY, EXTRA)
        rows = slice(group * group_rows, (group + 1) * group_rows)
        sent_ref[rows, :] = nn_dot(pick, ext_ref[...]).astype(jnp.bfloat16)


def send_kernel(me_ref, most_ref, request_ref, *refs):
    parts, (small_ref, sent_ref, ext_ref, place_ref, delta_ref) = refs[:N_SEQ], refs[N_SEQ:]
    turned = turned_requests(request_ref)
    join_columns(me_ref, parts, ext_ref, delta_ref)

    @pl.when(most_ref[0, 0] < SMALL)
    def _():
        fill(SMALL, most_ref, turned, small_ref, ext_ref, place_ref, delta_ref)

    @pl.when(most_ref[0, 0] >= SMALL)
    def _():
        fill(CAPACITY, most_ref, turned, sent_ref, ext_ref, place_ref, delta_ref)


def fill(capacity, most_ref, turned, sent_ref, ext_ref, place_ref, delta_ref):
    group_rows = 8 * capacity
    delta = jnp.concatenate([delta_ref[s] for s in range(N_SEQ)], axis=1)

    def places(pick, group, first, count):
        index = iota((8, 8 * count), 1)
        owner = index // count
        value = jnp.where(
            iota((8, 8 * count), 0) == 0, owner + 8 * group, index - owner * count + first
        )
        return nn_dot(value.astype(jnp.float32).astype(jnp.bfloat16), pick)

    place = jnp.zeros((8, GROUP), jnp.float32)
    for group in range(N_DP // 8):
        pick = group_picks(turned, group, 0, capacity)
        place = place + places(pick, group, 0, capacity)
        rows = slice(group * group_rows, (group + 1) * group_rows)
        sent_ref[rows, :] = nn_dot(pick, ext_ref[...]).astype(jnp.bfloat16)
    place_ref[...] = place

    if capacity == CAPACITY:

        @pl.when(most_ref[0, 0] >= CAPACITY)
        def _():
            more = jnp.zeros((8, GROUP), jnp.float32)
            for group in range(N_DP // 8):
                more = more + places(
                    group_picks(turned, group, CAPACITY, EXTRA), group, CAPACITY, EXTRA
                )
            place_ref[...] += more

    place = place_ref[...]
    owner_of = place[0:1]
    slot_cols = []
    for s in range(N_SEQ):
        part = place[:, s * ROWS : (s + 1) * ROWS]
        blank = jnp.zeros((LANES - 8, LANES), jnp.float32)
        slot_cols.append(jnp.concatenate([part, blank], axis=0).T[:, 1:2])
    slot_col = jnp.concatenate(slot_cols, axis=0)
    lane = iota((GROUP, LANES), 1).astype(jnp.float32)
    to_owner = iota((N_DP, GROUP), 0).astype(jnp.float32) == owner_of
    tail = jnp.zeros((2 * N_DP, LANES), jnp.float32)
    for head in range(2):
        spread = jnp.concatenate(
            [jnp.where(to_owner, delta[c : c + 1], 0.0) for c in (head, 2 + head)], axis=0
        )
        slot_pick = (slot_col + (64.0 * head - 1.0) == lane).astype(jnp.float32)
        tail = tail + nn_dot(spread.astype(jnp.bfloat16), slot_pick.astype(jnp.bfloat16))
    tail = jnp.concatenate([tail[:N_DP], tail[N_DP:]], axis=1)
    row = iota((16, 2 * LANES), 0)
    for owner in range(N_DP):
        inside = owner * capacity % 16
        rows = slice(owner * capacity - inside, owner * capacity - inside + 16)
        kept = sent_ref[rows, : 2 * LANES].astype(jnp.float32)
        mine = jnp.broadcast_to(tail[owner : owner + 1], (16, 2 * LANES))
        sent_ref[rows, : 2 * LANES] = jnp.where(row == inside, mine, kept).astype(jnp.bfloat16)


def attend_kernel(
    segment_ref, most_ref, small_ref, arrived_ref, extra_ref, rows_ref, cols_ref, out_ref,
    x_ref, kt_ref, parts_ref, lanes_ref, weight_ref, squash_ref, total_ref, gqt_ref, gk_ref, gv_ref,
):
    blocks = GROUP // BLOCK

    def gather(capacity, from_ref):
        slots = N_DP * capacity
        slot_id = iota((BLOCK, slots), 1).astype(jnp.float32)
        for block in range(blocks):
            rows = slice(block * BLOCK, (block + 1) * BLOCK)
            slot = cols_ref[rows, 1:2] + 1.0
            place = jnp.where(slot < capacity, cols_ref[rows, 0:1] * float(capacity) + slot, -1.0)
            pick = (place == slot_id).astype(jnp.float32).astype(jnp.bfloat16)
            x_ref[rows, :] = nn_dot(pick, from_ref[...]).astype(jnp.bfloat16)
        first = iota((LANES, slots), 0) * capacity == iota((LANES, slots), 1)
        first = first.astype(jnp.float32).astype(jnp.bfloat16)
        parts_ref[...] = nn_dot(first, from_ref[:, : 2 * LANES])

    @pl.when(most_ref[0, 0] < SMALL)
    def _():
        gather(SMALL, small_ref)

    @pl.when(most_ref[0, 0] >= SMALL)
    def _():
        gather(CAPACITY, arrived_ref)

    @pl.when(most_ref[0, 0] >= CAPACITY)
    def _():
        extra_id = iota((BLOCK, N_DP * EXTRA), 1).astype(jnp.float32)
        for block in range(blocks):
            rows = slice(block * BLOCK, (block + 1) * BLOCK)
            slot = cols_ref[rows, 1:2] - float(CAPACITY - 1)
            place = jnp.where(slot >= 0.0, cols_ref[rows, 0:1] * float(EXTRA) + slot, -1.0)
            pick = (place == extra_id).astype(jnp.float32).astype(jnp.bfloat16)
            x_ref[rows, :] += nn_dot(pick, extra_ref[...]).astype(jnp.bfloat16)

    for block in range(blocks):
        rows = slice(block * BLOCK, (block + 1) * BLOCK)
        kt_ref[:, rows] = x_ref[rows, 256:384].astype(jnp.float32).T.astype(jnp.bfloat16)
    parts = parts_ref[...]
    source = wide(rows_ref[0:8, :])
    slot = wide(rows_ref[8:16, :])
    segment = wide(rows_ref[16:24, :])
    from_source = iota((LANES, GROUP), 0).astype(jnp.float32) == source
    from_source = from_source.astype(jnp.float32).astype(jnp.bfloat16)
    high = parts[:, :LANES].T.astype(jnp.bfloat16)
    low = parts[:, LANES:].T.astype(jnp.bfloat16)
    both = nn_dot(high, from_source) + nn_dot(low, from_source)
    place = iota((LANES, GROUP), 0).astype(jnp.float32)
    for head in range(2):
        lanes_ref[head : head + 1, :] = jnp.sum(
            jnp.where(place == slot + 64.0 * head, both, 0.0), axis=0, keepdims=True
        )
    gk_ref[...] = jnp.zeros_like(gk_ref)
    gv_ref[...] = jnp.zeros_like(gv_ref)

    for block in range(blocks):
        rows = slice(block * BLOCK, (block + 1) * BLOCK)
        near = slice(max(block - 1, 0) * BLOCK, (block + 1) * BLOCK)
        near_count = near.stop - near.start
        queries = jnp.concatenate([x_ref[rows, 0:128], x_ref[rows, 128:256]], axis=0)
        grads = jnp.concatenate([x_ref[rows, 512:640], x_ref[rows, 640:768]], axis=0)
        delta = jnp.concatenate([lanes_ref[0:1, rows], lanes_ref[1:2, rows]], axis=1)
        segment_q = jnp.concatenate([segment[:, rows]] * 2, axis=1)
        far = range(block - 1)

        def weigh(keys, causal):
            score = nt_dot(x_ref[keys, 256:384], queries)
            squashed = jnp.tanh(score * (scaling / softcap))
            allowed = cols_ref[keys, 2:3] == segment_q
            if causal is not None:
                allowed = allowed & causal
            return squashed, jnp.where(allowed, jnp.exp(softcap * squashed), 0.0)

        def back(keys, squashed, weights, inverse):
            probabilities = weights * inverse
            gv_ref[keys, :] += nn_dot(probabilities.astype(jnp.bfloat16), grads)
            prob_grad = nt_dot(x_ref[keys, 384:512], grads)
            score_grad = probabilities * (prob_grad - delta) * (1.0 - squashed * squashed)
            score_grad = score_grad.astype(jnp.bfloat16)
            gk_ref[keys, :] += nn_dot(score_grad, queries)
            return nn_dot(kt_ref[:, keys], score_grad)

        def reaches(key_block):
            return segment_ref[(key_block + 1) * BLOCK - 1] == segment_ref[block * BLOCK]

        if len(far) > 0:
            total_ref[...] = jnp.zeros_like(total_ref)
        for key_block in far:

            @pl.when(reaches(key_block))
            def _(keys=slice(key_block * BLOCK, (key_block + 1) * BLOCK)):
                squashed, weights = weigh(keys, None)
                weight_ref[keys, :] = weights
                squash_ref[keys, :] = squashed
                total_ref[0:1, :] += jnp.sum(weights, axis=0, keepdims=True)

        ahead = iota((near_count, BLOCK), 0) - iota((near_count, BLOCK), 1)
        causal = (ahead <= near_count - BLOCK).astype(jnp.float32)
        causal = jnp.concatenate([causal, causal], axis=1) > 0.0
        squashed, weights = weigh(near, causal)
        total = jnp.sum(weights, axis=0, keepdims=True)
        if len(far) > 0:
            total = total + total_ref[0:1, :]
        inverse = 1.0 / total
        gqt_ref[...] = back(near, squashed, weights, inverse)
        if len(far) > 0:
            total_ref[0:1, :] = inverse
        for key_block in far:

            @pl.when(reaches(key_block))
            def _(keys=slice(key_block * BLOCK, (key_block + 1) * BLOCK)):
                gqt_ref[...] += back(
                    keys, squash_ref[keys, :], weight_ref[keys, :], total_ref[0:1, :]
                )

        turned = (gqt_ref[...].T * scaling).astype(jnp.bfloat16)
        out_ref[rows, 0:128] = turned[:BLOCK]
        out_ref[rows, 128:256] = turned[BLOCK:]
    out_ref[:, 256:384] = (gk_ref[...] * scaling).astype(jnp.bfloat16)
    out_ref[:, 384:512] = gv_ref[...].astype(jnp.bfloat16)


def unpack_kernel(returned_ref, query_ref, key_ref, value_ref):
    for group in range(N_SEQ):
        two = slice(2 * group * HEAD_DIM, 2 * (group + 1) * HEAD_DIM)
        one = slice(group * HEAD_DIM, (group + 1) * HEAD_DIM)
        query_ref[:, two] = returned_ref[group, :, 0:256]
        key_ref[:, one] = returned_ref[group, :, 256:384]
        value_ref[:, one] = returned_ref[group, :, 384:512]


def shape(dims, dtype=jnp.bfloat16):
    return jax.ShapeDtypeStruct(dims, dtype)


VMEM = pl.BlockSpec(memory_space=pltpu.VMEM)
SMEM = pl.BlockSpec(memory_space=pltpu.SMEM)


def cost(flops, moved, transcendentals=0):
    return pl.CostEstimate(flops=flops, bytes_accessed=moved, transcendentals=transcendentals)


def pack(me, query, key_rows, value_rows, attn_out, out_grad):
    return pl.pallas_call(
        pack_kernel,
        out_shape=[shape((ROWS + 8, WIDTH))] * N_SEQ,
        in_specs=[SMEM] + [pl.BlockSpec(memory_space=pltpu.HBM)] * 5,
        out_specs=[VMEM] * N_SEQ,
        scratch_shapes=[
            pltpu.VMEM((ROWS, 2048), jnp.bfloat16),
            pltpu.VMEM((ROWS, 1024), jnp.bfloat16),
            pltpu.VMEM((ROWS, 1024), jnp.bfloat16),
            pltpu.VMEM((ROWS, 2048), jnp.bfloat16),
            pltpu.VMEM((ROWS, 2048), jnp.bfloat16),
            pltpu.VMEM((N_SEQ, 8, LANES), jnp.float32),
            pltpu.SemaphoreType.DMA((5,)),
        ],
        compiler_params=FULL,
        name="pack",
    )(me, query, key_rows, value_rows, attn_out, out_grad)


def index(me, segments, lists):
    return pl.pallas_call(
        index_kernel,
        out_shape=(
            shape((24, LANES), jnp.float32),
            shape((GROUP, LANES), jnp.float32),
            shape((N_DP, LANES), jnp.int32),
            shape((1, 1), jnp.int32),
        ),
        in_specs=[SMEM] + [VMEM] * 9,
        out_specs=(VMEM, VMEM, VMEM, SMEM),
        scratch_shapes=[pltpu.VMEM((N_SEQ, LANES), jnp.int32)],
        compiler_params=PARAMS,
        name="index",
    )(me, segments.reshape(N_SEQ, ROWS), *lists)


def send(me, most, request, parts):
    return pl.pallas_call(
        send_kernel,
        out_shape=[shape((N_DP * SMALL, WIDTH)), shape((N_DP * CAPACITY, WIDTH))],
        in_specs=[SMEM, SMEM] + [VMEM] * 9,
        out_specs=[VMEM, VMEM],
        scratch_shapes=[
            pltpu.VMEM((GROUP, WIDTH), jnp.bfloat16),
            pltpu.VMEM((8, GROUP), jnp.float32),
            pltpu.VMEM((N_SEQ, 8, LANES), jnp.float32),
        ],
        compiler_params=PARAMS,
        cost_estimate=cost(2 * N_DP * CAPACITY * GROUP * WIDTH, 4_000_000),
        name="send",
    )(me, most, request, *parts)


def send_extra(me, request, parts):
    return pl.pallas_call(
        send_extra_kernel,
        out_shape=shape((N_DP * EXTRA, WIDTH)),
        in_specs=[SMEM] + [VMEM] * 9,
        scratch_shapes=[pltpu.VMEM((GROUP, WIDTH), jnp.bfloat16)],
        compiler_params=PARAMS,
        name="send_extra",
    )(me, request, *parts)


def attend(segments, most, small, arrived, extra, rows, cols):
    return pl.pallas_call(
        attend_kernel,
        out_shape=shape((GROUP, 4 * HEAD_DIM)),
        in_specs=[SMEM, SMEM] + [VMEM] * 5,
        scratch_shapes=[
            pltpu.VMEM((GROUP, WIDTH), jnp.bfloat16),
            pltpu.VMEM((HEAD_DIM, GROUP), jnp.bfloat16),
            pltpu.VMEM((LANES, 2 * LANES), jnp.float32),
            pltpu.VMEM((8, GROUP), jnp.float32),
            pltpu.VMEM((GROUP - 2 * BLOCK, 2 * BLOCK), jnp.float32),
            pltpu.VMEM((GROUP - 2 * BLOCK, 2 * BLOCK), jnp.float32),
            pltpu.VMEM((8, 2 * BLOCK), jnp.float32),
            pltpu.VMEM((HEAD_DIM, 2 * BLOCK), jnp.float32),
            pltpu.VMEM((GROUP, HEAD_DIM), jnp.float32),
            pltpu.VMEM((GROUP, HEAD_DIM), jnp.float32),
        ],
        compiler_params=PARAMS,
        name="attend",
    )(segments, most, small, arrived, extra, rows, cols)


def unpack(returned):
    return pl.pallas_call(
        unpack_kernel,
        out_shape=(shape((ROWS, 2048)), shape((ROWS, 1024)), shape((ROWS, 1024))),
        compiler_params=PARAMS,
        name="unpack",
    )(returned)


def relay(array):
    return lax.all_to_all(array, "dp", split_axis=0, concat_axis=0, tiled=True)


def local(query, key_rows, value_rows, attn_out, out_grad, source_row, segment_ids):
    me = lax.axis_index("seq").reshape(1)

    def swap(array, m):
        return lax.ppermute(array, "seq", [(s, s ^ m) for s in range(N_SEQ)]) if m else array

    lists = [swap(source_row.reshape(1, ROWS), m) for m in range(N_SEQ)]
    packed = pack(me, query, key_rows, value_rows, attn_out, out_grad)
    packed, lists = lax.optimization_barrier((packed, lists))
    parts = [swap(packed[m], m) for m in range(N_SEQ)]
    rows, cols, request, most = index(me, segment_ids, lists)
    request, rows, cols, most, segment_ids = lax.optimization_barrier(
        (relay(request), rows, cols, most, segment_ids)
    )
    small, arrived = lax.cond(
        most[0, 0] < SMALL,
        lambda small, large: (relay(small), jnp.zeros_like(large)),
        lambda small, large: (jnp.zeros_like(small), relay(large)),
        *send(me, most, request, parts),
    )
    extra = lax.cond(
        most[0, 0] >= CAPACITY,
        lambda request, *parts: relay(send_extra(me, request, parts)),
        lambda request, *parts: jnp.zeros((N_DP * EXTRA, WIDTH), jnp.bfloat16),
        request,
        *parts,
    )
    grads = attend(segment_ids, most, small, arrived, extra, rows, cols)
    returned = lax.all_to_all(
        grads.reshape(N_SEQ, ROWS, 4 * HEAD_DIM), "seq", split_axis=0, concat_axis=0, tiled=True
    )
    return unpack(returned)


def solution(mesh):
    in_specs = (
        P(("dp", "seq"), None),
        P(("dp", "seq"), None),
        P(("dp", "seq"), None),
        P(("dp", "seq"), None),
        P(("dp", "seq"), None),
        P(("dp", "seq")),
        P("dp"),
    )
    out_specs = (P(("dp", "seq"), None), P(("dp", "seq"), None), P(("dp", "seq"), None))
    return jax.shard_map(local, mesh=mesh, in_specs=in_specs, out_specs=out_specs, check_vma=False)
```

```python
import functools

import jax
import jax.numpy as jnp
from jax import lax
from jax.experimental import pallas as pl
from jax.experimental.pallas import tpu as pltpu
from jax.sharding import PartitionSpec as P

HEAD_DIM = 128
N_DP = 32
N_SEQ = 8
ROWS = 128
GROUP = N_SEQ * ROWS
WIDTH = 6 * HEAD_DIM
LANES = 128
BLOCK = 256
SMALL = 48
CAPACITY = 56
EXTRA = 16

scaling = 1.0 / 12.0
softcap = 50.0

PARAMS = pltpu.CompilerParams(vmem_limit_bytes=20 * 1024 * 1024)
FULL = pltpu.CompilerParams(vmem_limit_bytes=60 * 1024 * 1024)


def iota(shape, dim):
    return lax.broadcasted_iota(jnp.int32, shape, dim)


def nt_dot(left, right):
    return lax.dot_general(left, right, (((1,), (1,)), ((), ())), preferred_element_type=jnp.float32)


def nn_dot(left, right):
    return jnp.dot(left, right, preferred_element_type=jnp.float32)


def pack_kernel(me_ref, query_hbm, key_hbm, value_hbm, out_hbm, grad_hbm, *refs):
    packed_refs = refs[:N_SEQ]
    query_ref, key_ref, value_ref, out_ref, grad_ref, delta_ref, sems = refs[N_SEQ:]
    pairs = (
        (grad_hbm, grad_ref),
        (out_hbm, out_ref),
        (query_hbm, query_ref),
        (key_hbm, key_ref),
        (value_hbm, value_ref),
    )
    copies = [
        pltpu.make_async_copy(source, target, sems.at[i])
        for i, (source, target) in enumerate(pairs)
    ]
    for copy in copies:
        copy.start()
    copies[0].wait()
    copies[1].wait()
    lane = iota((ROWS, LANES), 1)
    table = jnp.zeros((ROWS, LANES), jnp.float32)
    for head in range(2 * N_SEQ):
        cols = slice(head * HEAD_DIM, (head + 1) * HEAD_DIM)
        product = grad_ref[:, cols].astype(jnp.float32) * out_ref[:, cols].astype(jnp.float32)
        table = jnp.where(lane == head, jnp.sum(product, axis=1, keepdims=True), table)
    delta = table.T
    high = delta.astype(jnp.bfloat16).astype(jnp.float32)
    low = delta - high
    for group in range(N_SEQ):
        pair = slice(2 * group, 2 * group + 2)
        delta_ref[group] = jnp.concatenate(
            [high[pair], low[pair], jnp.zeros((4, LANES), jnp.float32)], axis=0
        )
    pad_cols = jnp.zeros((8, WIDTH - LANES), jnp.float32)
    for copy in copies[2:]:
        copy.wait()
    me = me_ref[0]
    for m in range(N_SEQ):
        group = jnp.bitwise_xor(me, m)
        two = pl.ds(pl.multiple_of(group * 256, 256), 256)
        one = pl.ds(pl.multiple_of(group * 128, 128), 128)
        rows = jnp.concatenate(
            [query_ref[:, two], key_ref[:, one], value_ref[:, one], grad_ref[:, two]], axis=1
        )
        extra = jnp.concatenate([delta_ref[group], pad_cols], axis=1)
        packed_refs[m][...] = jnp.concatenate([rows.astype(jnp.float32), extra], axis=0).astype(
            jnp.bfloat16
        )


def wide(rows):
    return jnp.concatenate([rows[s : s + 1] for s in range(N_SEQ)], axis=1)


def index_kernel(me_ref, *refs):
    lists, (rows_ref, cols_ref, request_ref, most_ref, list_ref) = refs[:N_SEQ], refs[N_SEQ:]
    for m in range(N_SEQ):
        list_ref[pl.ds(jnp.bitwise_xor(me_ref[0], m), 1), :] = lists[m][...]
    listed = list_ref[...]
    source = (listed // GROUP).astype(jnp.float32)
    local_row = (listed % ROWS).astype(jnp.float32)
    blank = jnp.zeros((LANES - 8, LANES), jnp.float32)
    source_cols = jnp.concatenate([source, blank], axis=0).T
    before = iota((ROWS, ROWS), 0) < iota((ROWS, ROWS), 1)
    slots = []
    for s in range(N_SEQ):
        mine = source[s : s + 1]
        hits = ((source_cols[:, s : s + 1] == mine) & before).astype(jnp.float32)
        for earlier in range(s):
            hits = hits + (source_cols[:, earlier : earlier + 1] == mine).astype(jnp.float32)
        slots.append(jnp.sum(hits, axis=0, keepdims=True))
    slot = jnp.concatenate(slots, axis=0)
    blank = jnp.zeros((LANES - 16, LANES), jnp.float32)
    turned = jnp.concatenate([source, slot, blank], axis=0).T
    lane = iota((ROWS, LANES), 1)
    picks = []
    for s in range(N_SEQ):
        columns = jnp.where(lane == 0, turned[:, s : s + 1], 0.0)
        columns = jnp.where(lane == 1, turned[:, 8 + s : 9 + s], columns)
        cols_ref[s * ROWS : (s + 1) * ROWS, :] = columns
        picks.append((lane.astype(jnp.float32) == turned[:, 8 + s : 9 + s] + 1.0).astype(jnp.float32))
    rows_ref[0:8, :] = source
    rows_ref[8:16, :] = slot
    pick = jnp.concatenate(picks, axis=0).astype(jnp.bfloat16)
    from_source = iota((N_DP, GROUP), 0).astype(jnp.float32) == wide(source)
    column = (iota((1, GROUP), 1) // ROWS).astype(jnp.float32)
    low = jnp.where(from_source, wide(local_row) + 1.0, 0.0).astype(jnp.bfloat16)
    high = jnp.where(from_source, column, 0.0).astype(jnp.bfloat16)
    table = nn_dot(low, pick) + float(ROWS) * nn_dot(high, pick)
    request_ref[...] = table.astype(jnp.int32)
    most_ref[0, 0] = (jnp.max(slot) + 1.0).astype(jnp.int32)


def turned_requests(request_ref):
    blank = jnp.zeros((LANES - N_DP, LANES), jnp.float32)
    return jnp.concatenate([request_ref[...].astype(jnp.float32), blank], axis=0).T - 1.0


def group_picks(turned, group, first, capacity):
    column = jnp.concatenate(
        [turned[first : first + capacity, d : d + 1] for d in range(8 * group, 8 * group + 8)], axis=0
    )
    row_id = iota((8 * capacity, GROUP), 1).astype(jnp.float32)
    return (column == row_id).astype(jnp.float32).astype(jnp.bfloat16)


def join_columns(me_ref, parts, ext_ref, delta_ref):
    for m in range(N_SEQ):
        column = jnp.bitwise_xor(me_ref[0], m)
        whole = parts[m][...]
        ext_ref[pl.ds(pl.multiple_of(column * ROWS, ROWS), ROWS), :] = whole[:ROWS]
        if delta_ref is not None:
            delta_ref[column] = whole[ROWS:, :LANES].astype(jnp.float32)


def send_extra_kernel(me_ref, request_ref, *refs):
    parts, (sent_ref, ext_ref) = refs[:N_SEQ], refs[N_SEQ:]
    group_rows = 8 * EXTRA
    turned = turned_requests(request_ref)
    join_columns(me_ref, parts, ext_ref, None)
    for group in range(N_DP // 8):
        pick = group_picks(turned, group, CAPACITY, EXTRA)
        rows = slice(group * group_rows, (group + 1) * group_rows)
        sent_ref[rows, :] = nn_dot(pick, ext_ref[...]).astype(jnp.bfloat16)


def send_kernel(me_ref, most_ref, request_ref, *refs):
    parts, (small_ref, sent_ref, ext_ref, place_ref, delta_ref) = refs[:N_SEQ], refs[N_SEQ:]
    turned = turned_requests(request_ref)
    join_columns(me_ref, parts, ext_ref, delta_ref)

    @pl.when(most_ref[0, 0] < SMALL)
    def _():
        fill(SMALL, most_ref, turned, small_ref, ext_ref, place_ref, delta_ref)

    @pl.when(most_ref[0, 0] >= SMALL)
    def _():
        fill(CAPACITY, most_ref, turned, sent_ref, ext_ref, place_ref, delta_ref)


def fill(capacity, most_ref, turned, sent_ref, ext_ref, place_ref, delta_ref):
    group_rows = 8 * capacity
    delta = jnp.concatenate([delta_ref[s] for s in range(N_SEQ)], axis=1)

    def places(pick, group, first, count):
        index = iota((8, 8 * count), 1)
        owner = index // count
        value = jnp.where(
            iota((8, 8 * count), 0) == 0, owner + 8 * group, index - owner * count + first
        )
        return nn_dot(value.astype(jnp.float32).astype(jnp.bfloat16), pick)

    place = jnp.zeros((8, GROUP), jnp.float32)
    for group in range(N_DP // 8):
        pick = group_picks(turned, group, 0, capacity)
        place = place + places(pick, group, 0, capacity)
        rows = slice(group * group_rows, (group + 1) * group_rows)
        sent_ref[rows, :] = nn_dot(pick, ext_ref[...]).astype(jnp.bfloat16)
    place_ref[...] = place

    if capacity == CAPACITY:

        @pl.when(most_ref[0, 0] >= CAPACITY)
        def _():
            more = jnp.zeros((8, GROUP), jnp.float32)
            for group in range(N_DP // 8):
                more = more + places(
                    group_picks(turned, group, CAPACITY, EXTRA), group, CAPACITY, EXTRA
                )
            place_ref[...] += more

    place = place_ref[...]
    owner_of = place[0:1]
    slot_cols = []
    for s in range(N_SEQ):
        part = place[:, s * ROWS : (s + 1) * ROWS]
        blank = jnp.zeros((LANES - 8, LANES), jnp.float32)
        slot_cols.append(jnp.concatenate([part, blank], axis=0).T[:, 1:2])
    slot_col = jnp.concatenate(slot_cols, axis=0)
    lane = iota((GROUP, LANES), 1).astype(jnp.float32)
    to_owner = iota((N_DP, GROUP), 0).astype(jnp.float32) == owner_of
    tail = jnp.zeros((2 * N_DP, LANES), jnp.float32)
    for head in range(2):
        spread = jnp.concatenate(
            [jnp.where(to_owner, delta[c : c + 1], 0.0) for c in (head, 2 + head)], axis=0
        )
        slot_pick = (slot_col + (64.0 * head - 1.0) == lane).astype(jnp.float32)
        tail = tail + nn_dot(spread.astype(jnp.bfloat16), slot_pick.astype(jnp.bfloat16))
    tail = jnp.concatenate([tail[:N_DP], tail[N_DP:]], axis=1)
    row = iota((16, 2 * LANES), 0)
    for owner in range(N_DP):
        inside = owner * capacity % 16
        rows = slice(owner * capacity - inside, owner * capacity - inside + 16)
        kept = sent_ref[rows, : 2 * LANES].astype(jnp.float32)
        mine = jnp.broadcast_to(tail[owner : owner + 1], (16, 2 * LANES))
        sent_ref[rows, : 2 * LANES] = jnp.where(row == inside, mine, kept).astype(jnp.bfloat16)


def attend_kernel(
    segment_ref, most_ref, arrived_ref, extra_hbm, marks_ref, rows_ref, cols_ref, out_ref,
    x_ref, kt_ref, extra_ref, lanes_ref, weight_ref, squash_ref, total_ref, gqt_ref, gk_ref, gv_ref, sem,
):
    slots = N_DP * CAPACITY
    blocks = GROUP // BLOCK
    most = most_ref[0, 0]
    capacity = jnp.where(most < SMALL, SMALL, CAPACITY)
    spread = capacity.astype(jnp.float32)

    def rows_of(block):
        return slice(block * BLOCK, (block + 1) * BLOCK)

    def gather(block):
        rows = rows_of(block)
        slot = cols_ref[rows, 1:2] + 1.0
        place = jnp.where(slot < spread, cols_ref[rows, 0:1] * spread + slot, -1.0)
        pick = place == iota((BLOCK, slots), 1).astype(jnp.float32)
        pick = pick.astype(jnp.float32).astype(jnp.bfloat16)
        x_ref[rows, :] = nn_dot(pick, arrived_ref[...]).astype(jnp.bfloat16)

    def add_extra(block):
        @pl.when(most >= CAPACITY)
        def _():
            copy = pltpu.make_async_copy(extra_hbm, extra_ref, sem)
            copy.start()
            copy.wait()
            rows = rows_of(block)
            slot = cols_ref[rows, 1:2] - float(CAPACITY - 1)
            place = jnp.where(slot >= 0.0, cols_ref[rows, 0:1] * float(EXTRA) + slot, -1.0)
            pick = place == iota((BLOCK, N_DP * EXTRA), 1).astype(jnp.float32)
            pick = pick.astype(jnp.float32).astype(jnp.bfloat16)
            x_ref[rows, :] += nn_dot(pick, extra_ref[...]).astype(jnp.bfloat16)

    gather(0)
    first = iota((LANES, slots), 0) * capacity == iota((LANES, slots), 1)
    first = first.astype(jnp.float32).astype(jnp.bfloat16)
    parts = nn_dot(first, arrived_ref[:, : 2 * LANES])
    source = wide(rows_ref[0:8, :])
    slot = wide(rows_ref[8:16, :])
    from_source = iota((LANES, GROUP), 0).astype(jnp.float32) == source
    from_source = from_source.astype(jnp.float32).astype(jnp.bfloat16)
    high = parts[:, :LANES].T.astype(jnp.bfloat16)
    low = parts[:, LANES:].T.astype(jnp.bfloat16)
    both = nn_dot(high, from_source) + nn_dot(low, from_source)
    place = iota((LANES, GROUP), 0).astype(jnp.float32)
    for head in range(2):
        lanes_ref[head : head + 1, :] = jnp.sum(
            jnp.where(place == slot + 64.0 * head, both, 0.0), axis=0, keepdims=True
        )
    gk_ref[...] = jnp.zeros_like(gk_ref)
    gv_ref[...] = jnp.zeros_like(gv_ref)
    marks = marks_ref[...].astype(jnp.float32)
    segment = wide(marks)
    mark_cols = jnp.concatenate([marks, jnp.zeros((LANES - 8, LANES), jnp.float32)], axis=0).T
    add_extra(0)

    for block in range(blocks):
        rows = rows_of(block)
        near = slice(max(block - 1, 0) * BLOCK, (block + 1) * BLOCK)
        near_count = near.stop - near.start
        kt_ref[:, rows] = x_ref[rows, 256:384].astype(jnp.float32).T.astype(jnp.bfloat16)
        queries = jnp.concatenate([x_ref[rows, 0:128], x_ref[rows, 128:256]], axis=0)
        grads = jnp.concatenate([x_ref[rows, 512:640], x_ref[rows, 640:768]], axis=0)
        delta = jnp.concatenate([lanes_ref[0:1, rows], lanes_ref[1:2, rows]], axis=1)
        segment_q = jnp.concatenate([segment[:, rows]] * 2, axis=1)
        far = range(block - 1)

        def weigh(keys, causal):
            score = nt_dot(x_ref[keys, 256:384], queries)
            squashed = jnp.tanh(score * (scaling / softcap))
            columns = range(keys.start // ROWS, keys.stop // ROWS)
            segment_k = jnp.concatenate([mark_cols[:, s : s + 1] for s in columns], axis=0)
            allowed = segment_k == segment_q
            if causal is not None:
                allowed = allowed & causal
            return squashed, jnp.where(allowed, jnp.exp(softcap * squashed), 0.0)

        def back(keys, squashed, weights, inverse):
            probabilities = weights * inverse
            gv_ref[keys, :] += nn_dot(probabilities.astype(jnp.bfloat16), grads)
            prob_grad = nt_dot(x_ref[keys, 384:512], grads)
            score_grad = probabilities * (prob_grad - delta) * (1.0 - squashed * squashed)
            score_grad = score_grad.astype(jnp.bfloat16)
            gk_ref[keys, :] += nn_dot(score_grad, queries)
            return nn_dot(kt_ref[:, keys], score_grad)

        def reaches(key_block):
            return segment_ref[(key_block + 1) * BLOCK - 1] == segment_ref[block * BLOCK]

        if len(far) > 0:
            total_ref[...] = jnp.zeros_like(total_ref)
        for key_block in far:

            @pl.when(reaches(key_block))
            def _(keys=rows_of(key_block)):
                squashed, weights = weigh(keys, None)
                weight_ref[keys, :] = weights
                squash_ref[keys, :] = squashed
                total_ref[0:1, :] += jnp.sum(weights, axis=0, keepdims=True)

        ahead = iota((near_count, BLOCK), 0) - iota((near_count, BLOCK), 1)
        causal = (ahead <= near_count - BLOCK).astype(jnp.float32)
        causal = jnp.concatenate([causal, causal], axis=1) > 0.0
        squashed, weights = weigh(near, causal)
        total = jnp.sum(weights, axis=0, keepdims=True)
        if len(far) > 0:
            total = total + total_ref[0:1, :]
        inverse = 1.0 / total
        gqt_ref[...] = back(near, squashed, weights, inverse)
        if block + 1 < blocks:
            gather(block + 1)
        if len(far) > 0:
            total_ref[0:1, :] = inverse
        for key_block in far:

            @pl.when(reaches(key_block))
            def _(keys=rows_of(key_block)):
                gqt_ref[...] += back(
                    keys, squash_ref[keys, :], weight_ref[keys, :], total_ref[0:1, :]
                )

        turned = (gqt_ref[...].T * scaling).astype(jnp.bfloat16)
        out_ref[rows, 0:128] = turned[:BLOCK]
        out_ref[rows, 128:256] = turned[BLOCK:]
        if block + 1 < blocks:
            add_extra(block + 1)
    out_ref[:, 256:384] = (gk_ref[...] * scaling).astype(jnp.bfloat16)
    out_ref[:, 384:512] = gv_ref[...].astype(jnp.bfloat16)


def unpack_kernel(returned_ref, query_ref, key_ref, value_ref):
    for group in range(N_SEQ):
        two = slice(2 * group * HEAD_DIM, 2 * (group + 1) * HEAD_DIM)
        one = slice(group * HEAD_DIM, (group + 1) * HEAD_DIM)
        query_ref[:, two] = returned_ref[group, :, 0:256]
        key_ref[:, one] = returned_ref[group, :, 256:384]
        value_ref[:, one] = returned_ref[group, :, 384:512]


def shape(dims, dtype=jnp.bfloat16):
    return jax.ShapeDtypeStruct(dims, dtype)


VMEM = pl.BlockSpec(memory_space=pltpu.VMEM)
SMEM = pl.BlockSpec(memory_space=pltpu.SMEM)


def cost(flops, moved, transcendentals=0):
    return pl.CostEstimate(flops=flops, bytes_accessed=moved, transcendentals=transcendentals)


def pack(me, query, key_rows, value_rows, attn_out, out_grad):
    return pl.pallas_call(
        pack_kernel,
        out_shape=[shape((ROWS + 8, WIDTH))] * N_SEQ,
        in_specs=[SMEM] + [pl.BlockSpec(memory_space=pltpu.HBM)] * 5,
        out_specs=[VMEM] * N_SEQ,
        scratch_shapes=[
            pltpu.VMEM((ROWS, 2048), jnp.bfloat16),
            pltpu.VMEM((ROWS, 1024), jnp.bfloat16),
            pltpu.VMEM((ROWS, 1024), jnp.bfloat16),
            pltpu.VMEM((ROWS, 2048), jnp.bfloat16),
            pltpu.VMEM((ROWS, 2048), jnp.bfloat16),
            pltpu.VMEM((N_SEQ, 8, LANES), jnp.float32),
            pltpu.SemaphoreType.DMA((5,)),
        ],
        compiler_params=FULL,
        name="pack",
    )(me, query, key_rows, value_rows, attn_out, out_grad)


def index(me, lists):
    return pl.pallas_call(
        index_kernel,
        out_shape=(
            shape((16, LANES), jnp.float32),
            shape((GROUP, LANES), jnp.float32),
            shape((N_DP, LANES), jnp.int32),
            shape((1, 1), jnp.int32),
        ),
        in_specs=[SMEM] + [VMEM] * 8,
        out_specs=(VMEM, VMEM, VMEM, SMEM),
        scratch_shapes=[pltpu.VMEM((N_SEQ, LANES), jnp.int32)],
        compiler_params=PARAMS,
        name="index",
    )(me, *lists)


def send(me, most, request, parts):
    return pl.pallas_call(
        send_kernel,
        out_shape=[shape((N_DP * SMALL, WIDTH)), shape((N_DP * CAPACITY, WIDTH))],
        in_specs=[SMEM, SMEM] + [VMEM] * 9,
        out_specs=[VMEM, VMEM],
        scratch_shapes=[
            pltpu.VMEM((GROUP, WIDTH), jnp.bfloat16),
            pltpu.VMEM((8, GROUP), jnp.float32),
            pltpu.VMEM((N_SEQ, 8, LANES), jnp.float32),
        ],
        compiler_params=PARAMS,
        cost_estimate=cost(2 * N_DP * CAPACITY * GROUP * WIDTH, 4_000_000),
        name="send",
    )(me, most, request, *parts)


def send_extra(me, request, parts):
    return pl.pallas_call(
        send_extra_kernel,
        out_shape=shape((N_DP * EXTRA, WIDTH)),
        in_specs=[SMEM] + [VMEM] * 9,
        scratch_shapes=[pltpu.VMEM((GROUP, WIDTH), jnp.bfloat16)],
        compiler_params=PARAMS,
        name="send_extra",
    )(me, request, *parts)


def attend(segments, most, arrived, extra, rows, cols):
    return pl.pallas_call(
        attend_kernel,
        out_shape=shape((GROUP, 4 * HEAD_DIM)),
        in_specs=[SMEM, SMEM, VMEM, pl.BlockSpec(memory_space=pltpu.HBM), VMEM, VMEM, VMEM],
        scratch_shapes=[
            pltpu.VMEM((GROUP, WIDTH), jnp.bfloat16),
            pltpu.VMEM((HEAD_DIM, GROUP), jnp.bfloat16),
            pltpu.VMEM((N_DP * EXTRA, WIDTH), jnp.bfloat16),
            pltpu.VMEM((8, GROUP), jnp.float32),
            pltpu.VMEM((GROUP - 2 * BLOCK, 2 * BLOCK), jnp.float32),
            pltpu.VMEM((GROUP - 2 * BLOCK, 2 * BLOCK), jnp.float32),
            pltpu.VMEM((8, 2 * BLOCK), jnp.float32),
            pltpu.VMEM((HEAD_DIM, 2 * BLOCK), jnp.float32),
            pltpu.VMEM((GROUP, HEAD_DIM), jnp.float32),
            pltpu.VMEM((GROUP, HEAD_DIM), jnp.float32),
            pltpu.SemaphoreType.DMA,
        ],
        compiler_params=PARAMS,
        name="attend",
    )(segments, most, arrived, extra, segments.reshape(N_SEQ, ROWS), rows, cols)


def unpack(returned):
    return pl.pallas_call(
        unpack_kernel,
        out_shape=(shape((ROWS, 2048)), shape((ROWS, 1024)), shape((ROWS, 1024))),
        compiler_params=PARAMS,
        name="unpack",
    )(returned)


def relay(array):
    return lax.all_to_all(array, "dp", split_axis=0, concat_axis=0, tiled=True)


def local(query, key_rows, value_rows, attn_out, out_grad, source_row, segment_ids):
    me = lax.axis_index("seq").reshape(1)

    def swap(array, m):
        return lax.ppermute(array, "seq", [(s, s ^ m) for s in range(N_SEQ)]) if m else array

    lists = [swap(source_row.reshape(1, ROWS), m) for m in range(N_SEQ)]
    packed = pack(me, query, key_rows, value_rows, attn_out, out_grad)
    packed, lists = lax.optimization_barrier((packed, lists))
    parts = [swap(packed[m], m) for m in range(N_SEQ)]
    rows, cols, request, most = index(me, lists)
    request, rows, cols, most = lax.optimization_barrier((relay(request), rows, cols, most))
    pad = N_DP * (CAPACITY - SMALL)
    arrived = lax.cond(
        most[0, 0] < SMALL,
        lambda small, large: jnp.pad(relay(small), ((0, pad), (0, 0))),
        lambda small, large: relay(large),
        *send(me, most, request, parts),
    )
    extra = lax.cond(
        most[0, 0] >= CAPACITY,
        lambda request, *parts: relay(send_extra(me, request, parts)),
        lambda request, *parts: jnp.zeros((N_DP * EXTRA, WIDTH), jnp.bfloat16),
        request,
        *parts,
    )
    grads = attend(segment_ids, most, arrived, extra, rows, cols)
    returned = lax.all_to_all(
        grads.reshape(N_SEQ, ROWS, 4 * HEAD_DIM), "seq", split_axis=0, concat_axis=0, tiled=True
    )
    return unpack(returned)


def solution(mesh):
    in_specs = (
        P(("dp", "seq"), None),
        P(("dp", "seq"), None),
        P(("dp", "seq"), None),
        P(("dp", "seq"), None),
        P(("dp", "seq"), None),
        P(("dp", "seq")),
        P("dp"),
    )
    out_specs = (P(("dp", "seq"), None), P(("dp", "seq"), None), P(("dp", "seq"), None))
    return jax.shard_map(local, mesh=mesh, in_specs=in_specs, out_specs=out_specs, check_vma=False)
```

```python
import functools

import jax
import jax.numpy as jnp
from jax import lax
from jax.experimental import pallas as pl
from jax.experimental.pallas import tpu as pltpu
from jax.sharding import PartitionSpec as P

HEAD_DIM = 128
N_DP = 32
N_SEQ = 8
N_Y = 4
ROWS = 128
GROUP = N_SEQ * ROWS
WIDTH = 6 * HEAD_DIM
LANES = 128
BLOCK = 256
SMALL = 48
CAPACITY = 56
EXTRA = 16

scaling = 1.0 / 12.0
softcap = 50.0

PARAMS = pltpu.CompilerParams(vmem_limit_bytes=20 * 1024 * 1024)
FULL = pltpu.CompilerParams(vmem_limit_bytes=60 * 1024 * 1024)


def iota(shape, dim):
    return lax.broadcasted_iota(jnp.int32, shape, dim)


def nt_dot(left, right):
    return lax.dot_general(left, right, (((1,), (1,)), ((), ())), preferred_element_type=jnp.float32)


def nn_dot(left, right):
    return jnp.dot(left, right, preferred_element_type=jnp.float32)


def pack_kernel(me_ref, query_hbm, key_hbm, value_hbm, out_hbm, grad_hbm, *refs):
    packed_refs = refs[:N_SEQ]
    query_ref, key_ref, value_ref, out_ref, grad_ref, delta_ref, sems = refs[N_SEQ:]
    pairs = (
        (grad_hbm, grad_ref),
        (out_hbm, out_ref),
        (query_hbm, query_ref),
        (key_hbm, key_ref),
        (value_hbm, value_ref),
    )
    copies = [
        pltpu.make_async_copy(source, target, sems.at[i])
        for i, (source, target) in enumerate(pairs)
    ]
    for copy in copies:
        copy.start()
    copies[0].wait()
    copies[1].wait()
    lane = iota((ROWS, LANES), 1)
    table = jnp.zeros((ROWS, LANES), jnp.float32)
    for head in range(2 * N_SEQ):
        cols = slice(head * HEAD_DIM, (head + 1) * HEAD_DIM)
        product = grad_ref[:, cols].astype(jnp.float32) * out_ref[:, cols].astype(jnp.float32)
        table = jnp.where(lane == head, jnp.sum(product, axis=1, keepdims=True), table)
    delta = table.T
    high = delta.astype(jnp.bfloat16).astype(jnp.float32)
    low = delta - high
    for group in range(N_SEQ):
        pair = slice(2 * group, 2 * group + 2)
        delta_ref[group] = jnp.concatenate(
            [high[pair], low[pair], jnp.zeros((4, LANES), jnp.float32)], axis=0
        )
    pad_cols = jnp.zeros((8, WIDTH - LANES), jnp.float32)
    for copy in copies[2:]:
        copy.wait()
    me = me_ref[0]
    for m in range(N_SEQ):
        group = jnp.bitwise_xor(me, m)
        two = pl.ds(pl.multiple_of(group * 256, 256), 256)
        one = pl.ds(pl.multiple_of(group * 128, 128), 128)
        rows = jnp.concatenate(
            [query_ref[:, two], key_ref[:, one], value_ref[:, one], grad_ref[:, two]], axis=1
        )
        extra = jnp.concatenate([delta_ref[group], pad_cols], axis=1)
        packed_refs[m][...] = jnp.concatenate([rows.astype(jnp.float32), extra], axis=0).astype(
            jnp.bfloat16
        )


def wide(rows):
    return jnp.concatenate([rows[s : s + 1] for s in range(N_SEQ)], axis=1)


def index_kernel(me_ref, *refs):
    lists, (rows_ref, cols_ref, request_ref, most_ref, list_ref) = refs[:N_Y], refs[N_Y:]
    for m in range(N_SEQ):
        part = lists[m // 2][m % 2 : m % 2 + 1, :]
        list_ref[pl.ds(jnp.bitwise_xor(me_ref[0], m), 1), :] = part
    listed = list_ref[...]
    source = (listed // GROUP).astype(jnp.float32)
    local_row = (listed % ROWS).astype(jnp.float32)
    blank = jnp.zeros((LANES - 8, LANES), jnp.float32)
    source_cols = jnp.concatenate([source, blank], axis=0).T
    before = iota((ROWS, ROWS), 0) < iota((ROWS, ROWS), 1)
    slots = []
    for s in range(N_SEQ):
        mine = source[s : s + 1]
        hits = ((source_cols[:, s : s + 1] == mine) & before).astype(jnp.float32)
        for earlier in range(s):
            hits = hits + (source_cols[:, earlier : earlier + 1] == mine).astype(jnp.float32)
        slots.append(jnp.sum(hits, axis=0, keepdims=True))
    slot = jnp.concatenate(slots, axis=0)
    blank = jnp.zeros((LANES - 16, LANES), jnp.float32)
    turned = jnp.concatenate([source, slot, blank], axis=0).T
    lane = iota((ROWS, LANES), 1)
    picks = []
    for s in range(N_SEQ):
        columns = jnp.where(lane == 0, turned[:, s : s + 1], 0.0)
        columns = jnp.where(lane == 1, turned[:, 8 + s : 9 + s], columns)
        cols_ref[s * ROWS : (s + 1) * ROWS, :] = columns
        picks.append((lane.astype(jnp.float32) == turned[:, 8 + s : 9 + s] + 1.0).astype(jnp.float32))
    rows_ref[0:8, :] = source
    rows_ref[8:16, :] = slot
    pick = jnp.concatenate(picks, axis=0).astype(jnp.bfloat16)
    from_source = iota((N_DP, GROUP), 0).astype(jnp.float32) == wide(source)
    column = (iota((1, GROUP), 1) // ROWS).astype(jnp.float32)
    low = jnp.where(from_source, wide(local_row) + 1.0, 0.0).astype(jnp.bfloat16)
    high = jnp.where(from_source, column, 0.0).astype(jnp.bfloat16)
    table = nn_dot(low, pick) + float(ROWS) * nn_dot(high, pick)
    request_ref[...] = table.astype(jnp.int32)
    most_ref[0, 0] = (jnp.max(slot) + 1.0).astype(jnp.int32)


def turned_requests(request_ref):
    blank = jnp.zeros((LANES - N_DP, LANES), jnp.float32)
    return jnp.concatenate([request_ref[...].astype(jnp.float32), blank], axis=0).T - 1.0


def group_picks(turned, group, first, capacity):
    column = jnp.concatenate(
        [turned[first : first + capacity, d : d + 1] for d in range(8 * group, 8 * group + 8)], axis=0
    )
    row_id = iota((8 * capacity, GROUP), 1).astype(jnp.float32)
    return (column == row_id).astype(jnp.float32).astype(jnp.bfloat16)


def join_columns(me_ref, parts, ext_ref, delta_ref):
    for m in range(N_SEQ):
        column = jnp.bitwise_xor(me_ref[0], m)
        whole = parts[m][...]
        ext_ref[pl.ds(pl.multiple_of(column * ROWS, ROWS), ROWS), :] = whole[:ROWS]
        if delta_ref is not None:
            delta_ref[column] = whole[ROWS:, :LANES].astype(jnp.float32)


def send_extra_kernel(me_ref, request_ref, *refs):
    parts, (sent_ref, ext_ref) = refs[:N_SEQ], refs[N_SEQ:]
    group_rows = 8 * EXTRA
    turned = turned_requests(request_ref)
    join_columns(me_ref, parts, ext_ref, None)
    for group in range(N_DP // 8):
        pick = group_picks(turned, group, CAPACITY, EXTRA)
        rows = slice(group * group_rows, (group + 1) * group_rows)
        sent_ref[rows, :] = nn_dot(pick, ext_ref[...]).astype(jnp.bfloat16)


def send_kernel(me_ref, most_ref, request_ref, *refs):
    parts, (small_ref, sent_ref, ext_ref, place_ref, delta_ref) = refs[:N_SEQ], refs[N_SEQ:]
    turned = turned_requests(request_ref)
    join_columns(me_ref, parts, ext_ref, delta_ref)

    @pl.when(most_ref[0, 0] < SMALL)
    def _():
        fill(SMALL, most_ref, turned, small_ref, ext_ref, place_ref, delta_ref)

    @pl.when(most_ref[0, 0] >= SMALL)
    def _():
        fill(CAPACITY, most_ref, turned, sent_ref, ext_ref, place_ref, delta_ref)


def fill(capacity, most_ref, turned, sent_ref, ext_ref, place_ref, delta_ref):
    group_rows = 8 * capacity
    delta = jnp.concatenate([delta_ref[s] for s in range(N_SEQ)], axis=1)

    def places(pick, group, first, count):
        index = iota((8, 8 * count), 1)
        owner = index // count
        value = jnp.where(
            iota((8, 8 * count), 0) == 0, owner + 8 * group, index - owner * count + first
        )
        return nn_dot(value.astype(jnp.float32).astype(jnp.bfloat16), pick)

    place = jnp.zeros((8, GROUP), jnp.float32)
    for group in range(N_DP // 8):
        pick = group_picks(turned, group, 0, capacity)
        place = place + places(pick, group, 0, capacity)
        rows = slice(group * group_rows, (group + 1) * group_rows)
        sent_ref[rows, :] = nn_dot(pick, ext_ref[...]).astype(jnp.bfloat16)
    place_ref[...] = place

    if capacity == CAPACITY:

        @pl.when(most_ref[0, 0] >= CAPACITY)
        def _():
            more = jnp.zeros((8, GROUP), jnp.float32)
            for group in range(N_DP // 8):
                more = more + places(
                    group_picks(turned, group, CAPACITY, EXTRA), group, CAPACITY, EXTRA
                )
            place_ref[...] += more

    place = place_ref[...]
    owner_of = place[0:1]
    slot_cols = []
    for s in range(N_SEQ):
        part = place[:, s * ROWS : (s + 1) * ROWS]
        blank = jnp.zeros((LANES - 8, LANES), jnp.float32)
        slot_cols.append(jnp.concatenate([part, blank], axis=0).T[:, 1:2])
    slot_col = jnp.concatenate(slot_cols, axis=0)
    lane = iota((GROUP, LANES), 1).astype(jnp.float32)
    to_owner = iota((N_DP, GROUP), 0).astype(jnp.float32) == owner_of
    tail = jnp.zeros((2 * N_DP, LANES), jnp.float32)
    for head in range(2):
        spread = jnp.concatenate(
            [jnp.where(to_owner, delta[c : c + 1], 0.0) for c in (head, 2 + head)], axis=0
        )
        slot_pick = (slot_col + (64.0 * head - 1.0) == lane).astype(jnp.float32)
        tail = tail + nn_dot(spread.astype(jnp.bfloat16), slot_pick.astype(jnp.bfloat16))
    tail = jnp.concatenate([tail[:N_DP], tail[N_DP:]], axis=1)
    row = iota((16, 2 * LANES), 0)
    for owner in range(N_DP):
        inside = owner * capacity % 16
        rows = slice(owner * capacity - inside, owner * capacity - inside + 16)
        kept = sent_ref[rows, : 2 * LANES].astype(jnp.float32)
        mine = jnp.broadcast_to(tail[owner : owner + 1], (16, 2 * LANES))
        sent_ref[rows, : 2 * LANES] = jnp.where(row == inside, mine, kept).astype(jnp.bfloat16)


def attend_kernel(
    segment_ref, most_ref, arrived_ref, extra_hbm, marks_ref, rows_ref, cols_ref, out_ref,
    x_ref, kt_ref, extra_ref, lanes_ref, weight_ref, squash_ref, total_ref, gqt_ref, gk_ref, gv_ref, sem,
):
    slots = N_DP * CAPACITY
    blocks = GROUP // BLOCK
    most = most_ref[0, 0]
    capacity = jnp.where(most < SMALL, SMALL, CAPACITY)
    spread = capacity.astype(jnp.float32)

    def rows_of(block):
        return slice(block * BLOCK, (block + 1) * BLOCK)

    def gather(block):
        rows = rows_of(block)
        slot = cols_ref[rows, 1:2] + 1.0
        place = jnp.where(slot < spread, cols_ref[rows, 0:1] * spread + slot, -1.0)
        pick = place == iota((BLOCK, slots), 1).astype(jnp.float32)
        pick = pick.astype(jnp.float32).astype(jnp.bfloat16)
        x_ref[rows, :] = nn_dot(pick, arrived_ref[...]).astype(jnp.bfloat16)

    for block in range(blocks):
        gather(block)

    @pl.when(most >= CAPACITY)
    def _():
        copy = pltpu.make_async_copy(extra_hbm, extra_ref, sem)
        copy.start()
        copy.wait()
        for block in range(blocks):
            rows = rows_of(block)
            slot = cols_ref[rows, 1:2] - float(CAPACITY - 1)
            place = jnp.where(slot >= 0.0, cols_ref[rows, 0:1] * float(EXTRA) + slot, -1.0)
            pick = place == iota((BLOCK, N_DP * EXTRA), 1).astype(jnp.float32)
            pick = pick.astype(jnp.float32).astype(jnp.bfloat16)
            x_ref[rows, :] += nn_dot(pick, extra_ref[...]).astype(jnp.bfloat16)

    for block in range(blocks):
        rows = rows_of(block)
        kt_ref[:, rows] = x_ref[rows, 256:384].astype(jnp.float32).T.astype(jnp.bfloat16)
    first = iota((LANES, slots), 0) * capacity == iota((LANES, slots), 1)
    first = first.astype(jnp.float32).astype(jnp.bfloat16)
    parts = nn_dot(first, arrived_ref[:, : 2 * LANES])
    source = wide(rows_ref[0:8, :])
    slot = wide(rows_ref[8:16, :])
    from_source = iota((LANES, GROUP), 0).astype(jnp.float32) == source
    from_source = from_source.astype(jnp.float32).astype(jnp.bfloat16)
    high = parts[:, :LANES].T.astype(jnp.bfloat16)
    low = parts[:, LANES:].T.astype(jnp.bfloat16)
    both = nn_dot(high, from_source) + nn_dot(low, from_source)
    place = iota((LANES, GROUP), 0).astype(jnp.float32)
    for head in range(2):
        lanes_ref[head : head + 1, :] = jnp.sum(
            jnp.where(place == slot + 64.0 * head, both, 0.0), axis=0, keepdims=True
        )
    gk_ref[...] = jnp.zeros_like(gk_ref)
    gv_ref[...] = jnp.zeros_like(gv_ref)
    marks = marks_ref[...].astype(jnp.float32)
    segment = wide(marks)
    mark_cols = jnp.concatenate([marks, jnp.zeros((LANES - 8, LANES), jnp.float32)], axis=0).T

    for block in range(blocks):
        rows = rows_of(block)
        near = slice(max(block - 1, 0) * BLOCK, (block + 1) * BLOCK)
        near_count = near.stop - near.start
        queries = jnp.concatenate([x_ref[rows, 0:128], x_ref[rows, 128:256]], axis=0)
        grads = jnp.concatenate([x_ref[rows, 512:640], x_ref[rows, 640:768]], axis=0)
        delta = jnp.concatenate([lanes_ref[0:1, rows], lanes_ref[1:2, rows]], axis=1)
        segment_q = jnp.concatenate([segment[:, rows]] * 2, axis=1)
        far = range(block - 1)

        def weigh(keys, causal):
            score = nt_dot(x_ref[keys, 256:384], queries)
            squashed = jnp.tanh(score * (scaling / softcap))
            columns = range(keys.start // ROWS, keys.stop // ROWS)
            segment_k = jnp.concatenate([mark_cols[:, s : s + 1] for s in columns], axis=0)
            allowed = segment_k == segment_q
            if causal is not None:
                allowed = allowed & causal
            return squashed, jnp.where(allowed, jnp.exp(softcap * squashed), 0.0)

        def back(keys, squashed, weights, inverse):
            probabilities = weights * inverse
            gv_ref[keys, :] += nn_dot(probabilities.astype(jnp.bfloat16), grads)
            prob_grad = nt_dot(x_ref[keys, 384:512], grads)
            score_grad = probabilities * (prob_grad - delta) * (1.0 - squashed * squashed)
            score_grad = score_grad.astype(jnp.bfloat16)
            gk_ref[keys, :] += nn_dot(score_grad, queries)
            return nn_dot(kt_ref[:, keys], score_grad)

        def reaches(key_block):
            return segment_ref[(key_block + 1) * BLOCK - 1] == segment_ref[block * BLOCK]

        if len(far) > 0:
            total_ref[...] = jnp.zeros_like(total_ref)
        for key_block in far:

            @pl.when(reaches(key_block))
            def _(keys=rows_of(key_block)):
                squashed, weights = weigh(keys, None)
                weight_ref[keys, :] = weights
                squash_ref[keys, :] = squashed
                total_ref[0:1, :] += jnp.sum(weights, axis=0, keepdims=True)

        ahead = iota((near_count, BLOCK), 0) - iota((near_count, BLOCK), 1)
        causal = (ahead <= near_count - BLOCK).astype(jnp.float32)
        causal = jnp.concatenate([causal, causal], axis=1) > 0.0
        squashed, weights = weigh(near, causal)
        total = jnp.sum(weights, axis=0, keepdims=True)
        if len(far) > 0:
            total = total + total_ref[0:1, :]
        inverse = 1.0 / total
        gqt_ref[...] = back(near, squashed, weights, inverse)
        if len(far) > 0:
            total_ref[0:1, :] = inverse
        for key_block in far:

            @pl.when(reaches(key_block))
            def _(keys=rows_of(key_block)):
                gqt_ref[...] += back(
                    keys, squash_ref[keys, :], weight_ref[keys, :], total_ref[0:1, :]
                )

        turned = (gqt_ref[...].T * scaling).astype(jnp.bfloat16)
        out_ref[rows, 0:128] = turned[:BLOCK]
        out_ref[rows, 128:256] = turned[BLOCK:]
    out_ref[:, 256:384] = (gk_ref[...] * scaling).astype(jnp.bfloat16)
    out_ref[:, 384:512] = gv_ref[...].astype(jnp.bfloat16)


def unpack_kernel(returned_ref, query_ref, key_ref, value_ref):
    for group in range(N_SEQ):
        two = slice(2 * group * HEAD_DIM, 2 * (group + 1) * HEAD_DIM)
        one = slice(group * HEAD_DIM, (group + 1) * HEAD_DIM)
        query_ref[:, two] = returned_ref[group, :, 0:256]
        key_ref[:, one] = returned_ref[group, :, 256:384]
        value_ref[:, one] = returned_ref[group, :, 384:512]


def shape(dims, dtype=jnp.bfloat16):
    return jax.ShapeDtypeStruct(dims, dtype)


VMEM = pl.BlockSpec(memory_space=pltpu.VMEM)
SMEM = pl.BlockSpec(memory_space=pltpu.SMEM)


def cost(flops, moved, transcendentals=0):
    return pl.CostEstimate(flops=flops, bytes_accessed=moved, transcendentals=transcendentals)


def pack(me, query, key_rows, value_rows, attn_out, out_grad):
    return pl.pallas_call(
        pack_kernel,
        out_shape=[shape((ROWS + 8, WIDTH))] * N_SEQ,
        in_specs=[SMEM] + [pl.BlockSpec(memory_space=pltpu.HBM)] * 5,
        out_specs=[VMEM] * N_SEQ,
        scratch_shapes=[
            pltpu.VMEM((ROWS, 2048), jnp.bfloat16),
            pltpu.VMEM((ROWS, 1024), jnp.bfloat16),
            pltpu.VMEM((ROWS, 1024), jnp.bfloat16),
            pltpu.VMEM((ROWS, 2048), jnp.bfloat16),
            pltpu.VMEM((ROWS, 2048), jnp.bfloat16),
            pltpu.VMEM((N_SEQ, 8, LANES), jnp.float32),
            pltpu.SemaphoreType.DMA((5,)),
        ],
        compiler_params=FULL,
        name="pack",
    )(me, query, key_rows, value_rows, attn_out, out_grad)


def index(me, lists):
    return pl.pallas_call(
        index_kernel,
        out_shape=(
            shape((16, LANES), jnp.float32),
            shape((GROUP, LANES), jnp.float32),
            shape((N_DP, LANES), jnp.int32),
            shape((1, 1), jnp.int32),
        ),
        in_specs=[SMEM] + [VMEM] * N_Y,
        out_specs=(VMEM, VMEM, VMEM, SMEM),
        scratch_shapes=[pltpu.VMEM((N_SEQ, LANES), jnp.int32)],
        compiler_params=PARAMS,
        name="index",
    )(me, *lists)


def send(me, most, request, parts):
    return pl.pallas_call(
        send_kernel,
        out_shape=[shape((N_DP * SMALL, WIDTH)), shape((N_DP * CAPACITY, WIDTH))],
        in_specs=[SMEM, SMEM] + [VMEM] * 9,
        out_specs=[VMEM, VMEM],
        scratch_shapes=[
            pltpu.VMEM((GROUP, WIDTH), jnp.bfloat16),
            pltpu.VMEM((8, GROUP), jnp.float32),
            pltpu.VMEM((N_SEQ, 8, LANES), jnp.float32),
        ],
        compiler_params=PARAMS,
        cost_estimate=cost(2 * N_DP * CAPACITY * GROUP * WIDTH, 4_000_000),
        name="send",
    )(me, most, request, *parts)


def send_extra(me, request, parts):
    return pl.pallas_call(
        send_extra_kernel,
        out_shape=shape((N_DP * EXTRA, WIDTH)),
        in_specs=[SMEM] + [VMEM] * 9,
        scratch_shapes=[pltpu.VMEM((GROUP, WIDTH), jnp.bfloat16)],
        compiler_params=PARAMS,
        name="send_extra",
    )(me, request, *parts)


def attend(segments, most, arrived, extra, rows, cols):
    return pl.pallas_call(
        attend_kernel,
        out_shape=shape((GROUP, 4 * HEAD_DIM)),
        in_specs=[SMEM, SMEM, VMEM, pl.BlockSpec(memory_space=pltpu.HBM), VMEM, VMEM, VMEM],
        scratch_shapes=[
            pltpu.VMEM((GROUP, WIDTH), jnp.bfloat16),
            pltpu.VMEM((HEAD_DIM, GROUP), jnp.bfloat16),
            pltpu.VMEM((N_DP * EXTRA, WIDTH), jnp.bfloat16),
            pltpu.VMEM((8, GROUP), jnp.float32),
            pltpu.VMEM((GROUP - 2 * BLOCK, 2 * BLOCK), jnp.float32),
            pltpu.VMEM((GROUP - 2 * BLOCK, 2 * BLOCK), jnp.float32),
            pltpu.VMEM((8, 2 * BLOCK), jnp.float32),
            pltpu.VMEM((HEAD_DIM, 2 * BLOCK), jnp.float32),
            pltpu.VMEM((GROUP, HEAD_DIM), jnp.float32),
            pltpu.VMEM((GROUP, HEAD_DIM), jnp.float32),
            pltpu.SemaphoreType.DMA,
        ],
        compiler_params=PARAMS,
        name="attend",
    )(segments, most, arrived, extra, segments.reshape(N_SEQ, ROWS), rows, cols)


def unpack(returned):
    return pl.pallas_call(
        unpack_kernel,
        out_shape=(shape((ROWS, 2048)), shape((ROWS, 1024)), shape((ROWS, 1024))),
        compiler_params=PARAMS,
        name="unpack",
    )(returned)


def relay(array):
    return lax.all_to_all(array, "dp", split_axis=0, concat_axis=0, tiled=True)


def local(query, key_rows, value_rows, attn_out, out_grad, source_row, segment_ids):
    me = lax.axis_index("seq").reshape(1)

    def swap(array, m):
        return lax.ppermute(array, "seq", [(s, s ^ m) for s in range(N_SEQ)]) if m else array

    mine = source_row.reshape(1, ROWS)
    chip = jnp.concatenate([mine, swap(mine, 1)], axis=0)
    lists = [swap(chip, 2 * m) for m in range(N_Y)]
    packed = pack(me, query, key_rows, value_rows, attn_out, out_grad)
    packed, lists = lax.optimization_barrier((packed, lists))
    parts = [swap(packed[m], m) for m in range(N_SEQ)]
    rows, cols, request, most = index(me, lists)
    request, rows, cols, most = lax.optimization_barrier((relay(request), rows, cols, most))
    pad = N_DP * (CAPACITY - SMALL)
    arrived = lax.cond(
        most[0, 0] < SMALL,
        lambda small, large: jnp.pad(relay(small), ((0, pad), (0, 0))),
        lambda small, large: relay(large),
        *send(me, most, request, parts),
    )
    extra = lax.cond(
        most[0, 0] >= CAPACITY,
        lambda request, *parts: relay(send_extra(me, request, parts)),
        lambda request, *parts: jnp.zeros((N_DP * EXTRA, WIDTH), jnp.bfloat16),
        request,
        *parts,
    )
    grads = attend(segment_ids, most, arrived, extra, rows, cols)
    returned = lax.all_to_all(
        grads.reshape(N_SEQ, ROWS, 4 * HEAD_DIM), "seq", split_axis=0, concat_axis=0, tiled=True
    )
    return unpack(returned)


def solution(mesh):
    in_specs = (
        P(("dp", "seq"), None),
        P(("dp", "seq"), None),
        P(("dp", "seq"), None),
        P(("dp", "seq"), None),
        P(("dp", "seq"), None),
        P(("dp", "seq")),
        P("dp"),
    )
    out_specs = (P(("dp", "seq"), None), P(("dp", "seq"), None), P(("dp", "seq"), None))
    return jax.shard_map(local, mesh=mesh, in_specs=in_specs, out_specs=out_specs, check_vma=False)
```

```python
import functools

import jax
import jax.numpy as jnp
from jax import lax
from jax.experimental import pallas as pl
from jax.experimental.pallas import tpu as pltpu
from jax.sharding import PartitionSpec as P

HEAD_DIM = 128
N_DP = 32
N_SEQ = 8
N_Y = 4
ROWS = 128
GROUP = N_SEQ * ROWS
WIDTH = 6 * HEAD_DIM
LANES = 128
BLOCK = 256
SMALL = 48
CAPACITY = 56
EXTRA = 16
ORDER = (0, 1, 2, 4, 5, 6, 7, 3)

scaling = 1.0 / 12.0
softcap = 50.0

PARAMS = pltpu.CompilerParams(vmem_limit_bytes=20 * 1024 * 1024)
FULL = pltpu.CompilerParams(vmem_limit_bytes=60 * 1024 * 1024)


def iota(shape, dim):
    return lax.broadcasted_iota(jnp.int32, shape, dim)


def nt_dot(left, right):
    return lax.dot_general(left, right, (((1,), (1,)), ((), ())), preferred_element_type=jnp.float32)


def nn_dot(left, right):
    return jnp.dot(left, right, preferred_element_type=jnp.float32)


def pack_kernel(me_ref, query_hbm, key_hbm, value_hbm, out_hbm, grad_hbm, *refs):
    packed_refs = refs[:N_SEQ]
    query_ref, key_ref, value_ref, out_ref, grad_ref, delta_ref, sems = refs[N_SEQ:]
    pairs = (
        (grad_hbm, grad_ref),
        (out_hbm, out_ref),
        (query_hbm, query_ref),
        (key_hbm, key_ref),
        (value_hbm, value_ref),
    )
    copies = [
        pltpu.make_async_copy(source, target, sems.at[i])
        for i, (source, target) in enumerate(pairs)
    ]
    for copy in copies:
        copy.start()
    copies[0].wait()
    copies[1].wait()
    lane = iota((ROWS, LANES), 1)
    table = jnp.zeros((ROWS, LANES), jnp.float32)
    for head in range(2 * N_SEQ):
        cols = slice(head * HEAD_DIM, (head + 1) * HEAD_DIM)
        product = grad_ref[:, cols].astype(jnp.float32) * out_ref[:, cols].astype(jnp.float32)
        table = jnp.where(lane == head, jnp.sum(product, axis=1, keepdims=True), table)
    delta = table.T
    high = delta.astype(jnp.bfloat16).astype(jnp.float32)
    low = delta - high
    for group in range(N_SEQ):
        pair = slice(2 * group, 2 * group + 2)
        delta_ref[group] = jnp.concatenate(
            [high[pair], low[pair], jnp.zeros((4, LANES), jnp.float32)], axis=0
        )
    pad_cols = jnp.zeros((8, WIDTH - LANES), jnp.float32)
    for copy in copies[2:]:
        copy.wait()
    me = me_ref[0]
    for m in range(N_SEQ):
        group = jnp.bitwise_xor(me, m)
        two = pl.ds(pl.multiple_of(group * 256, 256), 256)
        one = pl.ds(pl.multiple_of(group * 128, 128), 128)
        rows = jnp.concatenate(
            [query_ref[:, two], key_ref[:, one], value_ref[:, one], grad_ref[:, two]], axis=1
        )
        extra = jnp.concatenate([delta_ref[group], pad_cols], axis=1)
        packed_refs[m][...] = jnp.concatenate([rows.astype(jnp.float32), extra], axis=0).astype(
            jnp.bfloat16
        )


def wide(rows):
    return jnp.concatenate([rows[s : s + 1] for s in range(N_SEQ)], axis=1)


def index_kernel(me_ref, *refs):
    lists, (rows_ref, cols_ref, request_ref, most_ref, list_ref) = refs[:N_Y], refs[N_Y:]
    for m in range(N_SEQ):
        part = lists[m // 2][m % 2 : m % 2 + 1, :]
        list_ref[pl.ds(jnp.bitwise_xor(me_ref[0], m), 1), :] = part
    listed = list_ref[...]
    source = (listed // GROUP).astype(jnp.float32)
    local_row = (listed % ROWS).astype(jnp.float32)
    blank = jnp.zeros((LANES - 8, LANES), jnp.float32)
    source_cols = jnp.concatenate([source, blank], axis=0).T
    before = iota((ROWS, ROWS), 0) < iota((ROWS, ROWS), 1)
    slots = []
    for s in range(N_SEQ):
        mine = source[s : s + 1]
        hits = ((source_cols[:, s : s + 1] == mine) & before).astype(jnp.float32)
        for earlier in range(s):
            hits = hits + (source_cols[:, earlier : earlier + 1] == mine).astype(jnp.float32)
        slots.append(jnp.sum(hits, axis=0, keepdims=True))
    slot = jnp.concatenate(slots, axis=0)
    blank = jnp.zeros((LANES - 16, LANES), jnp.float32)
    turned = jnp.concatenate([source, slot, blank], axis=0).T
    lane = iota((ROWS, LANES), 1)
    picks = []
    for s in range(N_SEQ):
        columns = jnp.where(lane == 0, turned[:, s : s + 1], 0.0)
        columns = jnp.where(lane == 1, turned[:, 8 + s : 9 + s], columns)
        cols_ref[s * ROWS : (s + 1) * ROWS, :] = columns
        picks.append((lane.astype(jnp.float32) == turned[:, 8 + s : 9 + s] + 1.0).astype(jnp.float32))
    rows_ref[0:8, :] = source
    rows_ref[8:16, :] = slot
    pick = jnp.concatenate(picks, axis=0).astype(jnp.bfloat16)
    from_source = iota((N_DP, GROUP), 0).astype(jnp.float32) == wide(source)
    column = (iota((1, GROUP), 1) // ROWS).astype(jnp.float32)
    low = jnp.where(from_source, wide(local_row) + 1.0, 0.0).astype(jnp.bfloat16)
    high = jnp.where(from_source, column, 0.0).astype(jnp.bfloat16)
    table = nn_dot(low, pick) + float(ROWS) * nn_dot(high, pick)
    request_ref[...] = table.astype(jnp.int32)
    most_ref[0, 0] = (jnp.max(slot) + 1.0).astype(jnp.int32)


def turned_requests(request_ref):
    blank = jnp.zeros((LANES - N_DP, LANES), jnp.float32)
    return jnp.concatenate([request_ref[...].astype(jnp.float32), blank], axis=0).T - 1.0


def group_picks(turned, group, first, capacity):
    column = jnp.concatenate(
        [turned[first : first + capacity, d : d + 1] for d in range(8 * group, 8 * group + 8)], axis=0
    )
    row_id = iota((8 * capacity, GROUP), 1).astype(jnp.float32)
    return (column == row_id).astype(jnp.float32).astype(jnp.bfloat16)


def join_columns(me_ref, parts, ext_ref, delta_ref):
    for part, m in zip(parts, ORDER):
        column = jnp.bitwise_xor(me_ref[0], m)
        whole = part[...]
        ext_ref[pl.ds(pl.multiple_of(column * ROWS, ROWS), ROWS), :] = whole[:ROWS]
        if delta_ref is not None:
            delta_ref[column] = whole[ROWS:, :LANES].astype(jnp.float32)


def send_extra_kernel(me_ref, request_ref, *refs):
    parts, (sent_ref, ext_ref) = refs[:N_SEQ], refs[N_SEQ:]
    group_rows = 8 * EXTRA
    turned = turned_requests(request_ref)
    join_columns(me_ref, parts, ext_ref, None)
    for group in range(N_DP // 8):
        pick = group_picks(turned, group, CAPACITY, EXTRA)
        rows = slice(group * group_rows, (group + 1) * group_rows)
        sent_ref[rows, :] = nn_dot(pick, ext_ref[...]).astype(jnp.bfloat16)


def send_kernel(me_ref, most_ref, request_ref, *refs):
    parts, (sent_ref, ext_ref, place_ref, delta_ref) = refs[:N_SEQ], refs[N_SEQ:]
    turned = turned_requests(request_ref)
    join_columns(me_ref, parts, ext_ref, delta_ref)

    @pl.when(most_ref[0, 0] < SMALL)
    def _():
        fill(SMALL, most_ref, turned, sent_ref, ext_ref, place_ref, delta_ref)

    @pl.when(most_ref[0, 0] >= SMALL)
    def _():
        fill(CAPACITY, most_ref, turned, sent_ref, ext_ref, place_ref, delta_ref)


def fill(capacity, most_ref, turned, sent_ref, ext_ref, place_ref, delta_ref):
    group_rows = 8 * capacity
    delta = jnp.concatenate([delta_ref[s] for s in range(N_SEQ)], axis=1)

    def places(pick, group, first, count):
        index = iota((8, 8 * count), 1)
        owner = index // count
        value = jnp.where(
            iota((8, 8 * count), 0) == 0, owner + 8 * group, index - owner * count + first
        )
        return nn_dot(value.astype(jnp.float32).astype(jnp.bfloat16), pick)

    place = jnp.zeros((8, GROUP), jnp.float32)
    for group in range(N_DP // 8):
        pick = group_picks(turned, group, 0, capacity)
        place = place + places(pick, group, 0, capacity)
        rows = slice(group * group_rows, (group + 1) * group_rows)
        sent_ref[rows, :] = nn_dot(pick, ext_ref[...]).astype(jnp.bfloat16)
    place_ref[...] = place

    if capacity == CAPACITY:

        @pl.when(most_ref[0, 0] >= CAPACITY)
        def _():
            more = jnp.zeros((8, GROUP), jnp.float32)
            for group in range(N_DP // 8):
                more = more + places(
                    group_picks(turned, group, CAPACITY, EXTRA), group, CAPACITY, EXTRA
                )
            place_ref[...] += more

    place = place_ref[...]
    owner_of = place[0:1]
    slot_cols = []
    for s in range(N_SEQ):
        part = place[:, s * ROWS : (s + 1) * ROWS]
        blank = jnp.zeros((LANES - 8, LANES), jnp.float32)
        slot_cols.append(jnp.concatenate([part, blank], axis=0).T[:, 1:2])
    slot_col = jnp.concatenate(slot_cols, axis=0)
    lane = iota((GROUP, LANES), 1).astype(jnp.float32)
    to_owner = iota((N_DP, GROUP), 0).astype(jnp.float32) == owner_of
    tail = jnp.zeros((2 * N_DP, LANES), jnp.float32)
    for head in range(2):
        spread = jnp.concatenate(
            [jnp.where(to_owner, delta[c : c + 1], 0.0) for c in (head, 2 + head)], axis=0
        )
        slot_pick = (slot_col + (64.0 * head - 1.0) == lane).astype(jnp.float32)
        tail = tail + nn_dot(spread.astype(jnp.bfloat16), slot_pick.astype(jnp.bfloat16))
    tail = jnp.concatenate([tail[:N_DP], tail[N_DP:]], axis=1)
    row = iota((16, 2 * LANES), 0)
    for owner in range(N_DP):
        inside = owner * capacity % 16
        rows = slice(owner * capacity - inside, owner * capacity - inside + 16)
        kept = sent_ref[rows, : 2 * LANES].astype(jnp.float32)
        mine = jnp.broadcast_to(tail[owner : owner + 1], (16, 2 * LANES))
        sent_ref[rows, : 2 * LANES] = jnp.where(row == inside, mine, kept).astype(jnp.bfloat16)


def attend_kernel(
    segment_ref, most_ref, arrived_ref, extra_hbm, marks_ref, rows_ref, cols_ref, out_ref,
    x_ref, kt_ref, extra_ref, lanes_ref, weight_ref, squash_ref, total_ref, gqt_ref, gk_ref, gv_ref, sem,
):
    slots = N_DP * CAPACITY
    blocks = GROUP // BLOCK
    most = most_ref[0, 0]
    capacity = jnp.where(most < SMALL, SMALL, CAPACITY)
    spread = capacity.astype(jnp.float32)

    def rows_of(block):
        return slice(block * BLOCK, (block + 1) * BLOCK)

    def gather(block):
        rows = rows_of(block)
        slot = cols_ref[rows, 1:2] + 1.0
        place = jnp.where(slot < spread, cols_ref[rows, 0:1] * spread + slot, -1.0)
        pick = place == iota((BLOCK, slots), 1).astype(jnp.float32)
        pick = pick.astype(jnp.float32).astype(jnp.bfloat16)
        x_ref[rows, :] = nn_dot(pick, arrived_ref[...]).astype(jnp.bfloat16)

    for block in range(blocks):
        gather(block)

    @pl.when(most >= CAPACITY)
    def _():
        copy = pltpu.make_async_copy(extra_hbm, extra_ref, sem)
        copy.start()
        copy.wait()
        for block in range(blocks):
            rows = rows_of(block)
            slot = cols_ref[rows, 1:2] - float(CAPACITY - 1)
            place = jnp.where(slot >= 0.0, cols_ref[rows, 0:1] * float(EXTRA) + slot, -1.0)
            pick = place == iota((BLOCK, N_DP * EXTRA), 1).astype(jnp.float32)
            pick = pick.astype(jnp.float32).astype(jnp.bfloat16)
            x_ref[rows, :] += nn_dot(pick, extra_ref[...]).astype(jnp.bfloat16)

    for block in range(blocks):
        rows = rows_of(block)
        kt_ref[:, rows] = x_ref[rows, 256:384].astype(jnp.float32).T.astype(jnp.bfloat16)
    first = iota((LANES, slots), 0) * capacity == iota((LANES, slots), 1)
    first = first.astype(jnp.float32).astype(jnp.bfloat16)
    parts = nn_dot(first, arrived_ref[:, : 2 * LANES])
    source = wide(rows_ref[0:8, :])
    slot = wide(rows_ref[8:16, :])
    from_source = iota((LANES, GROUP), 0).astype(jnp.float32) == source
    from_source = from_source.astype(jnp.float32).astype(jnp.bfloat16)
    high = parts[:, :LANES].T.astype(jnp.bfloat16)
    low = parts[:, LANES:].T.astype(jnp.bfloat16)
    both = nn_dot(high, from_source) + nn_dot(low, from_source)
    place = iota((LANES, GROUP), 0).astype(jnp.float32)
    for head in range(2):
        lanes_ref[head : head + 1, :] = jnp.sum(
            jnp.where(place == slot + 64.0 * head, both, 0.0), axis=0, keepdims=True
        )
    gk_ref[...] = jnp.zeros_like(gk_ref)
    gv_ref[...] = jnp.zeros_like(gv_ref)
    marks = marks_ref[...].astype(jnp.float32)
    segment = wide(marks)
    mark_cols = jnp.concatenate([marks, jnp.zeros((LANES - 8, LANES), jnp.float32)], axis=0).T

    for block in range(blocks):
        rows = rows_of(block)
        near = slice(max(block - 1, 0) * BLOCK, (block + 1) * BLOCK)
        near_count = near.stop - near.start
        queries = jnp.concatenate([x_ref[rows, 0:128], x_ref[rows, 128:256]], axis=0)
        grads = jnp.concatenate([x_ref[rows, 512:640], x_ref[rows, 640:768]], axis=0)
        delta = jnp.concatenate([lanes_ref[0:1, rows], lanes_ref[1:2, rows]], axis=1)
        segment_q = jnp.concatenate([segment[:, rows]] * 2, axis=1)
        far = range(block - 1)

        def weigh(keys, causal):
            score = nt_dot(x_ref[keys, 256:384], queries)
            squashed = jnp.tanh(score * (scaling / softcap))
            columns = range(keys.start // ROWS, keys.stop // ROWS)
            segment_k = jnp.concatenate([mark_cols[:, s : s + 1] for s in columns], axis=0)
            allowed = segment_k == segment_q
            if causal is not None:
                allowed = allowed & causal
            return squashed, jnp.where(allowed, jnp.exp(softcap * squashed), 0.0)

        def back(keys, squashed, weights, inverse):
            probabilities = weights * inverse
            gv_ref[keys, :] += nn_dot(probabilities.astype(jnp.bfloat16), grads)
            prob_grad = nt_dot(x_ref[keys, 384:512], grads)
            score_grad = probabilities * (prob_grad - delta) * (1.0 - squashed * squashed)
            score_grad = score_grad.astype(jnp.bfloat16)
            gk_ref[keys, :] += nn_dot(score_grad, queries)
            return nn_dot(kt_ref[:, keys], score_grad)

        def reaches(key_block):
            return segment_ref[(key_block + 1) * BLOCK - 1] == segment_ref[block * BLOCK]

        if len(far) > 0:
            total_ref[...] = jnp.zeros_like(total_ref)
        for key_block in far:

            @pl.when(reaches(key_block))
            def _(keys=rows_of(key_block)):
                squashed, weights = weigh(keys, None)
                weight_ref[keys, :] = weights
                squash_ref[keys, :] = squashed
                total_ref[0:1, :] += jnp.sum(weights, axis=0, keepdims=True)

        ahead = iota((near_count, BLOCK), 0) - iota((near_count, BLOCK), 1)
        causal = (ahead <= near_count - BLOCK).astype(jnp.float32)
        causal = jnp.concatenate([causal, causal], axis=1) > 0.0
        squashed, weights = weigh(near, causal)
        total = jnp.sum(weights, axis=0, keepdims=True)
        if len(far) > 0:
            total = total + total_ref[0:1, :]
        inverse = 1.0 / total
        gqt_ref[...] = back(near, squashed, weights, inverse)
        if len(far) > 0:
            total_ref[0:1, :] = inverse
        for key_block in far:

            @pl.when(reaches(key_block))
            def _(keys=rows_of(key_block)):
                gqt_ref[...] += back(
                    keys, squash_ref[keys, :], weight_ref[keys, :], total_ref[0:1, :]
                )

        turned = (gqt_ref[...].T * scaling).astype(jnp.bfloat16)
        out_ref[rows, 0:128] = turned[:BLOCK]
        out_ref[rows, 128:256] = turned[BLOCK:]
    out_ref[:, 256:384] = (gk_ref[...] * scaling).astype(jnp.bfloat16)
    out_ref[:, 384:512] = gv_ref[...].astype(jnp.bfloat16)


def unpack_kernel(returned_ref, query_ref, key_ref, value_ref):
    for group in range(N_SEQ):
        two = slice(2 * group * HEAD_DIM, 2 * (group + 1) * HEAD_DIM)
        one = slice(group * HEAD_DIM, (group + 1) * HEAD_DIM)
        query_ref[:, two] = returned_ref[group, :, 0:256]
        key_ref[:, one] = returned_ref[group, :, 256:384]
        value_ref[:, one] = returned_ref[group, :, 384:512]


def shape(dims, dtype=jnp.bfloat16):
    return jax.ShapeDtypeStruct(dims, dtype)


VMEM = pl.BlockSpec(memory_space=pltpu.VMEM)
SMEM = pl.BlockSpec(memory_space=pltpu.SMEM)


def cost(flops, moved, transcendentals=0):
    return pl.CostEstimate(flops=flops, bytes_accessed=moved, transcendentals=transcendentals)


def pack(me, query, key_rows, value_rows, attn_out, out_grad):
    return pl.pallas_call(
        pack_kernel,
        out_shape=[shape((ROWS + 8, WIDTH))] * N_SEQ,
        in_specs=[SMEM] + [pl.BlockSpec(memory_space=pltpu.HBM)] * 5,
        out_specs=[VMEM] * N_SEQ,
        scratch_shapes=[
            pltpu.VMEM((ROWS, 2048), jnp.bfloat16),
            pltpu.VMEM((ROWS, 1024), jnp.bfloat16),
            pltpu.VMEM((ROWS, 1024), jnp.bfloat16),
            pltpu.VMEM((ROWS, 2048), jnp.bfloat16),
            pltpu.VMEM((ROWS, 2048), jnp.bfloat16),
            pltpu.VMEM((N_SEQ, 8, LANES), jnp.float32),
            pltpu.SemaphoreType.DMA((5,)),
        ],
        compiler_params=FULL,
        name="pack",
    )(me, query, key_rows, value_rows, attn_out, out_grad)


def index(me, lists):
    return pl.pallas_call(
        index_kernel,
        out_shape=(
            shape((16, LANES), jnp.float32),
            shape((GROUP, LANES), jnp.float32),
            shape((N_DP, LANES), jnp.int32),
            shape((1, 1), jnp.int32),
        ),
        in_specs=[SMEM] + [VMEM] * N_Y,
        out_specs=(VMEM, VMEM, VMEM, SMEM),
        scratch_shapes=[pltpu.VMEM((N_SEQ, LANES), jnp.int32)],
        compiler_params=PARAMS,
        name="index",
    )(me, *lists)


def send(me, most, request, parts):
    return pl.pallas_call(
        send_kernel,
        out_shape=shape((N_DP * CAPACITY, WIDTH)),
        in_specs=[SMEM, SMEM] + [VMEM] * 9,
        scratch_shapes=[
            pltpu.VMEM((GROUP, WIDTH), jnp.bfloat16),
            pltpu.VMEM((8, GROUP), jnp.float32),
            pltpu.VMEM((N_SEQ, 8, LANES), jnp.float32),
        ],
        compiler_params=PARAMS,
        cost_estimate=cost(2 * N_DP * CAPACITY * GROUP * WIDTH, 4_000_000),
        name="send",
    )(me, most, request, *parts)


def send_extra(me, request, parts):
    return pl.pallas_call(
        send_extra_kernel,
        out_shape=shape((N_DP * EXTRA, WIDTH)),
        in_specs=[SMEM] + [VMEM] * 9,
        scratch_shapes=[pltpu.VMEM((GROUP, WIDTH), jnp.bfloat16)],
        compiler_params=PARAMS,
        name="send_extra",
    )(me, request, *parts)


def attend(segments, most, arrived, extra, rows, cols):
    return pl.pallas_call(
        attend_kernel,
        out_shape=shape((GROUP, 4 * HEAD_DIM)),
        in_specs=[SMEM, SMEM, VMEM, pl.BlockSpec(memory_space=pltpu.HBM), VMEM, VMEM, VMEM],
        scratch_shapes=[
            pltpu.VMEM((GROUP, WIDTH), jnp.bfloat16),
            pltpu.VMEM((HEAD_DIM, GROUP), jnp.bfloat16),
            pltpu.VMEM((N_DP * EXTRA, WIDTH), jnp.bfloat16),
            pltpu.VMEM((8, GROUP), jnp.float32),
            pltpu.VMEM((GROUP - 2 * BLOCK, 2 * BLOCK), jnp.float32),
            pltpu.VMEM((GROUP - 2 * BLOCK, 2 * BLOCK), jnp.float32),
            pltpu.VMEM((8, 2 * BLOCK), jnp.float32),
            pltpu.VMEM((HEAD_DIM, 2 * BLOCK), jnp.float32),
            pltpu.VMEM((GROUP, HEAD_DIM), jnp.float32),
            pltpu.VMEM((GROUP, HEAD_DIM), jnp.float32),
            pltpu.SemaphoreType.DMA,
        ],
        compiler_params=PARAMS,
        name="attend",
    )(segments, most, arrived, extra, segments.reshape(N_SEQ, ROWS), rows, cols)


def unpack(returned):
    return pl.pallas_call(
        unpack_kernel,
        out_shape=(shape((ROWS, 2048)), shape((ROWS, 1024)), shape((ROWS, 1024))),
        compiler_params=PARAMS,
        name="unpack",
    )(returned)


def relay(array):
    return lax.all_to_all(array, "dp", split_axis=0, concat_axis=0, tiled=True)


def local(query, key_rows, value_rows, attn_out, out_grad, source_row, segment_ids):
    me = lax.axis_index("seq").reshape(1)

    def swap(array, m):
        return lax.ppermute(array, "seq", [(s, s ^ m) for s in range(N_SEQ)]) if m else array

    mine = source_row.reshape(1, ROWS)
    chip = jnp.concatenate([mine, swap(mine, 1)], axis=0)
    lists = [swap(chip, 2 * m) for m in range(N_Y)]
    packed = pack(me, query, key_rows, value_rows, attn_out, out_grad)
    packed, lists = lax.optimization_barrier((packed, lists))
    parts = [swap(packed[m], m) for m in ORDER]
    rows, cols, request, most = index(me, lists)
    request, rows, cols, most = lax.optimization_barrier((relay(request), rows, cols, most))
    used, pad = N_DP * SMALL, N_DP * (CAPACITY - SMALL)
    arrived = lax.cond(
        most[0, 0] < SMALL,
        lambda sent: jnp.pad(relay(sent[:used]), ((0, pad), (0, 0))),
        relay,
        send(me, most, request, parts),
    )
    extra = lax.cond(
        most[0, 0] >= CAPACITY,
        lambda request, *parts: relay(send_extra(me, request, parts)),
        lambda request, *parts: jnp.zeros((N_DP * EXTRA, WIDTH), jnp.bfloat16),
        request,
        *parts,
    )
    grads = attend(segment_ids, most, arrived, extra, rows, cols)
    returned = lax.all_to_all(
        grads.reshape(N_SEQ, ROWS, 4 * HEAD_DIM), "seq", split_axis=0, concat_axis=0, tiled=True
    )
    return unpack(returned)


def solution(mesh):
    in_specs = (
        P(("dp", "seq"), None),
        P(("dp", "seq"), None),
        P(("dp", "seq"), None),
        P(("dp", "seq"), None),
        P(("dp", "seq"), None),
        P(("dp", "seq")),
        P("dp"),
    )
    out_specs = (P(("dp", "seq"), None), P(("dp", "seq"), None), P(("dp", "seq"), None))
    return jax.shard_map(local, mesh=mesh, in_specs=in_specs, out_specs=out_specs, check_vma=False)
```

```python
import functools

import jax
import jax.numpy as jnp
from jax import lax
from jax.experimental import pallas as pl
from jax.experimental.pallas import tpu as pltpu
from jax.sharding import PartitionSpec as P

HEAD_DIM = 128
N_DP = 32
N_SEQ = 8
N_Y = 4
ROWS = 128
GROUP = N_SEQ * ROWS
WIDTH = 6 * HEAD_DIM
LANES = 128
BLOCK = 256
SMALL = 48
CAPACITY = 56
EXTRA = 16
ORDER = (0, 1, 2, 4, 5, 6, 7, 3)

scaling = 1.0 / 12.0
softcap = 50.0

PARAMS = pltpu.CompilerParams(vmem_limit_bytes=20 * 1024 * 1024)
ROOMY = pltpu.CompilerParams(vmem_limit_bytes=28 * 1024 * 1024)
FULL = pltpu.CompilerParams(vmem_limit_bytes=60 * 1024 * 1024)


def iota(shape, dim):
    return lax.broadcasted_iota(jnp.int32, shape, dim)


def nt_dot(left, right):
    return lax.dot_general(left, right, (((1,), (1,)), ((), ())), preferred_element_type=jnp.float32)


def nn_dot(left, right):
    return jnp.dot(left, right, preferred_element_type=jnp.float32)


def pack_kernel(me_ref, query_hbm, key_hbm, value_hbm, out_hbm, grad_hbm, *refs):
    packed_refs = refs[:N_SEQ]
    query_ref, key_ref, value_ref, out_ref, grad_ref, delta_ref, sems = refs[N_SEQ:]
    pairs = (
        (grad_hbm, grad_ref),
        (out_hbm, out_ref),
        (query_hbm, query_ref),
        (key_hbm, key_ref),
        (value_hbm, value_ref),
    )
    copies = [
        pltpu.make_async_copy(source, target, sems.at[i])
        for i, (source, target) in enumerate(pairs)
    ]
    for copy in copies:
        copy.start()
    copies[0].wait()
    copies[1].wait()
    lane = iota((ROWS, LANES), 1)
    table = jnp.zeros((ROWS, LANES), jnp.float32)
    for head in range(2 * N_SEQ):
        cols = slice(head * HEAD_DIM, (head + 1) * HEAD_DIM)
        product = grad_ref[:, cols].astype(jnp.float32) * out_ref[:, cols].astype(jnp.float32)
        table = jnp.where(lane == head, jnp.sum(product, axis=1, keepdims=True), table)
    delta = table.T
    high = delta.astype(jnp.bfloat16).astype(jnp.float32)
    low = delta - high
    for group in range(N_SEQ):
        pair = slice(2 * group, 2 * group + 2)
        delta_ref[group] = jnp.concatenate(
            [high[pair], low[pair], jnp.zeros((4, LANES), jnp.float32)], axis=0
        )
    pad_cols = jnp.zeros((8, WIDTH - LANES), jnp.float32)
    for copy in copies[2:]:
        copy.wait()
    me = me_ref[0]
    for m in range(N_SEQ):
        group = jnp.bitwise_xor(me, m)
        two = pl.ds(pl.multiple_of(group * 256, 256), 256)
        one = pl.ds(pl.multiple_of(group * 128, 128), 128)
        rows = jnp.concatenate(
            [query_ref[:, two], key_ref[:, one], value_ref[:, one], grad_ref[:, two]], axis=1
        )
        extra = jnp.concatenate([delta_ref[group], pad_cols], axis=1)
        packed_refs[m][...] = jnp.concatenate([rows.astype(jnp.float32), extra], axis=0).astype(
            jnp.bfloat16
        )


def wide(rows):
    return jnp.concatenate([rows[s : s + 1] for s in range(N_SEQ)], axis=1)


def index_kernel(me_ref, *refs):
    lists, (rows_ref, cols_ref, request_ref, most_ref, list_ref) = refs[:N_Y], refs[N_Y:]
    for m in range(N_SEQ):
        part = lists[m // 2][m % 2 : m % 2 + 1, :]
        list_ref[pl.ds(jnp.bitwise_xor(me_ref[0], m), 1), :] = part
    listed = list_ref[...]
    source = (listed // GROUP).astype(jnp.float32)
    local_row = (listed % ROWS).astype(jnp.float32)
    blank = jnp.zeros((LANES - 8, LANES), jnp.float32)
    source_cols = jnp.concatenate([source, blank], axis=0).T
    before = iota((ROWS, ROWS), 0) < iota((ROWS, ROWS), 1)
    slots = []
    for s in range(N_SEQ):
        mine = source[s : s + 1]
        hits = ((source_cols[:, s : s + 1] == mine) & before).astype(jnp.float32)
        for earlier in range(s):
            hits = hits + (source_cols[:, earlier : earlier + 1] == mine).astype(jnp.float32)
        slots.append(jnp.sum(hits, axis=0, keepdims=True))
    slot = jnp.concatenate(slots, axis=0)
    blank = jnp.zeros((LANES - 16, LANES), jnp.float32)
    turned = jnp.concatenate([source, slot, blank], axis=0).T
    lane = iota((ROWS, LANES), 1)
    picks = []
    for s in range(N_SEQ):
        columns = jnp.where(lane == 0, turned[:, s : s + 1], 0.0)
        columns = jnp.where(lane == 1, turned[:, 8 + s : 9 + s], columns)
        cols_ref[s * ROWS : (s + 1) * ROWS, :] = columns
        picks.append((lane.astype(jnp.float32) == turned[:, 8 + s : 9 + s] + 1.0).astype(jnp.float32))
    rows_ref[0:8, :] = source
    rows_ref[8:16, :] = slot
    pick = jnp.concatenate(picks, axis=0).astype(jnp.bfloat16)
    from_source = iota((N_DP, GROUP), 0).astype(jnp.float32) == wide(source)
    column = (iota((1, GROUP), 1) // ROWS).astype(jnp.float32)
    low = jnp.where(from_source, wide(local_row) + 1.0, 0.0).astype(jnp.bfloat16)
    high = jnp.where(from_source, column, 0.0).astype(jnp.bfloat16)
    table = nn_dot(low, pick) + float(ROWS) * nn_dot(high, pick)
    request_ref[...] = table.astype(jnp.int32)
    most_ref[0, 0] = (jnp.max(slot) + 1.0).astype(jnp.int32)


def turned_requests(request_ref):
    blank = jnp.zeros((LANES - N_DP, LANES), jnp.float32)
    return jnp.concatenate([request_ref[...].astype(jnp.float32), blank], axis=0).T - 1.0


def group_picks(turned, group, first, capacity):
    column = jnp.concatenate(
        [turned[first : first + capacity, d : d + 1] for d in range(8 * group, 8 * group + 8)], axis=0
    )
    row_id = iota((8 * capacity, GROUP), 1).astype(jnp.float32)
    return (column == row_id).astype(jnp.float32).astype(jnp.bfloat16)


def join_columns(me_ref, parts, ext_ref, delta_ref):
    for part, m in zip(parts, ORDER):
        column = jnp.bitwise_xor(me_ref[0], m)
        whole = part[...]
        ext_ref[pl.ds(pl.multiple_of(column * ROWS, ROWS), ROWS), :] = whole[:ROWS]
        if delta_ref is not None:
            delta_ref[column] = whole[ROWS:, :LANES].astype(jnp.float32)


def send_extra_kernel(me_ref, request_ref, *refs):
    parts, (sent_ref, ext_ref) = refs[:N_SEQ], refs[N_SEQ:]
    group_rows = 8 * EXTRA
    turned = turned_requests(request_ref)
    join_columns(me_ref, parts, ext_ref, None)
    for group in range(N_DP // 8):
        pick = group_picks(turned, group, CAPACITY, EXTRA)
        rows = slice(group * group_rows, (group + 1) * group_rows)
        sent_ref[rows, :] = nn_dot(pick, ext_ref[...]).astype(jnp.bfloat16)


def send_kernel(me_ref, most_ref, request_ref, *refs):
    parts, (sent_ref, ext_ref, place_ref, delta_ref) = refs[:N_SEQ], refs[N_SEQ:]
    turned = turned_requests(request_ref)
    join_columns(me_ref, parts, ext_ref, delta_ref)

    @pl.when(most_ref[0, 0] < SMALL)
    def _():
        fill(SMALL, most_ref, turned, sent_ref, ext_ref, place_ref, delta_ref)

    @pl.when(most_ref[0, 0] >= SMALL)
    def _():
        fill(CAPACITY, most_ref, turned, sent_ref, ext_ref, place_ref, delta_ref)


def fill(capacity, most_ref, turned, sent_ref, ext_ref, place_ref, delta_ref):
    group_rows = 8 * capacity
    delta = jnp.concatenate([delta_ref[s] for s in range(N_SEQ)], axis=1)

    def places(pick, group, first, count):
        index = iota((8, 8 * count), 1)
        owner = index // count
        value = jnp.where(
            iota((8, 8 * count), 0) == 0, owner + 8 * group, index - owner * count + first
        )
        return nn_dot(value.astype(jnp.float32).astype(jnp.bfloat16), pick)

    place = jnp.zeros((8, GROUP), jnp.float32)
    for group in range(N_DP // 8):
        pick = group_picks(turned, group, 0, capacity)
        place = place + places(pick, group, 0, capacity)
        rows = slice(group * group_rows, (group + 1) * group_rows)
        sent_ref[rows, :] = nn_dot(pick, ext_ref[...]).astype(jnp.bfloat16)
    place_ref[...] = place

    if capacity == CAPACITY:

        @pl.when(most_ref[0, 0] >= CAPACITY)
        def _():
            more = jnp.zeros((8, GROUP), jnp.float32)
            for group in range(N_DP // 8):
                more = more + places(
                    group_picks(turned, group, CAPACITY, EXTRA), group, CAPACITY, EXTRA
                )
            place_ref[...] += more

    place = place_ref[...]
    owner_of = place[0:1]
    slot_cols = []
    for s in range(N_SEQ):
        part = place[:, s * ROWS : (s + 1) * ROWS]
        blank = jnp.zeros((LANES - 8, LANES), jnp.float32)
        slot_cols.append(jnp.concatenate([part, blank], axis=0).T[:, 1:2])
    slot_col = jnp.concatenate(slot_cols, axis=0)
    lane = iota((GROUP, LANES), 1).astype(jnp.float32)
    to_owner = iota((N_DP, GROUP), 0).astype(jnp.float32) == owner_of
    tail = jnp.zeros((2 * N_DP, LANES), jnp.float32)
    for head in range(2):
        spread = jnp.concatenate(
            [jnp.where(to_owner, delta[c : c + 1], 0.0) for c in (head, 2 + head)], axis=0
        )
        slot_pick = (slot_col + (64.0 * head - 1.0) == lane).astype(jnp.float32)
        tail = tail + nn_dot(spread.astype(jnp.bfloat16), slot_pick.astype(jnp.bfloat16))
    tail = jnp.concatenate([tail[:N_DP], tail[N_DP:]], axis=1)
    row = iota((16, 2 * LANES), 0)
    for owner in range(N_DP):
        inside = owner * capacity % 16
        rows = slice(owner * capacity - inside, owner * capacity - inside + 16)
        kept = sent_ref[rows, : 2 * LANES].astype(jnp.float32)
        mine = jnp.broadcast_to(tail[owner : owner + 1], (16, 2 * LANES))
        sent_ref[rows, : 2 * LANES] = jnp.where(row == inside, mine, kept).astype(jnp.bfloat16)


def attend_kernel(
    segment_ref, most_ref, arrived_ref, extra_ref, marks_ref, rows_ref, cols_ref, out_ref,
    x_ref, kt_ref, lanes_ref, weight_ref, squash_ref, total_ref, gqt_ref, gk_ref, gv_ref,
):
    slots = N_DP * CAPACITY
    blocks = GROUP // BLOCK
    most = most_ref[0, 0]
    capacity = jnp.where(most < SMALL, SMALL, CAPACITY)
    spread = capacity.astype(jnp.float32)

    def rows_of(block):
        return slice(block * BLOCK, (block + 1) * BLOCK)

    def gather(block):
        rows = rows_of(block)
        slot = cols_ref[rows, 1:2] + 1.0
        place = jnp.where(slot < spread, cols_ref[rows, 0:1] * spread + slot, -1.0)
        pick = place == iota((BLOCK, slots), 1).astype(jnp.float32)
        pick = pick.astype(jnp.float32).astype(jnp.bfloat16)
        x_ref[rows, :] = nn_dot(pick, arrived_ref[...]).astype(jnp.bfloat16)

    for block in range(blocks):
        gather(block)

    @pl.when(most >= CAPACITY)
    def _():
        for block in range(blocks):
            rows = rows_of(block)
            slot = cols_ref[rows, 1:2] - float(CAPACITY - 1)
            place = jnp.where(slot >= 0.0, cols_ref[rows, 0:1] * float(EXTRA) + slot, -1.0)
            pick = place == iota((BLOCK, N_DP * EXTRA), 1).astype(jnp.float32)
            pick = pick.astype(jnp.float32).astype(jnp.bfloat16)
            x_ref[rows, :] += nn_dot(pick, extra_ref[...]).astype(jnp.bfloat16)

    for block in range(blocks):
        rows = rows_of(block)
        kt_ref[:, rows] = x_ref[rows, 256:384].astype(jnp.float32).T.astype(jnp.bfloat16)
    first = iota((LANES, slots), 0) * capacity == iota((LANES, slots), 1)
    first = first.astype(jnp.float32).astype(jnp.bfloat16)
    parts = nn_dot(first, arrived_ref[:, : 2 * LANES])
    source = wide(rows_ref[0:8, :])
    slot = wide(rows_ref[8:16, :])
    from_source = iota((LANES, GROUP), 0).astype(jnp.float32) == source
    from_source = from_source.astype(jnp.float32).astype(jnp.bfloat16)
    high = parts[:, :LANES].T.astype(jnp.bfloat16)
    low = parts[:, LANES:].T.astype(jnp.bfloat16)
    both = nn_dot(high, from_source) + nn_dot(low, from_source)
    place = iota((LANES, GROUP), 0).astype(jnp.float32)
    for head in range(2):
        lanes_ref[head : head + 1, :] = jnp.sum(
            jnp.where(place == slot + 64.0 * head, both, 0.0), axis=0, keepdims=True
        )
    gk_ref[...] = jnp.zeros_like(gk_ref)
    gv_ref[...] = jnp.zeros_like(gv_ref)
    marks = marks_ref[...].astype(jnp.float32)
    segment = wide(marks)
    mark_cols = jnp.concatenate([marks, jnp.zeros((LANES - 8, LANES), jnp.float32)], axis=0).T

    for block in range(blocks):
        rows = rows_of(block)
        near = slice(max(block - 1, 0) * BLOCK, (block + 1) * BLOCK)
        near_count = near.stop - near.start
        queries = jnp.concatenate([x_ref[rows, 0:128], x_ref[rows, 128:256]], axis=0)
        grads = jnp.concatenate([x_ref[rows, 512:640], x_ref[rows, 640:768]], axis=0)
        delta = jnp.concatenate([lanes_ref[0:1, rows], lanes_ref[1:2, rows]], axis=1)
        segment_q = jnp.concatenate([segment[:, rows]] * 2, axis=1)
        far = range(block - 1)

        def weigh(keys, causal):
            score = nt_dot(x_ref[keys, 256:384], queries)
            squashed = jnp.tanh(score * (scaling / softcap))
            columns = range(keys.start // ROWS, keys.stop // ROWS)
            segment_k = jnp.concatenate([mark_cols[:, s : s + 1] for s in columns], axis=0)
            allowed = segment_k == segment_q
            if causal is not None:
                allowed = allowed & causal
            return squashed, jnp.where(allowed, jnp.exp(softcap * squashed), 0.0)

        def back(keys, squashed, weights, inverse):
            probabilities = weights * inverse
            gv_ref[keys, :] += nn_dot(probabilities.astype(jnp.bfloat16), grads)
            prob_grad = nt_dot(x_ref[keys, 384:512], grads)
            score_grad = probabilities * (prob_grad - delta) * (1.0 - squashed * squashed)
            score_grad = score_grad.astype(jnp.bfloat16)
            gk_ref[keys, :] += nn_dot(score_grad, queries)
            return nn_dot(kt_ref[:, keys], score_grad)

        def reaches(key_block):
            return segment_ref[(key_block + 1) * BLOCK - 1] == segment_ref[block * BLOCK]

        if len(far) > 0:
            total_ref[...] = jnp.zeros_like(total_ref)
        for key_block in far:

            @pl.when(reaches(key_block))
            def _(keys=rows_of(key_block)):
                squashed, weights = weigh(keys, None)
                weight_ref[keys, :] = weights
                squash_ref[keys, :] = squashed
                total_ref[0:1, :] += jnp.sum(weights, axis=0, keepdims=True)

        ahead = iota((near_count, BLOCK), 0) - iota((near_count, BLOCK), 1)
        causal = (ahead <= near_count - BLOCK).astype(jnp.float32)
        causal = jnp.concatenate([causal, causal], axis=1) > 0.0
        squashed, weights = weigh(near, causal)
        total = jnp.sum(weights, axis=0, keepdims=True)
        if len(far) > 0:
            total = total + total_ref[0:1, :]
        inverse = 1.0 / total
        gqt_ref[...] = back(near, squashed, weights, inverse)
        if len(far) > 0:
            total_ref[0:1, :] = inverse
        for key_block in far:

            @pl.when(reaches(key_block))
            def _(keys=rows_of(key_block)):
                gqt_ref[...] += back(
                    keys, squash_ref[keys, :], weight_ref[keys, :], total_ref[0:1, :]
                )

        turned = (gqt_ref[...].T * scaling).astype(jnp.bfloat16)
        out_ref[rows, 0:128] = turned[:BLOCK]
        out_ref[rows, 128:256] = turned[BLOCK:]
    out_ref[:, 256:384] = (gk_ref[...] * scaling).astype(jnp.bfloat16)
    out_ref[:, 384:512] = gv_ref[...].astype(jnp.bfloat16)


def unpack_kernel(returned_ref, query_ref, key_ref, value_ref):
    for group in range(N_SEQ):
        two = slice(2 * group * HEAD_DIM, 2 * (group + 1) * HEAD_DIM)
        one = slice(group * HEAD_DIM, (group + 1) * HEAD_DIM)
        query_ref[:, two] = returned_ref[group, :, 0:256]
        key_ref[:, one] = returned_ref[group, :, 256:384]
        value_ref[:, one] = returned_ref[group, :, 384:512]


def shape(dims, dtype=jnp.bfloat16):
    return jax.ShapeDtypeStruct(dims, dtype)


VMEM = pl.BlockSpec(memory_space=pltpu.VMEM)
SMEM = pl.BlockSpec(memory_space=pltpu.SMEM)


def cost(flops, moved, transcendentals=0):
    return pl.CostEstimate(flops=flops, bytes_accessed=moved, transcendentals=transcendentals)


def pack(me, query, key_rows, value_rows, attn_out, out_grad):
    return pl.pallas_call(
        pack_kernel,
        out_shape=[shape((ROWS + 8, WIDTH))] * N_SEQ,
        in_specs=[SMEM] + [pl.BlockSpec(memory_space=pltpu.HBM)] * 5,
        out_specs=[VMEM] * N_SEQ,
        scratch_shapes=[
            pltpu.VMEM((ROWS, 2048), jnp.bfloat16),
            pltpu.VMEM((ROWS, 1024), jnp.bfloat16),
            pltpu.VMEM((ROWS, 1024), jnp.bfloat16),
            pltpu.VMEM((ROWS, 2048), jnp.bfloat16),
            pltpu.VMEM((ROWS, 2048), jnp.bfloat16),
            pltpu.VMEM((N_SEQ, 8, LANES), jnp.float32),
            pltpu.SemaphoreType.DMA((5,)),
        ],
        compiler_params=FULL,
        name="pack",
    )(me, query, key_rows, value_rows, attn_out, out_grad)


def index(me, lists):
    return pl.pallas_call(
        index_kernel,
        out_shape=(
            shape((16, LANES), jnp.float32),
            shape((GROUP, LANES), jnp.float32),
            shape((N_DP, LANES), jnp.int32),
            shape((1, 1), jnp.int32),
        ),
        in_specs=[SMEM] + [VMEM] * N_Y,
        out_specs=(VMEM, VMEM, VMEM, SMEM),
        scratch_shapes=[pltpu.VMEM((N_SEQ, LANES), jnp.int32)],
        compiler_params=PARAMS,
        name="index",
    )(me, *lists)


def send(me, most, request, parts):
    return pl.pallas_call(
        send_kernel,
        out_shape=shape((N_DP * CAPACITY, WIDTH)),
        in_specs=[SMEM, SMEM] + [VMEM] * 9,
        scratch_shapes=[
            pltpu.VMEM((GROUP, WIDTH), jnp.bfloat16),
            pltpu.VMEM((8, GROUP), jnp.float32),
            pltpu.VMEM((N_SEQ, 8, LANES), jnp.float32),
        ],
        compiler_params=ROOMY,
        cost_estimate=cost(2 * N_DP * CAPACITY * GROUP * WIDTH, 4_000_000),
        name="send",
    )(me, most, request, *parts)


def send_extra(me, request, parts):
    return pl.pallas_call(
        send_extra_kernel,
        out_shape=shape((N_DP * EXTRA, WIDTH)),
        in_specs=[SMEM] + [VMEM] * 9,
        scratch_shapes=[pltpu.VMEM((GROUP, WIDTH), jnp.bfloat16)],
        compiler_params=PARAMS,
        name="send_extra",
    )(me, request, *parts)


def attend(segments, most, arrived, extra, rows, cols):
    return pl.pallas_call(
        attend_kernel,
        out_shape=shape((GROUP, 4 * HEAD_DIM)),
        in_specs=[SMEM, SMEM] + [VMEM] * 5,
        scratch_shapes=[
            pltpu.VMEM((GROUP, WIDTH), jnp.bfloat16),
            pltpu.VMEM((HEAD_DIM, GROUP), jnp.bfloat16),
            pltpu.VMEM((8, GROUP), jnp.float32),
            pltpu.VMEM((GROUP - 2 * BLOCK, 2 * BLOCK), jnp.float32),
            pltpu.VMEM((GROUP - 2 * BLOCK, 2 * BLOCK), jnp.float32),
            pltpu.VMEM((8, 2 * BLOCK), jnp.float32),
            pltpu.VMEM((HEAD_DIM, 2 * BLOCK), jnp.float32),
            pltpu.VMEM((GROUP, HEAD_DIM), jnp.float32),
            pltpu.VMEM((GROUP, HEAD_DIM), jnp.float32),
        ],
        compiler_params=PARAMS,
        name="attend",
    )(segments, most, arrived, extra, segments.reshape(N_SEQ, ROWS), rows, cols)


def unpack(returned):
    return pl.pallas_call(
        unpack_kernel,
        out_shape=(shape((ROWS, 2048)), shape((ROWS, 1024)), shape((ROWS, 1024))),
        compiler_params=PARAMS,
        name="unpack",
    )(returned)


def relay(array):
    return lax.all_to_all(array, "dp", split_axis=0, concat_axis=0, tiled=True)


def local(query, key_rows, value_rows, attn_out, out_grad, source_row, segment_ids):
    me = lax.axis_index("seq").reshape(1)

    def swap(array, m):
        return lax.ppermute(array, "seq", [(s, s ^ m) for s in range(N_SEQ)]) if m else array

    mine = source_row.reshape(1, ROWS)
    chip = jnp.concatenate([mine, swap(mine, 1)], axis=0)
    lists = [swap(chip, 2 * m) for m in range(N_Y)]
    packed = pack(me, query, key_rows, value_rows, attn_out, out_grad)
    packed, lists = lax.optimization_barrier((packed, lists))
    parts = [swap(packed[m], m) for m in ORDER]
    rows, cols, request, most = index(me, lists)
    request, rows, cols, most = lax.optimization_barrier((relay(request), rows, cols, most))
    used, pad = N_DP * SMALL, N_DP * (CAPACITY - SMALL)
    arrived = lax.cond(
        most[0, 0] < SMALL,
        lambda sent: jnp.pad(relay(sent[:used]), ((0, pad), (0, 0))),
        relay,
        send(me, most, request, parts),
    )
    extra = lax.cond(
        most[0, 0] >= CAPACITY,
        lambda request, *parts: relay(send_extra(me, request, parts)),
        lambda request, *parts: jnp.zeros((N_DP * EXTRA, WIDTH), jnp.bfloat16),
        request,
        *parts,
    )
    grads = attend(segment_ids, most, arrived, extra, rows, cols)
    returned = lax.all_to_all(
        grads.reshape(N_SEQ, ROWS, 4 * HEAD_DIM), "seq", split_axis=0, concat_axis=0, tiled=True
    )
    return unpack(returned)


def solution(mesh):
    in_specs = (
        P(("dp", "seq"), None),
        P(("dp", "seq"), None),
        P(("dp", "seq"), None),
        P(("dp", "seq"), None),
        P(("dp", "seq"), None),
        P(("dp", "seq")),
        P("dp"),
    )
    out_specs = (P(("dp", "seq"), None), P(("dp", "seq"), None), P(("dp", "seq"), None))
    return jax.shard_map(local, mesh=mesh, in_specs=in_specs, out_specs=out_specs, check_vma=False)
```

```python
import functools

import jax
import jax.numpy as jnp
from jax import lax
from jax.experimental import pallas as pl
from jax.experimental.pallas import tpu as pltpu
from jax.sharding import PartitionSpec as P

HEAD_DIM = 128
N_DP = 32
N_SEQ = 8
N_Y = 4
ROWS = 128
GROUP = N_SEQ * ROWS
WIDTH = 6 * HEAD_DIM
LANES = 128
BLOCK = 256
SMALL = 48
CAPACITY = 56
EXTRA = 16
ORDER = (0, 1, 2, 4, 5, 6, 7, 3)

scaling = 1.0 / 12.0
softcap = 50.0

PARAMS = pltpu.CompilerParams(vmem_limit_bytes=20 * 1024 * 1024)
ROOMY = pltpu.CompilerParams(vmem_limit_bytes=28 * 1024 * 1024)
FULL = pltpu.CompilerParams(vmem_limit_bytes=60 * 1024 * 1024)


def iota(shape, dim):
    return lax.broadcasted_iota(jnp.int32, shape, dim)


def nt_dot(left, right):
    return lax.dot_general(left, right, (((1,), (1,)), ((), ())), preferred_element_type=jnp.float32)


def nn_dot(left, right):
    return jnp.dot(left, right, preferred_element_type=jnp.float32)


def pack_kernel(me_ref, query_hbm, key_hbm, value_hbm, out_hbm, grad_hbm, *refs):
    packed_refs = refs[:N_SEQ]
    query_ref, key_ref, value_ref, out_ref, grad_ref, delta_ref, sems = refs[N_SEQ:]
    pairs = (
        (grad_hbm, grad_ref),
        (out_hbm, out_ref),
        (query_hbm, query_ref),
        (key_hbm, key_ref),
        (value_hbm, value_ref),
    )
    copies = [
        pltpu.make_async_copy(source, target, sems.at[i])
        for i, (source, target) in enumerate(pairs)
    ]
    for copy in copies:
        copy.start()
    copies[0].wait()
    copies[1].wait()
    lane = iota((ROWS, LANES), 1)
    table = jnp.zeros((ROWS, LANES), jnp.float32)
    for head in range(2 * N_SEQ):
        cols = slice(head * HEAD_DIM, (head + 1) * HEAD_DIM)
        product = grad_ref[:, cols].astype(jnp.float32) * out_ref[:, cols].astype(jnp.float32)
        table = jnp.where(lane == head, jnp.sum(product, axis=1, keepdims=True), table)
    delta = table.T
    high = delta.astype(jnp.bfloat16).astype(jnp.float32)
    low = delta - high
    for group in range(N_SEQ):
        pair = slice(2 * group, 2 * group + 2)
        delta_ref[group] = jnp.concatenate(
            [high[pair], low[pair], jnp.zeros((4, LANES), jnp.float32)], axis=0
        )
    pad_cols = jnp.zeros((8, WIDTH - LANES), jnp.float32)
    for copy in copies[2:]:
        copy.wait()
    me = me_ref[0]
    for m in range(N_SEQ):
        group = jnp.bitwise_xor(me, m)
        two = pl.ds(pl.multiple_of(group * 256, 256), 256)
        one = pl.ds(pl.multiple_of(group * 128, 128), 128)
        rows = jnp.concatenate(
            [query_ref[:, two], key_ref[:, one], value_ref[:, one], grad_ref[:, two]], axis=1
        )
        extra = jnp.concatenate([delta_ref[group], pad_cols], axis=1)
        packed_refs[m][...] = jnp.concatenate([rows.astype(jnp.float32), extra], axis=0).astype(
            jnp.bfloat16
        )


def wide(rows):
    return jnp.concatenate([rows[s : s + 1] for s in range(N_SEQ)], axis=1)


def index_kernel(me_ref, *refs):
    lists, (rows_ref, cols_ref, request_ref, most_ref, list_ref) = refs[:N_Y], refs[N_Y:]
    for m in range(N_SEQ):
        part = lists[m // 2][m % 2 : m % 2 + 1, :]
        list_ref[pl.ds(jnp.bitwise_xor(me_ref[0], m), 1), :] = part
    listed = list_ref[...]
    source = (listed // GROUP).astype(jnp.float32)
    local_row = (listed % ROWS).astype(jnp.float32)
    blank = jnp.zeros((LANES - 8, LANES), jnp.float32)
    source_cols = jnp.concatenate([source, blank], axis=0).T
    before = iota((ROWS, ROWS), 0) < iota((ROWS, ROWS), 1)
    slots = []
    for s in range(N_SEQ):
        mine = source[s : s + 1]
        hits = ((source_cols[:, s : s + 1] == mine) & before).astype(jnp.float32)
        for earlier in range(s):
            hits = hits + (source_cols[:, earlier : earlier + 1] == mine).astype(jnp.float32)
        slots.append(jnp.sum(hits, axis=0, keepdims=True))
    slot = jnp.concatenate(slots, axis=0)
    blank = jnp.zeros((LANES - 16, LANES), jnp.float32)
    turned = jnp.concatenate([source, slot, blank], axis=0).T
    lane = iota((ROWS, LANES), 1)
    picks = []
    for s in range(N_SEQ):
        columns = jnp.where(lane == 0, turned[:, s : s + 1], 0.0)
        columns = jnp.where(lane == 1, turned[:, 8 + s : 9 + s], columns)
        cols_ref[s * ROWS : (s + 1) * ROWS, :] = columns
        picks.append((lane.astype(jnp.float32) == turned[:, 8 + s : 9 + s] + 1.0).astype(jnp.float32))
    rows_ref[0:8, :] = source
    rows_ref[8:16, :] = slot
    pick = jnp.concatenate(picks, axis=0).astype(jnp.bfloat16)
    from_source = iota((N_DP, GROUP), 0).astype(jnp.float32) == wide(source)
    column = (iota((1, GROUP), 1) // ROWS).astype(jnp.float32)
    low = jnp.where(from_source, wide(local_row) + 1.0, 0.0).astype(jnp.bfloat16)
    high = jnp.where(from_source, column, 0.0).astype(jnp.bfloat16)
    table = nn_dot(low, pick) + float(ROWS) * nn_dot(high, pick)
    request_ref[...] = table.astype(jnp.int32)
    most_ref[0, 0] = (jnp.max(slot) + 1.0).astype(jnp.int32)


def turned_requests(request_ref):
    blank = jnp.zeros((LANES - N_DP, LANES), jnp.float32)
    return jnp.concatenate([request_ref[...].astype(jnp.float32), blank], axis=0).T - 1.0


def group_picks(turned, group, first, capacity):
    column = jnp.concatenate(
        [turned[first : first + capacity, d : d + 1] for d in range(8 * group, 8 * group + 8)], axis=0
    )
    row_id = iota((8 * capacity, GROUP), 1).astype(jnp.float32)
    return (column == row_id).astype(jnp.float32).astype(jnp.bfloat16)


def join_columns(me_ref, parts, ext_ref, delta_ref):
    for part, m in zip(parts, ORDER):
        column = jnp.bitwise_xor(me_ref[0], m)
        whole = part[...]
        ext_ref[pl.ds(pl.multiple_of(column * ROWS, ROWS), ROWS), :] = whole[:ROWS]
        if delta_ref is not None:
            delta_ref[column] = whole[ROWS:, :LANES].astype(jnp.float32)


def send_extra_kernel(me_ref, request_ref, *refs):
    parts, (sent_ref, ext_ref) = refs[:N_SEQ], refs[N_SEQ:]
    group_rows = 8 * EXTRA
    turned = turned_requests(request_ref)
    join_columns(me_ref, parts, ext_ref, None)
    for group in range(N_DP // 8):
        pick = group_picks(turned, group, CAPACITY, EXTRA)
        rows = slice(group * group_rows, (group + 1) * group_rows)
        sent_ref[rows, :] = nn_dot(pick, ext_ref[...]).astype(jnp.bfloat16)


def send_kernel(me_ref, most_ref, request_ref, *refs):
    parts, (sent_ref, ext_ref, place_ref, delta_ref) = refs[:N_SEQ], refs[N_SEQ:]
    turned = turned_requests(request_ref)
    join_columns(me_ref, parts, ext_ref, delta_ref)

    @pl.when(most_ref[0, 0] < SMALL)
    def _():
        fill(SMALL, most_ref, turned, sent_ref, ext_ref, place_ref, delta_ref)

    @pl.when(most_ref[0, 0] >= SMALL)
    def _():
        fill(CAPACITY, most_ref, turned, sent_ref, ext_ref, place_ref, delta_ref)


def fill(capacity, most_ref, turned, sent_ref, ext_ref, place_ref, delta_ref):
    group_rows = 8 * capacity
    delta = jnp.concatenate([delta_ref[s] for s in range(N_SEQ)], axis=1)

    def places(pick, group, first, count):
        index = iota((8, 8 * count), 1)
        owner = index // count
        value = jnp.where(
            iota((8, 8 * count), 0) == 0, owner + 8 * group, index - owner * count + first
        )
        return nn_dot(value.astype(jnp.float32).astype(jnp.bfloat16), pick)

    place = jnp.zeros((8, GROUP), jnp.float32)
    for group in range(N_DP // 8):
        pick = group_picks(turned, group, 0, capacity)
        place = place + places(pick, group, 0, capacity)
        rows = slice(group * group_rows, (group + 1) * group_rows)
        sent_ref[rows, :] = nn_dot(pick, ext_ref[...]).astype(jnp.bfloat16)
    place_ref[...] = place

    if capacity == CAPACITY:

        @pl.when(most_ref[0, 0] >= CAPACITY)
        def _():
            more = jnp.zeros((8, GROUP), jnp.float32)
            for group in range(N_DP // 8):
                more = more + places(
                    group_picks(turned, group, CAPACITY, EXTRA), group, CAPACITY, EXTRA
                )
            place_ref[...] += more

    place = place_ref[...]
    owner_of = place[0:1]
    slot_cols = []
    for s in range(N_SEQ):
        part = place[:, s * ROWS : (s + 1) * ROWS]
        blank = jnp.zeros((LANES - 8, LANES), jnp.float32)
        slot_cols.append(jnp.concatenate([part, blank], axis=0).T[:, 1:2])
    slot_col = jnp.concatenate(slot_cols, axis=0)
    lane = iota((GROUP, LANES), 1).astype(jnp.float32)
    to_owner = iota((N_DP, GROUP), 0).astype(jnp.float32) == owner_of
    tail = jnp.zeros((2 * N_DP, LANES), jnp.float32)
    for head in range(2):
        spread = jnp.concatenate(
            [jnp.where(to_owner, delta[c : c + 1], 0.0) for c in (head, 2 + head)], axis=0
        )
        slot_pick = (slot_col + (64.0 * head - 1.0) == lane).astype(jnp.float32)
        tail = tail + nn_dot(spread.astype(jnp.bfloat16), slot_pick.astype(jnp.bfloat16))
    tail = jnp.concatenate([tail[:N_DP], tail[N_DP:]], axis=1)
    row = iota((16, 2 * LANES), 0)
    for owner in range(N_DP):
        inside = owner * capacity % 16
        rows = slice(owner * capacity - inside, owner * capacity - inside + 16)
        kept = sent_ref[rows, : 2 * LANES].astype(jnp.float32)
        mine = jnp.broadcast_to(tail[owner : owner + 1], (16, 2 * LANES))
        sent_ref[rows, : 2 * LANES] = jnp.where(row == inside, mine, kept).astype(jnp.bfloat16)


def attend_kernel(
    segment_ref, most_ref, arrived_ref, extra_hbm, marks_ref, rows_ref, cols_ref, out_ref,
    x_ref, kt_ref, extra_ref, lanes_ref, weight_ref, squash_ref, total_ref, gqt_ref, gk_ref, gv_ref, sem,
):
    slots = N_DP * CAPACITY
    blocks = GROUP // BLOCK
    most = most_ref[0, 0]
    capacity = jnp.where(most < SMALL, SMALL, CAPACITY)
    spread = capacity.astype(jnp.float32)

    def rows_of(block):
        return slice(block * BLOCK, (block + 1) * BLOCK)

    def gather(block):
        rows = rows_of(block)
        slot = cols_ref[rows, 1:2] + 1.0
        place = jnp.where(slot < spread, cols_ref[rows, 0:1] * spread + slot, -1.0)
        pick = place == iota((BLOCK, slots), 1).astype(jnp.float32)
        pick = pick.astype(jnp.float32).astype(jnp.bfloat16)
        x_ref[rows, :] = nn_dot(pick, arrived_ref[...]).astype(jnp.bfloat16)

    for block in range(blocks):
        gather(block)

    @pl.when(most >= CAPACITY)
    def _():
        copy = pltpu.make_async_copy(extra_hbm, extra_ref, sem)
        copy.start()
        copy.wait()
        for block in range(blocks):
            rows = rows_of(block)
            slot = cols_ref[rows, 1:2] - float(CAPACITY - 1)
            place = jnp.where(slot >= 0.0, cols_ref[rows, 0:1] * float(EXTRA) + slot, -1.0)
            pick = place == iota((BLOCK, N_DP * EXTRA), 1).astype(jnp.float32)
            pick = pick.astype(jnp.float32).astype(jnp.bfloat16)
            x_ref[rows, :] += nn_dot(pick, extra_ref[...]).astype(jnp.bfloat16)

    for block in range(blocks):
        rows = rows_of(block)
        kt_ref[:, rows] = x_ref[rows, 256:384].astype(jnp.float32).T.astype(jnp.bfloat16)
    first = iota((LANES, slots), 0) * capacity == iota((LANES, slots), 1)
    first = first.astype(jnp.float32).astype(jnp.bfloat16)
    parts = nn_dot(first, arrived_ref[:, : 2 * LANES])
    source = wide(rows_ref[0:8, :])
    slot = wide(rows_ref[8:16, :])
    from_source = iota((LANES, GROUP), 0).astype(jnp.float32) == source
    from_source = from_source.astype(jnp.float32).astype(jnp.bfloat16)
    high = parts[:, :LANES].T.astype(jnp.bfloat16)
    low = parts[:, LANES:].T.astype(jnp.bfloat16)
    both = nn_dot(high, from_source) + nn_dot(low, from_source)
    place = iota((LANES, GROUP), 0).astype(jnp.float32)
    for head in range(2):
        lanes_ref[head : head + 1, :] = jnp.sum(
            jnp.where(place == slot + 64.0 * head, both, 0.0), axis=0, keepdims=True
        )
    gk_ref[...] = jnp.zeros_like(gk_ref)
    gv_ref[...] = jnp.zeros_like(gv_ref)
    marks = marks_ref[...].astype(jnp.float32)
    segment = wide(marks)
    mark_cols = jnp.concatenate([marks, jnp.zeros((LANES - 8, LANES), jnp.float32)], axis=0).T

    for block in range(blocks):
        rows = rows_of(block)
        near = slice(max(block - 1, 0) * BLOCK, (block + 1) * BLOCK)
        near_count = near.stop - near.start
        queries = jnp.concatenate([x_ref[rows, 0:128], x_ref[rows, 128:256]], axis=0)
        grads = jnp.concatenate([x_ref[rows, 512:640], x_ref[rows, 640:768]], axis=0)
        delta = jnp.concatenate([lanes_ref[0:1, rows], lanes_ref[1:2, rows]], axis=1)
        segment_q = jnp.concatenate([segment[:, rows]] * 2, axis=1)
        far = range(block - 1)

        def weigh(keys, causal):
            score = nt_dot(x_ref[keys, 256:384], queries)
            squashed = jnp.tanh(score * (scaling / softcap))
            columns = range(keys.start // ROWS, keys.stop // ROWS)
            segment_k = jnp.concatenate([mark_cols[:, s : s + 1] for s in columns], axis=0)
            allowed = segment_k == segment_q
            if causal is not None:
                allowed = allowed & causal
            return squashed, jnp.where(allowed, jnp.exp(softcap * squashed), 0.0)

        def back(keys, squashed, weights, inverse):
            probabilities = weights * inverse
            gv_ref[keys, :] += nn_dot(probabilities.astype(jnp.bfloat16), grads)
            prob_grad = nt_dot(x_ref[keys, 384:512], grads)
            score_grad = probabilities * (prob_grad - delta) * (1.0 - squashed * squashed)
            score_grad = score_grad.astype(jnp.bfloat16)
            gk_ref[keys, :] += nn_dot(score_grad, queries)
            return nn_dot(kt_ref[:, keys], score_grad)

        def reaches(key_block):
            return segment_ref[(key_block + 1) * BLOCK - 1] == segment_ref[block * BLOCK]

        if len(far) > 0:
            total_ref[...] = jnp.zeros_like(total_ref)
        for key_block in far:

            @pl.when(reaches(key_block))
            def _(keys=rows_of(key_block)):
                squashed, weights = weigh(keys, None)
                weight_ref[keys, :] = weights
                squash_ref[keys, :] = squashed
                total_ref[0:1, :] += jnp.sum(weights, axis=0, keepdims=True)

        ahead = iota((near_count, BLOCK), 0) - iota((near_count, BLOCK), 1)
        causal = (ahead <= near_count - BLOCK).astype(jnp.float32)
        causal = jnp.concatenate([causal, causal], axis=1) > 0.0
        squashed, weights = weigh(near, causal)
        total = jnp.sum(weights, axis=0, keepdims=True)
        if len(far) > 0:
            total = total + total_ref[0:1, :]
        inverse = 1.0 / total
        gqt_ref[...] = back(near, squashed, weights, inverse)
        if len(far) > 0:
            total_ref[0:1, :] = inverse
        for key_block in far:

            @pl.when(reaches(key_block))
            def _(keys=rows_of(key_block)):
                gqt_ref[...] += back(
                    keys, squash_ref[keys, :], weight_ref[keys, :], total_ref[0:1, :]
                )

        turned = (gqt_ref[...].T * scaling).astype(jnp.bfloat16)
        out_ref[rows, 0:128] = turned[:BLOCK]
        out_ref[rows, 128:256] = turned[BLOCK:]
    out_ref[:, 256:384] = (gk_ref[...] * scaling).astype(jnp.bfloat16)
    out_ref[:, 384:512] = gv_ref[...].astype(jnp.bfloat16)


def unpack_kernel(returned_ref, query_ref, key_ref, value_ref):
    for group in range(N_SEQ):
        two = slice(2 * group * HEAD_DIM, 2 * (group + 1) * HEAD_DIM)
        one = slice(group * HEAD_DIM, (group + 1) * HEAD_DIM)
        query_ref[:, two] = returned_ref[group, :, 0:256]
        key_ref[:, one] = returned_ref[group, :, 256:384]
        value_ref[:, one] = returned_ref[group, :, 384:512]


def shape(dims, dtype=jnp.bfloat16):
    return jax.ShapeDtypeStruct(dims, dtype)


VMEM = pl.BlockSpec(memory_space=pltpu.VMEM)
SMEM = pl.BlockSpec(memory_space=pltpu.SMEM)


def cost(flops, moved, transcendentals=0):
    return pl.CostEstimate(flops=flops, bytes_accessed=moved, transcendentals=transcendentals)


def pack(me, query, key_rows, value_rows, attn_out, out_grad):
    return pl.pallas_call(
        pack_kernel,
        out_shape=[shape((ROWS + 8, WIDTH))] * N_SEQ,
        in_specs=[SMEM] + [pl.BlockSpec(memory_space=pltpu.HBM)] * 5,
        out_specs=[VMEM] * N_SEQ,
        scratch_shapes=[
            pltpu.VMEM((ROWS, 2048), jnp.bfloat16),
            pltpu.VMEM((ROWS, 1024), jnp.bfloat16),
            pltpu.VMEM((ROWS, 1024), jnp.bfloat16),
            pltpu.VMEM((ROWS, 2048), jnp.bfloat16),
            pltpu.VMEM((ROWS, 2048), jnp.bfloat16),
            pltpu.VMEM((N_SEQ, 8, LANES), jnp.float32),
            pltpu.SemaphoreType.DMA((5,)),
        ],
        compiler_params=FULL,
        name="pack",
    )(me, query, key_rows, value_rows, attn_out, out_grad)


def index(me, lists):
    return pl.pallas_call(
        index_kernel,
        out_shape=(
            shape((16, LANES), jnp.float32),
            shape((GROUP, LANES), jnp.float32),
            shape((N_DP, LANES), jnp.int32),
            shape((1, 1), jnp.int32),
        ),
        in_specs=[SMEM] + [VMEM] * N_Y,
        out_specs=(VMEM, VMEM, VMEM, SMEM),
        scratch_shapes=[pltpu.VMEM((N_SEQ, LANES), jnp.int32)],
        compiler_params=PARAMS,
        name="index",
    )(me, *lists)


def send(me, most, request, parts):
    return pl.pallas_call(
        send_kernel,
        out_shape=shape((N_DP * CAPACITY, WIDTH)),
        in_specs=[SMEM, SMEM] + [VMEM] * 9,
        scratch_shapes=[
            pltpu.VMEM((GROUP, WIDTH), jnp.bfloat16),
            pltpu.VMEM((8, GROUP), jnp.float32),
            pltpu.VMEM((N_SEQ, 8, LANES), jnp.float32),
        ],
        compiler_params=ROOMY,
        cost_estimate=cost(2 * N_DP * CAPACITY * GROUP * WIDTH, 4_000_000),
        name="send",
    )(me, most, request, *parts)


def send_extra(me, request, parts):
    return pl.pallas_call(
        send_extra_kernel,
        out_shape=shape((N_DP * EXTRA, WIDTH)),
        in_specs=[SMEM] + [VMEM] * 9,
        scratch_shapes=[pltpu.VMEM((GROUP, WIDTH), jnp.bfloat16)],
        compiler_params=PARAMS,
        name="send_extra",
    )(me, request, *parts)


def attend(segments, most, arrived, extra, rows, cols):
    return pl.pallas_call(
        attend_kernel,
        out_shape=shape((GROUP, 4 * HEAD_DIM)),
        in_specs=[SMEM, SMEM, VMEM, pl.BlockSpec(memory_space=pltpu.HBM), VMEM, VMEM, VMEM],
        scratch_shapes=[
            pltpu.VMEM((GROUP, WIDTH), jnp.bfloat16),
            pltpu.VMEM((HEAD_DIM, GROUP), jnp.bfloat16),
            pltpu.VMEM((N_DP * EXTRA, WIDTH), jnp.bfloat16),
            pltpu.VMEM((8, GROUP), jnp.float32),
            pltpu.VMEM((GROUP - 2 * BLOCK, 2 * BLOCK), jnp.float32),
            pltpu.VMEM((GROUP - 2 * BLOCK, 2 * BLOCK), jnp.float32),
            pltpu.VMEM((8, 2 * BLOCK), jnp.float32),
            pltpu.VMEM((HEAD_DIM, 2 * BLOCK), jnp.float32),
            pltpu.VMEM((GROUP, HEAD_DIM), jnp.float32),
            pltpu.VMEM((GROUP, HEAD_DIM), jnp.float32),
            pltpu.SemaphoreType.DMA,
        ],
        compiler_params=PARAMS,
        name="attend",
    )(segments, most, arrived, extra, segments.reshape(N_SEQ, ROWS), rows, cols)


def unpack(returned):
    return pl.pallas_call(
        unpack_kernel,
        out_shape=(shape((ROWS, 2048)), shape((ROWS, 1024)), shape((ROWS, 1024))),
        compiler_params=PARAMS,
        name="unpack",
    )(returned)


def relay(array):
    return lax.all_to_all(array, "dp", split_axis=0, concat_axis=0, tiled=True)


def local(query, key_rows, value_rows, attn_out, out_grad, source_row, segment_ids):
    me = lax.axis_index("seq").reshape(1)

    def swap(array, m):
        return lax.ppermute(array, "seq", [(s, s ^ m) for s in range(N_SEQ)]) if m else array

    mine = source_row.reshape(1, ROWS)
    chip = jnp.concatenate([mine, swap(mine, 1)], axis=0)
    lists = [swap(chip, 2 * m) for m in range(N_Y)]
    packed = pack(me, query, key_rows, value_rows, attn_out, out_grad)
    packed, lists = lax.optimization_barrier((packed, lists))
    parts = [swap(packed[m], m) for m in ORDER]
    rows, cols, request, most = index(me, lists)
    request, rows, cols, most = lax.optimization_barrier((relay(request), rows, cols, most))
    extra = lax.cond(
        most[0, 0] >= CAPACITY,
        lambda request, *parts: relay(send_extra(me, request, parts)),
        lambda request, *parts: jnp.zeros((N_DP * EXTRA, WIDTH), jnp.bfloat16),
        request,
        *parts,
    )
    request, extra = lax.optimization_barrier((request, extra))
    used, pad = N_DP * SMALL, N_DP * (CAPACITY - SMALL)
    arrived = lax.cond(
        most[0, 0] < SMALL,
        lambda sent: jnp.pad(relay(sent[:used]), ((0, pad), (0, 0))),
        relay,
        send(me, most, request, parts),
    )
    grads = attend(segment_ids, most, arrived, extra, rows, cols)
    returned = lax.all_to_all(
        grads.reshape(N_SEQ, ROWS, 4 * HEAD_DIM), "seq", split_axis=0, concat_axis=0, tiled=True
    )
    return unpack(returned)


def solution(mesh):
    in_specs = (
        P(("dp", "seq"), None),
        P(("dp", "seq"), None),
        P(("dp", "seq"), None),
        P(("dp", "seq"), None),
        P(("dp", "seq"), None),
        P(("dp", "seq")),
        P("dp"),
    )
    out_specs = (P(("dp", "seq"), None), P(("dp", "seq"), None), P(("dp", "seq"), None))
    return jax.shard_map(local, mesh=mesh, in_specs=in_specs, out_specs=out_specs, check_vma=False)
```
